128 devices in a mesh: rows: 32 (over x_hi, y, z), text: 4 (over x_lo, core).
Axes of the slice: x: 4 (x_hi: 2, x_lo: 2; x = x_hi * 2 + x_lo), y: 4, z: 4, core: 2. Of those that a mesh axis runs over, the one named last changes fastest.
Arguments:
- image_tokens: bfloat16 [32, 512, 2048], P('rows', 'text'), may hold values from -6 to 6
- caption_embed: bfloat16 [32, 32, 4096], P('rows', 'text'), may hold values from -6 to 6
- caption_lengths: int32 [32, 2], P('rows'), may hold values from 5 to 16, as said below
- output_grad: bfloat16 [32, 512, 2048], P('rows', 'text'), may hold values from -6 to 6
- norm_self: bfloat16 [2048], P('rows'), may hold values from 0.5 to 1.5
- norm_cross: bfloat16 [2048], P('rows'), may hold values from 0.5 to 1.5
- norm_feed: bfloat16 [2048], P('rows'), may hold values from 0.5 to 1.5
- self_query: bfloat16 [2048, 2048], P('rows', 'text'), may hold values from -0.125 to 0.125
- self_key: bfloat16 [2048, 2048], P('rows', 'text'), may hold values from -0.125 to 0.125
- self_value: bfloat16 [2048, 2048], P('rows', 'text'), may hold values from -0.125 to 0.125
- self_output: bfloat16 [2048, 2048], P('text', 'rows'), may hold values from -1.5 to 1.5
- cross_query: bfloat16 [2048, 2048], P('rows', 'text'), may hold values from -0.125 to 0.125
- cross_key: bfloat16 [4096, 2048], P('rows', 'text'), may hold values from -0.09375 to 0.09375
- cross_value: bfloat16 [4096, 2048], P('rows', 'text'), may hold values from -0.09375 to 0.09375
- cross_output: bfloat16 [2048, 2048], P('text', 'rows'), may hold values from -0.375 to 0.375
- up_weight: bfloat16 [2048, 8192], P('rows', 'text'), may hold values from -0.125 to 0.125
- down_weight: bfloat16 [8192, 2048], P('text', 'rows'), may hold values from -0.0625 to 0.0625
Outputs:
- layer_output_array: bfloat16 [32, 512, 2048], P('rows', 'text')
- image_grad: float32 [32, 512, 2048], P('rows', 'text')
- caption_grad: float32 [32, 32, 4096], P('rows', 'text')
- norm_self_grad: float32 [2048], P('rows')
- norm_cross_grad: float32 [2048], P('rows')
- norm_feed_grad: float32 [2048], P('rows')
- self_query_grad: float32 [2048, 2048], P('rows', 'text')
- self_key_grad: float32 [2048, 2048], P('rows', 'text')
- self_value_grad: float32 [2048, 2048], P('rows', 'text')
- self_output_grad: float32 [2048, 2048], P('text', 'rows')
- cross_query_grad: float32 [2048, 2048], P('rows', 'text')
- cross_key_grad: float32 [4096, 2048], P('rows', 'text')
- cross_value_grad: float32 [4096, 2048], P('rows', 'text')
- cross_output_grad: float32 [2048, 2048], P('text', 'rows')
- up_grad: float32 [2048, 8192], P('rows', 'text')
- down_grad: float32 [8192, 2048], P('text', 'rows')
The draws below stay inside these ranges and needn't reach their ends.
Inputs may be any that keep to these rules, and one draw needn't show every extreme that they name: caption_lengths[r, i] counts the live slots of image i's caption; slots at or past it are padding. Some image has 16 live slots and some has 5.
All inputs are finite; a program needn't handle non-finite values.
Results may differ from the reference program's by a relative error of at most 0.029.
Values may be sent and summed in bfloat16 or wider, within the bound.
No kernel may reach another device: no remote copies, remote signals or barrier semaphores. Data moves between devices by JAX's collectives and lax.ppermute only.
A program may use at most 192 MiB of HBM per device.

```python
import jax
import jax.numpy as jnp
from jax import lax

D = 2048
HEADS = 16
HEAD_DIM = 128
FF = 8192
TD = 4096
IMAGE_TOKENS = 256
PER_ROW = 2
CAP = 16
SEQ = 512
IMAGE_ROWS = 32


def draw_caption_lengths(key, part):
    count = IMAGE_ROWS * PER_ROW
    first_key, second_key, third_key = jax.random.split(key, 3)
    lengths = jax.random.randint(first_key, (count,), 5, CAP + 1)
    longest = jax.random.randint(second_key, (), 0, count)
    offset = jax.random.randint(third_key, (), 1, count)
    shortest = (longest + offset) % count
    places = jnp.arange(count)
    lengths = jnp.where(places == longest, CAP, lengths)
    lengths = jnp.where(places == shortest, 5, lengths)
    return lengths.reshape(IMAGE_ROWS, PER_ROW).astype(jnp.int32)


def block_scale(stream_key, dims, cuts, low, top_value):
    def one(axis_at, blocks):
        heights = jax.random.uniform(jax.random.fold_in(jax.random.fold_in(stream_key, 6), axis_at), (blocks,), jnp.float32, low / len(cuts), top_value / len(cuts))
        return jnp.repeat(jnp.exp(heights), dims[axis_at] // blocks).reshape((-1,) + (1,) * (len(dims) - axis_at - 1))

    loudness = one(*cuts[0])
    for cut in cuts[1:]:
        loudness = loudness * one(*cut)
    return loudness


def gaussian(stream_key, extent, deviation, reach, cuts=(), held_as=jnp.bfloat16):
    array = jax.random.normal(stream_key, extent, jnp.float32) * deviation
    if len(cuts) > 0:
        array = block_scale(stream_key, extent, cuts, -0.22, 0.18) * array
    return jnp.clip(array, min=-reach, max=reach).astype(held_as)


def setup_inputs(seed: int = 0) -> dict:
    splits = jax.random.split(jax.random.key(seed), 18)
    return {
        "image_tokens": gaussian(splits[0], (IMAGE_ROWS, SEQ, D), 1.0, 6.0, ((0, 32), (1, 4))),
        "caption_embed": gaussian(splits[1], (IMAGE_ROWS, PER_ROW * CAP, TD), 1.0, 6.0, ((0, 32), (1, 4))),
        "caption_lengths": draw_caption_lengths(jax.random.fold_in(splits[17], 71), 0),
        "output_grad": gaussian(splits[3], (IMAGE_ROWS, SEQ, D), 1.0, 6.0, ((0, 32), (1, 4))),
        "norm_self": jnp.clip(1.0 + 0.1 * jax.random.normal(splits[4], (D,), jnp.float32), 0.5, 1.5).astype(jnp.bfloat16),
        "norm_cross": jnp.clip(1.0 + 0.1 * jax.random.normal(splits[5], (D,), jnp.float32), 0.5, 1.5).astype(jnp.bfloat16),
        "norm_feed": jnp.clip(1.0 + 0.1 * jax.random.normal(splits[6], (D,), jnp.float32), 0.5, 1.5).astype(jnp.bfloat16),
        "self_query": gaussian(splits[7], (D, D), D ** -0.5, 0.125, ((0, 32), (1, 4))),
        "self_key": gaussian(splits[8], (D, D), D ** -0.5, 0.125, ((0, 32), (1, 4))),
        "self_value": gaussian(splits[9], (D, D), D ** -0.5, 0.125, ((0, 32), (1, 4))),
        "self_output": gaussian(splits[10], (D, D), (D * 2 // IMAGE_TOKENS) ** -0.5, 1.5, ((0, 4), (1, 32))),
        "cross_query": gaussian(splits[11], (D, D), D ** -0.5, 0.125, ((0, 32), (1, 4))),
        "cross_key": gaussian(splits[12], (TD, D), TD ** -0.5, 0.09375, ((0, 32), (1, 4))),
        "cross_value": gaussian(splits[13], (TD, D), TD ** -0.5, 0.09375, ((0, 32), (1, 4))),
        "cross_output": gaussian(splits[14], (D, D), (D * 2 // CAP) ** -0.5, 0.375, ((0, 4), (1, 32))),
        "up_weight": gaussian(splits[15], (D, FF), D ** -0.5, 0.125, ((0, 32), (1, 4))),
        "down_weight": gaussian(splits[16], (FF, D), FF ** -0.5, 0.0625, ((0, 4), (1, 32))),
    }


HIGHEST = lax.Precision.HIGHEST

@jax.custom_vjp
def low(v):
    return lax.optimization_barrier(v.astype(jnp.bfloat16)).astype(jnp.float32)

@jax.custom_vjp
def low_back(v):
    return v

def low_keep(v):
    return (low(v), None)

def low_pass(kept, grad):
    return (grad,)

def back_keep(v):
    return (v, None)

def back_low(kept, grad):
    return (low(grad),)
low.defvjp(low_keep, low_pass)
low_back.defvjp(back_keep, back_low)

def matmul(operand, factor):
    return jnp.dot(operand, factor, precision=HIGHEST, preferred_element_type=jnp.float32)

def normalize(resid, gain):
    mean = lax.optimization_barrier(jnp.mean(resid, -1, keepdims=True))
    centered = resid - mean
    inverse = lax.rsqrt(lax.optimization_barrier(jnp.mean(centered * centered, -1, keepdims=True)) + 1e-05)
    return centered * inverse * gain

def split_heads(value_rows):
    return value_rows.reshape(PER_ROW, -1, HEADS, HEAD_DIM)

def attend(query_rows, key_rows, value_rows, live_slots):
    scores = jnp.einsum('bqhe,bkhe->bhqk', query_rows, key_rows, precision=HIGHEST) * HEAD_DIM ** (-0.5)
    scores = low_back(scores)
    if live_slots is not None:
        scores = jnp.where(live_slots, scores, -1e+30)
    row_max = lax.optimization_barrier(jnp.max(scores, -1, keepdims=True))
    shifted = jnp.exp(scores - row_max)
    attention = shifted / lax.optimization_barrier(jnp.sum(shifted, -1, keepdims=True))
    return jnp.einsum('bhqk,bkhe->bqhe', low(attention), value_rows, precision=HIGHEST)

def forward(image_row, caption, lengths, params):
    norm_self, norm_cross, norm_feed, self_query, self_key, self_value, self_output, cross_query, cross_key, cross_value, cross_output, up_weight, down_weight = params
    first_input_tensor = low(normalize(image_row, norm_self))
    query_one = low(low_back(matmul(first_input_tensor, self_query)))
    key_one = low(low_back(matmul(first_input_tensor, self_key)))
    value_one = low(low_back(matmul(first_input_tensor, self_value)))
    mixed_one = attend(split_heads(query_one), split_heads(key_one), split_heads(value_one), None)
    mixed_one = low(low_back(mixed_one.reshape(SEQ, D)))
    after_self = image_row + low_back(matmul(mixed_one, self_output))
    input_two = low(normalize(after_self, norm_cross))
    query_two = low(low_back(matmul(input_two, cross_query)))
    key_two = low(low_back(matmul(caption, cross_key)))
    value_two = low(low_back(matmul(caption, cross_value)))
    slot_index = jnp.arange(CAP)
    live_slots = (slot_index[None, :] < lengths[:, None])[:, None, None, :]
    mixed_two = attend(split_heads(query_two), split_heads(key_two), split_heads(value_two), live_slots)
    mixed_two = low(low_back(mixed_two.reshape(SEQ, D)))
    after_cross = after_self + low_back(matmul(mixed_two, cross_output))
    input_three = low(normalize(after_cross, norm_feed))
    hidden_pre = low_back(matmul(input_three, up_weight))
    hidden_act = low(jax.nn.gelu(hidden_pre, approximate=False))
    return after_cross + low_back(matmul(hidden_act, down_weight))

def reference(image_tokens, caption_embed, caption_lengths, output_grad, norm_self, norm_cross, norm_feed, self_query, self_key, self_value, self_output, cross_query, cross_key, cross_value, cross_output, up_weight, down_weight):
    params = tuple((weight.astype(jnp.float32) for weight in (norm_self, norm_cross, norm_feed, self_query, self_key, self_value, self_output, cross_query, cross_key, cross_value, cross_output, up_weight, down_weight)))

    def one_row(totals, row_data):
        image_row, caption, lengths, cotangent = row_data

        def run(image_value, caption_value, weight_set):
            return forward(image_value, caption_value, lengths, weight_set)
        result, pullback = jax.vjp(run, image_row.astype(jnp.float32), caption.astype(jnp.float32), params)
        grad_image, grad_caption, grad_params = pullback(cotangent.astype(jnp.float32))
        totals = jax.tree.map(jnp.add, totals, grad_params)
        return (totals, (result.astype(jnp.bfloat16), grad_image, grad_caption))
    start_sums = tuple((jnp.zeros(weight.shape, jnp.float32) for weight in params))
    totals, outputs = lax.scan(one_row, start_sums, (image_tokens, caption_embed, caption_lengths, output_grad))
    layer_output_array, image_grad, caption_grad = outputs
    grad_ns, grad_nc, grad_nf, grad_sq, grad_sk, grad_sv, grad_so, grad_cq, grad_ck, grad_cv, cross_attention_output_gradient, grad_up, grad_down = totals
    return (layer_output_array, image_grad, caption_grad, grad_ns, grad_nc, grad_nf, grad_sq, grad_sk, grad_sv, grad_so, grad_cq, grad_ck, grad_cv, cross_attention_output_gradient, grad_up, grad_down)
```

```python
import jax
import jax.numpy as jnp
from jax import lax
from jax.sharding import Mesh, PartitionSpec as P

HEAD = 128
CAP = 16
EPSILON = 1e-05
SCALE = HEAD ** (-0.5)
BF = jnp.bfloat16
F32 = jnp.float32
RING = ("xh", "xl")
PLANE = ("y", "z")


def px(value, step):
    return lax.ppermute(value, RING, [(i, (i + step) % 4) for i in range(4)])


def swap(value, axis):
    return lax.ppermute(value, axis, [(0, 1), (1, 0)])


def dot(a, b, ca, cb, out=F32):
    return lax.dot_general(a, b, (((ca,), (cb,)), ((), ())), preferred_element_type=F32).astype(out)


def gather_tokens(part):
    half = part.shape[0] // 2
    left, right = px(part, 1), px(part, -1)
    far = jnp.concatenate([px(left[:half], 1), px(right[half:], -1)], 0)
    pieces = []
    for piece in (part, left, right, far):
        pieces += [piece, swap(piece, "c")]
    return jnp.concatenate(pieces, 0)


def scatter_tokens(partial):
    parts = partial.reshape(4, 2, partial.shape[0] // 8, partial.shape[1])
    other = swap(parts[:, 1], "c")
    total = parts[:, 0].astype(F32) + other.astype(F32)
    low = total.astype(BF)
    a, b, c = px(low[1], -1), px(low[2], 1), px(low[3], 2)
    return total[0] + a.astype(F32) + b.astype(F32) + c.astype(F32)


def stats(resid):
    mean = jnp.mean(resid, -1, keepdims=True)
    centered = resid - mean
    inverse = lax.rsqrt(jnp.mean(centered * centered, -1, keepdims=True) + EPSILON)
    return centered * inverse, inverse


def norm_back(grad, normed, inverse, gain):
    scaled = grad * gain
    inner = (
        scaled
        - jnp.mean(scaled, -1, keepdims=True)
        - normed * jnp.mean(scaled * normed, -1, keepdims=True)
    )
    return inverse * inner, jnp.sum(grad * normed, axis=0)


def gelu_back(pre, grad):
    _, pullback = jax.vjp(lambda v: jax.nn.gelu(v, approximate=False), pre)
    return pullback(grad)[0]


def mix_features(value):
    n = value.shape[0]
    return value.reshape(n, 2, 16, 64).transpose(0, 2, 1, 3).reshape(n, 2048)


def unmix_features(value):
    n = value.shape[0]
    return value.reshape(n, 16, 2, 64).transpose(0, 2, 1, 3).reshape(n, 2048)


def per_device(
    image_tokens,
    caption_embed,
    caption_lengths,
    output_grad,
    norm_self,
    norm_cross,
    norm_feed,
    self_query,
    self_key,
    self_value,
    self_output,
    cross_query,
    cross_key,
    cross_value,
    cross_output,
    up_weight,
    down_weight,
):
    xh = lax.axis_index("xh")
    xl = lax.axis_index("xl")
    core = lax.axis_index("c")

    def halves(weight):
        n = weight.shape[1] // 2
        first, second = weight[:, :n], weight[:, n:]
        return jnp.where(xh == 0, first, second), jnp.where(xh == 0, second, first)

    def in_order(mine, theirs):
        return jnp.where(xh == 0, mine, theirs), jnp.where(xh == 0, theirs, mine)

    def gather_weights(weights, extra=None):
        pairs = [halves(w) for w in weights]
        mine = [p[0] for p in pairs]
        send = [p[1] for p in pairs]
        if extra is not None:
            mine.append(extra)
            send.append(extra)
        mine = jnp.concatenate(mine, 1)
        theirs = swap(jnp.concatenate(send, 1), "xh")
        pair = jnp.concatenate(in_order(mine, theirs), 0)
        return lax.all_gather(pair, PLANE, axis=0, tiled=True)

    def scatter_grads(grads, widths):
        total = lax.psum_scatter(grads.astype(BF), PLANE, scatter_dimension=0, tiled=True)
        keep = jnp.where(xh == 0, total[:64], total[64:])
        send = jnp.where(xh == 0, total[64:], total[:64])
        theirs = swap(send, "xh")
        outs, at = [], 0
        for width in widths:
            outs.append(
                jnp.concatenate(
                    in_order(keep[:, at : at + width], theirs[:, at : at + width]), 1
                ).astype(F32)
            )
            at += width
        return outs

    gains = jnp.stack([norm_self, norm_cross, norm_feed], 1)
    gains = jnp.pad(gains, ((0, 0), (0, 125)))
    first = gather_weights((self_query, self_key, self_value), gains)
    qkv_weight = first[:, :768]
    gain = first[:, 768:771].astype(F32).T
    gain_one, gain_two, gain_three = gain[0:1], gain[1:2], gain[2:3]
    second = gather_weights(
        (
            self_output.T,
            cross_query,
            cross_output.T,
            cross_key[:64],
            cross_value[:64],
            cross_key[64:],
            cross_value[64:],
        )
    )
    out_weight = second[:, :256]
    cq_weight = second[:, 256:512]
    co_weight = second[:, 512:768]
    kv_weight = (second[:, 768:1280], second[:, 1280:1792])
    third = gather_weights((up_weight, down_weight.T))
    up, down = third[:, :1024], third[:, 1024:]

    resid = mix_features(image_tokens[0]).astype(F32)
    normed_one, inverse_one = stats(resid)
    grad_low = mix_features(output_grad[0])
    h1 = (gather_tokens(normed_one.astype(BF)).astype(F32) * gain_one).astype(BF)
    grad_full = gather_tokens(grad_low)

    caption = caption_embed[0].reshape(8, 2, 16, 2, 64).transpose(0, 3, 2, 1, 4).reshape(8, 4096)
    sibling = swap(caption, "c")
    caption = jnp.concatenate(
        [jnp.where(core == 0, caption, sibling), jnp.where(core == 0, sibling, caption)], 0
    )
    caption = jnp.concatenate([caption, px(caption, 1), px(caption, -1), px(caption, 2)], 0)
    cap_a, cap_b = caption[:, :2048], caption[:, 2048:]

    qkv = dot(h1, qkv_weight, 1, 0, BF)
    q1 = qkv[:, :256].reshape(4, 256, 2, HEAD)
    k1 = qkv[:, 256:512].reshape(4, 256, 2, HEAD)
    v1 = qkv[:, 512:].reshape(4, 256, 2, HEAD)
    scores = jnp.einsum("iqhe,ikhe->ihqk", q1, k1, preferred_element_type=F32) * SCALE
    shifted = jnp.exp(scores - jnp.max(scores, -1, keepdims=True))
    p1 = shifted / jnp.sum(shifted, -1, keepdims=True)
    o1 = jnp.einsum("ihqk,ikhe->iqhe", p1.astype(BF), v1, preferred_element_type=F32)
    o1 = o1.astype(BF).reshape(1024, 256)
    resid_two = resid + scatter_tokens(dot(o1, out_weight, 1, 1, BF))
    normed_two, inverse_two = stats(resid_two)
    h2 = (normed_two * gain_two).astype(BF)

    kv = (dot(cap_a, kv_weight[0], 1, 0) + dot(cap_b, kv_weight[1], 1, 0)).astype(BF)
    k2 = kv[:, :256].reshape(64, 2, HEAD)
    v2 = kv[:, 256:].reshape(64, 2, HEAD)
    cq_heads = cq_weight.reshape(2048, 2, HEAD)
    co_heads = co_weight.reshape(2048, 2, HEAD)
    m_part = jnp.einsum("she,dhe->hsd", k2, cq_heads, preferred_element_type=F32).astype(BF)
    n_part = jnp.einsum("she,dhe->hsd", v2, co_heads, preferred_element_type=F32).astype(BF)
    both = jnp.stack([m_part, n_part], 0).reshape(4, 4, CAP, 2048).transpose(1, 0, 2, 3)
    both = both.reshape(4, 64, 2048)
    got = jnp.stack([both[0], px(both[1], -1), px(both[2], 1), px(both[3], 2)], 0)
    got = jnp.stack([got, swap(got, "c")], 0).reshape(8, 2, 32, 2048)
    m_all = got[:, 0].reshape(256, 2048)
    n_all = got[:, 1].reshape(256, 2048)
    length = jnp.where(xl == 0, caption_lengths[0, 0], caption_lengths[0, 1])
    live = lax.broadcasted_iota(jnp.int32, (1, CAP, 1), 1) < length
    scores = dot(m_all, h2, 1, 1).reshape(16, CAP, 128) * SCALE
    scores = jnp.where(live, scores, -1e30)
    shifted = jnp.exp(scores - jnp.max(scores, 1, keepdims=True))
    p2 = shifted / jnp.sum(shifted, 1, keepdims=True)
    p2_low = p2.astype(BF).reshape(256, 128)
    resid_three = resid_two + dot(p2_low, n_all, 0, 0)
    normed_three, inverse_three = stats(resid_three)
    h3 = gather_tokens((normed_three * gain_three).astype(BF))

    hidden = dot(h3, up, 1, 0)
    act = jax.nn.gelu(hidden, approximate=False).astype(BF)
    grad_hidden = gelu_back(hidden, dot(grad_full, down, 1, 0)).astype(BF)
    grad_norm = scatter_tokens(dot(grad_hidden, up, 1, 1, BF))
    block_out = resid_three + scatter_tokens(dot(act, down, 1, 1, BF))
    up_grad = dot(h3, grad_hidden, 0, 0, BF)
    down_grad = dot(grad_full, act, 0, 0, BF)
    up_out, down_out = scatter_grads(jnp.concatenate([up_grad, down_grad], 1), (1024, 1024))
    grad_resid = grad_low.astype(F32)
    step, feed_gain = norm_back(grad_norm, normed_three, inverse_three, gain_three)
    grad_resid = grad_resid + step

    low = grad_resid.astype(BF)
    grad_p = dot(n_all, low, 1, 1).reshape(16, CAP, 128)
    grad_s = p2 * (grad_p - jnp.sum(p2 * grad_p, 1, keepdims=True))
    grad_s = grad_s.astype(BF).reshape(256, 128)
    grad_norm = dot(grad_s, m_all, 0, 0) * SCALE
    step, cross_gain = norm_back(grad_norm, normed_two, inverse_two, gain_two)
    grad_resid = grad_resid + step
    grad_m = (dot(grad_s, h2, 1, 0) * SCALE).astype(BF).reshape(8, 32, 2048)
    grad_n = dot(p2_low, low, 1, 0, BF).reshape(8, 32, 2048)
    back = jnp.concatenate([grad_m, grad_n], 1).reshape(2, 4, 64, 2048)
    back = (back[0].astype(F32) + swap(back[1], "c").astype(F32)).astype(BF)
    back = jnp.stack([back[0], px(back[1], 1), px(back[2], -1), px(back[3], 2)], 0)
    back = back.reshape(4, 2, 2, CAP, 2048).transpose(1, 2, 0, 3, 4).reshape(2, 2, 64, 2048)
    cq_grad = jnp.einsum("hsd,she->dhe", back[0], k2, preferred_element_type=F32)
    co_grad = jnp.einsum("hsd,she->dhe", back[1], v2, preferred_element_type=F32)
    grad_k = jnp.einsum("hsd,dhe->she", back[0], cq_heads, preferred_element_type=F32)
    grad_v = jnp.einsum("hsd,dhe->she", back[1], co_heads, preferred_element_type=F32)
    grad_kv = jnp.concatenate([grad_k.reshape(64, 256), grad_v.reshape(64, 256)], 1).astype(BF)
    kv_grad_a = dot(cap_a, grad_kv, 0, 0, BF)
    kv_grad_b = dot(cap_b, grad_kv, 0, 0, BF)
    cap_grad = jnp.concatenate(
        [dot(grad_kv, kv_weight[0], 1, 1), dot(grad_kv, kv_weight[1], 1, 1)], 1
    )
    cap_grad = cap_grad.astype(BF).reshape(4, 2, 8, 4096)
    keep = jnp.where(core == 0, cap_grad[:, 0], cap_grad[:, 1])
    send = jnp.where(core == 0, cap_grad[:, 1], cap_grad[:, 0])
    total = keep.astype(F32) + swap(send, "c").astype(F32)
    low_cap = total.astype(BF)
    cap_out = (
        total[0]
        + px(low_cap[1], -1).astype(F32)
        + px(low_cap[2], 1).astype(F32)
        + px(low_cap[3], 2).astype(F32)
    )
    cap_out = cap_out.reshape(8, 2, 16, 2, 64).transpose(0, 3, 2, 1, 4).reshape(1, 8, 4096)

    grad_full = gather_tokens(grad_resid.astype(BF))
    out_grad = dot(grad_full, o1, 0, 0, BF)
    go1 = dot(grad_full, out_weight, 1, 0, BF).reshape(4, 256, 2, HEAD)
    grad_v1 = jnp.einsum("ihqk,iqhe->ikhe", p1.astype(BF), go1, preferred_element_type=F32)
    grad_p = jnp.einsum("iqhe,ikhe->ihqk", go1, v1, preferred_element_type=F32)
    grad_s = (p1 * (grad_p - jnp.sum(p1 * grad_p, -1, keepdims=True))).astype(BF)
    grad_q1 = jnp.einsum("ihqk,ikhe->iqhe", grad_s, k1, preferred_element_type=F32) * SCALE
    grad_k1 = jnp.einsum("ihqk,iqhe->ikhe", grad_s, q1, preferred_element_type=F32) * SCALE
    grad_qkv = jnp.concatenate(
        [g.astype(BF).reshape(1024, 256) for g in (grad_q1, grad_k1, grad_v1)], 1
    )
    grad_norm = scatter_tokens(dot(grad_qkv, qkv_weight, 1, 1, BF))
    qkv_grad = dot(h1, grad_qkv, 0, 0, BF)
    step, self_gain = norm_back(grad_norm, normed_one, inverse_one, gain_one)
    image_grad = unmix_features(grad_resid + step)[None]

    rest = scatter_grads(
        jnp.concatenate(
            [
                qkv_grad,
                out_grad,
                cq_grad.reshape(2048, 256).astype(BF),
                co_grad.reshape(2048, 256).astype(BF),
                kv_grad_a,
                kv_grad_b,
            ],
            1,
        ),
        (256,) * 10,
    )

    terms = jnp.stack([self_gain, cross_gain, feed_gain], 0)
    terms = terms.reshape(3, 16, 128).transpose(1, 0, 2).reshape(16, 384)
    terms = lax.all_to_all(terms, PLANE, split_axis=0, concat_axis=0)
    terms = jnp.sum(terms.reshape(16, 3, 2, 64), 0)
    keep = jnp.where(xh == 0, terms[:, 0], terms[:, 1])
    keep = keep + swap(jnp.where(xh == 0, terms[:, 1], terms[:, 0]), "xh")
    keep = keep + swap(keep, "xl")
    keep = keep + swap(keep, "c")

    return (
        unmix_features(block_out.astype(BF))[None],
        image_grad,
        cap_out,
        keep[0],
        keep[1],
        keep[2],
        rest[0],
        rest[1],
        rest[2],
        rest[3].T,
        rest[4],
        jnp.concatenate([rest[6], rest[8]], 0),
        jnp.concatenate([rest[7], rest[9]], 0),
        rest[5].T,
        up_out,
        down_out.T,
    )


def solution(mesh):
    names = ("xh", "y", "z", "xl", "c")
    fine = Mesh(mesh.devices.reshape(2, 4, 4, 2, 2), names)
    rows, text = ("xh", "y", "z"), ("xl", "c")
    tokens = P(rows, text, None)
    by_row = P(rows, text)
    by_text = P(text, rows)
    in_specs = (
        (tokens, tokens, P(rows, None), tokens)
        + (P(rows),) * 3
        + (by_row, by_row, by_row, by_text)
        + (by_row, by_row, by_row, by_text)
        + (by_row, by_text)
    )
    out_specs = (
        (tokens,) * 3
        + (P(rows),) * 3
        + (by_row, by_row, by_row, by_text)
        + (by_row, by_row, by_row, by_text)
        + (by_row, by_text)
    )
    return jax.shard_map(
        per_device, mesh=fine, in_specs=in_specs, out_specs=out_specs, check_vma=False
    )
```

```python
import functools

import jax
import jax.numpy as jnp
from jax import lax
from jax.experimental import pallas as pl
from jax.experimental.pallas import tpu as pltpu
from jax.sharding import Mesh, PartitionSpec as P

HEAD = 128
CAP = 16
EPSILON = 1e-05
SCALE = HEAD ** (-0.5)
BF = jnp.bfloat16
F32 = jnp.float32
RING = ("xh", "xl")
PLANE = ("y", "z")
WHOLE = pl.BlockSpec(memory_space=pltpu.VMEM)
HBM = pl.BlockSpec(memory_space=pltpu.MemorySpace.HBM)
ANY = pl.BlockSpec(memory_space=pl.ANY)
SCALAR = pl.BlockSpec(memory_space=pltpu.SMEM)


def shape(dims, dtype=BF):
    return jax.ShapeDtypeStruct(dims, dtype)


def out_of(value):
    return pltpu.with_memory_space_constraint(value, pltpu.MemorySpace.HBM)


def far(dims, dtype=BF):
    return pltpu.MemorySpace.HBM(dims, dtype)


def kernel(body, outs, args, order=(), vmem=24, in_specs=None, out_specs=None, **more):
    n, outer = len(order), body
    if in_specs is None:
        in_specs = [WHOLE] * len(args)
    if out_specs is None:
        out_specs = jax.tree.map(lambda _: WHOLE, outs)
    spec = more.pop("grid_spec", None)
    if n:
        m = len(args)

        def outer(*refs):
            body(*refs[:m], *refs[m + n :])

    specs = dict(in_specs=list(in_specs) + [HBM] * n, out_specs=out_specs)
    if spec is not None:
        scalars, grid, scratch = spec
        specs = dict(
            grid_spec=pltpu.PrefetchScalarGridSpec(
                num_scalar_prefetch=scalars, grid=grid, scratch_shapes=scratch, **specs
            )
        )
    return pl.pallas_call(
        outer,
        out_shape=outs,
        compiler_params=pltpu.CompilerParams(vmem_limit_bytes=vmem * 2**20),
        cost_estimate=pl.CostEstimate(flops=1000, bytes_accessed=1000, transcendentals=0),
        **specs,
        **more,
    )(*args, *order)


def hold_body(value, out):
    pass


def hold(value, order, away=False):
    return kernel(
        hold_body,
        far(value.shape, value.dtype) if away else shape(value.shape, value.dtype),
        (out_of(value) if away else value,),
        order,
        vmem=4,
        in_specs=[ANY],
        out_specs=ANY,
        input_output_aliases={0: 0},
        name="hold",
    )


def dot(a, b, ca, cb, out=F32):
    return lax.dot_general(a, b, (((ca,), (cb,)), ((), ())), preferred_element_type=F32).astype(out)


def px(value, step):
    return lax.ppermute(value, RING, [(i, (i + step) % 4) for i in range(4)])


def pp(value, axis, step):
    return lax.ppermute(value, axis, [(i, (i + step) % 4) for i in range(4)])


def swap(value, axis):
    return lax.ppermute(value, axis, [(0, 1), (1, 0)])


def after(value, dep):
    first = dep[(slice(0, 1),) * dep.ndim].reshape((1,) * value.ndim).astype(F32)
    return (value.astype(F32) + first * 0.0).astype(value.dtype)


def far_of(left, right):
    half = left.shape[0] // 2
    return [px(left[:half], 1), px(right[half:], -1)]


def pick(value, at):
    return lax.dynamic_index_in_dim(value, at & 3, 0, False, allow_negative_indices=False)


def reduce_tokens(keep, other):
    low = [(keep[i].astype(F32) + other[i].astype(F32)).astype(BF) for i in range(1, 4)]
    return [keep[0], other[0], px(low[0], -1), px(low[1], 1), px(low[2], 2)]


def stats(resid):
    mean = jnp.mean(resid, -1, keepdims=True)
    centered = resid - mean
    inverse = lax.rsqrt(jnp.mean(centered * centered, -1, keepdims=True) + EPSILON)
    return centered * inverse, inverse


def norm_back(scaled, normed, inverse):
    return inverse * (
        scaled
        - jnp.mean(scaled, -1, keepdims=True)
        - normed * jnp.mean(scaled * normed, -1, keepdims=True)
    )


def total_of(refs):
    total = refs[0][...].astype(F32)
    for ref in refs[1:]:
        total = total + ref[...].astype(F32)
    return total


def rows_of(refs, part=slice(None)):
    return jnp.concatenate([ref[part, :] for ref in refs], 0)


def attend_body(count, *refs):
    pieces, (w_ref, wo_ref) = refs[: 2 * count], refs[2 * count : 2 * count + 2]
    qkv_ref, p_ref, o_ref, keep_ref, send_ref = refs[-5:]
    for i in range(count):
        rows = slice(256 * i, 256 * (i + 1))
        qkv_ref[rows, :] = dot(rows_of(pieces[2 * i : 2 * i + 2]), w_ref[...], 1, 0, BF)
        for h in range(2):
            at = h * HEAD
            q = qkv_ref[rows, at : at + HEAD]
            k = qkv_ref[rows, 256 + at : 256 + at + HEAD]
            v = qkv_ref[rows, 512 + at : 512 + at + HEAD]
            s = dot(q, k, 1, 1) * SCALE
            e = jnp.exp(s - jnp.max(s, -1, keepdims=True))
            p = (e / jnp.sum(e, -1, keepdims=True)).astype(BF)
            p_ref[i, h] = p
            o_ref[rows, at : at + HEAD] = dot(p, v, 1, 0, BF)
    part = dot(o_ref[...], wo_ref[...], 1, 1, BF)
    for i in range(count):
        keep_ref[i] = part[256 * i : 256 * i + 128]
        send_ref[i] = part[256 * i + 128 : 256 * (i + 1)]


def attend(first, count, pieces, weights, saved=(), order=()):
    at = first // count
    half = pl.BlockSpec((count, 128, 2048), lambda j: (at, 0, 0))
    return kernel(
        functools.partial(attend_body, count),
        (
            far((1024, 768)),
            far((4, 2, 256, 256)),
            far((1024, 256)),
            far((4, 128, 2048)),
            far((4, 128, 2048)),
        ),
        (*pieces, *map(out_of, (weights, weights, *saved))),
        order,
        vmem=36,
        grid=(1,),
        in_specs=[pl.BlockSpec((128, 2048), lambda j: (0, 0))] * (2 * count)
        + [
            pl.BlockSpec((2048, 768), lambda j: (0, 0)),
            pl.BlockSpec((2048, 256), lambda j: (0, 3)),
        ]
        + [HBM] * len(saved),
        out_specs=(
            pl.BlockSpec((256 * count, 768), lambda j: (at, 0)),
            pl.BlockSpec((count, 2, 256, 256), lambda j: (at, 0, 0, 0)),
            pl.BlockSpec((256 * count, 256), lambda j: (at, 0)),
            half,
            half,
        ),
        input_output_aliases={2 * count + 2 + n: n for n in range(5)} if saved else {},
        name="attend",
    )


def attend_back_body(ca, cb, wo_ref, qkv_ref, p_ref, w_ref, *refs):
    g_ref, all_ref, keep_ref, send_ref = refs[-4:]
    c = rows_of((ca, cb))
    all_ref[...] = c
    go = dot(c, wo_ref[...], 1, 0, BF)
    for h in range(2):
        at = h * HEAD
        q = qkv_ref[:, at : at + HEAD]
        k = qkv_ref[:, 256 + at : 256 + at + HEAD]
        v = qkv_ref[:, 512 + at : 512 + at + HEAD]
        low = p_ref[0, h]
        g = go[:, at : at + HEAD]
        g_ref[:, 512 + at : 512 + at + HEAD] = dot(low, g, 0, 0, BF)
        gp = dot(g, v, 1, 1)
        p = low.astype(F32)
        gs = (p * (gp - jnp.sum(p * gp, -1, keepdims=True))).astype(BF)
        g_ref[:, at : at + HEAD] = (dot(gs, k, 1, 0) * SCALE).astype(BF)
        g_ref[:, 256 + at : 256 + at + HEAD] = (dot(gs, q, 0, 0) * SCALE).astype(BF)
    part = dot(g_ref[...], w_ref[...], 1, 1, BF)
    keep_ref[...] = part[:128]
    send_ref[...] = part[128:]


def attend_back(i, ca, cb, weights, qkv, p, saved, order=()):
    token = pl.BlockSpec((128, 2048), lambda j: (0, 0))
    more = () if saved is None else saved
    return kernel(
        attend_back_body,
        (far((1024, 768)), far((1024, 2048)), shape((128, 2048)), shape((128, 2048))),
        (ca, cb, *map(out_of, (weights, qkv, p, weights, *more))),
        order,
        grid=(1,),
        in_specs=[
            token,
            token,
            pl.BlockSpec((2048, 256), lambda j: (0, 3)),
            pl.BlockSpec((256, 768), lambda j: (i, 0)),
            pl.BlockSpec((1, 2, 256, 256), lambda j: (i, 0, 0, 0)),
            pl.BlockSpec((2048, 768), lambda j: (0, 0)),
        ]
        + [HBM] * len(more),
        out_specs=(
            pl.BlockSpec((256, 768), lambda j: (i, 0)),
            pl.BlockSpec((256, 2048), lambda j: (i, 0)),
            token,
            token,
        ),
        input_output_aliases={6: 0, 7: 1} if more else {},
        name="attend_back",
    )


def feed_body(xa, xb, ga, gb, up_ref, down_ref, *refs):
    act_ref, g_ref, all_ref, keep_ref, send_ref, sum_ref = refs[-6:]
    step = pl.program_id(0)
    x = rows_of((xa, xb))
    u = dot(x, up_ref[...], 1, 0)
    ga_hidden = dot(rows_of((ga, gb)), down_ref[...], 1, 0)
    phi = 0.5 + 0.5 * lax.erf(u * 0.5**0.5)
    act_ref[...] = (u * phi).astype(BF)
    slope = phi + u * jnp.exp(-0.5 * u * u) * (0.5 / jnp.pi) ** 0.5
    g = (ga_hidden * slope).astype(BF)
    g_ref[...] = g
    part = dot(g, up_ref[...], 1, 1)

    @pl.when(step == 0)
    def _():
        all_ref[...] = x
        sum_ref[...] = part

    @pl.when(step > 0)
    def _():
        sum_ref[...] += part

    @pl.when(step == pl.num_programs(0) - 1)
    def _():
        keep_ref[...] = sum_ref[:128, :].astype(BF)
        send_ref[...] = sum_ref[128:, :].astype(BF)


def feed(i, xa, xb, ga, gb, weights, saved, order=()):
    token = pl.BlockSpec((128, 2048), lambda j: (0, 0))
    final = pl.BlockSpec((128, 2048), lambda j: (1, 0))
    hidden = pl.BlockSpec((256, 256), lambda j: (i, j))
    more = () if saved is None else saved
    return kernel(
        feed_body,
        (
            far((1024, 1024)),
            far((1024, 1024)),
            far((1024, 2048)),
            shape((128, 2048)),
            shape((128, 2048)),
        ),
        (xa, xb, ga, gb, *map(out_of, (weights, weights, *more))),
        order,
        vmem=28,
        grid=(4,),
        in_specs=[
            token,
            token,
            final,
            final,
            pl.BlockSpec((2048, 256), lambda j: (0, j)),
            pl.BlockSpec((2048, 256), lambda j: (0, j + 4)),
        ]
        + [HBM] * len(more),
        out_specs=(
            hidden,
            hidden,
            pl.BlockSpec((256, 2048), lambda j: (i, 0)),
            token,
            token,
        ),
        scratch_shapes=[pltpu.VMEM((256, 2048), F32)],
        input_output_aliases={6: 0, 7: 1, 8: 2} if more else {},
        name="feed",
    )


def feed_out_body(act_ref, down_ref, keep_ref, send_ref):
    part = dot(act_ref[...], down_ref[...], 1, 1, BF)
    for i in range(4):
        keep_ref[i] = part[256 * i : 256 * i + 128]
        send_ref[i] = part[256 * i + 128 : 256 * (i + 1)]


def feed_out(act, weights, order=()):
    out = pl.BlockSpec((4, 128, 256), lambda j: (0, 0, j))
    return kernel(
        feed_out_body,
        (far((4, 128, 2048)), far((4, 128, 2048))),
        (out_of(act), out_of(weights)),
        order,
        grid=(8,),
        in_specs=[
            pl.BlockSpec((1024, 1024), lambda j: (0, 0)),
            pl.BlockSpec((256, 1024), lambda j: (j, 1)),
        ],
        out_specs=(out, out),
        name="feed_out",
    )


def feed_grad_body(x, g, act, *refs):
    gm, out = refs[:8], refs[8]
    out[:, :1024] = dot(x[...], g[...], 0, 0, BF)
    out[:, 1024:] = dot(rows_of(gm), act[...], 0, 0, BF)


def feed_grad(x, g, act, pieces, order=()):
    hidden = pl.BlockSpec((1024, 1024), lambda j: (0, 0))
    return kernel(
        feed_grad_body,
        far((2048, 2048)),
        tuple(map(out_of, (x, g, act, *pieces))),
        order,
        grid=(8,),
        in_specs=[pl.BlockSpec((1024, 256), lambda j: (0, j)), hidden, hidden]
        + [pl.BlockSpec((128, 256), lambda j: (1, j))] * 8,
        out_specs=pl.BlockSpec((256, 2048), lambda j: (j, 0)),
        name="feed_grad",
    )


def more_grad_body(g, c, o, cross, *refs):
    x, out = refs[:8], refs[8]
    out[:, :768] = dot(rows_of(x), g[...], 0, 0, BF)
    out[:, 768:1024] = dot(c[...], o[...], 0, 0, BF)
    out[:, 1024:] = cross[...]


def more_grad(g, c, o, cross, pieces, order=()):
    return kernel(
        more_grad_body,
        far((2048, 1536)),
        (*map(out_of, (g, c, o)), cross, *map(out_of, pieces)),
        order,
        grid=(8,),
        in_specs=[
            pl.BlockSpec((1024, 768), lambda j: (0, 0)),
            pl.BlockSpec((1024, 256), lambda j: (0, j)),
            pl.BlockSpec((1024, 256), lambda j: (0, 0)),
            pl.BlockSpec((256, 512), lambda j: (j, 0)),
        ]
        + [pl.BlockSpec((128, 256), lambda j: (0, j))] * 8,
        out_specs=pl.BlockSpec((256, 1536), lambda j: (j, 0)),
        name="more_grad",
    )


def fold_body(at_ref, kv_ref, w_ref, kv_out, both_ref):
    kv = jnp.sum(kv_ref[...].astype(F32), 0).astype(BF)
    kv_out[...] = kv
    for n in range(4):
        at = n * HEAD
        part = dot(kv[:, at : at + HEAD], w_ref[:, at : at + HEAD], 1, 1, BF)
        for i in range(4):
            away = (i + 4 - at_ref[2]) & 3
            away = jnp.where(away == 0, 0, jnp.where(away == 3, 1, away + 1))
            both_ref[away, n * CAP : (n + 1) * CAP, :] = part[i * CAP : (i + 1) * CAP]


def fold(place, kv, weights, order=()):
    outs = (shape((64, 512)), shape((4, 64, 2048)))
    return kernel(
        fold_body,
        outs,
        (place, kv, out_of(weights)),
        order,
        in_specs=[
            SCALAR,
            pl.BlockSpec((16, 64, 512), lambda j: (0, 0, 0)),
            pl.BlockSpec((2048, 512), lambda j: (0, 2)),
        ],
        out_specs=(
            pl.BlockSpec((64, 512), lambda j: (0, 0)),
            pl.BlockSpec((4, 64, 2048), lambda j: (0, 0, 0)),
        ),
        grid=(1,),
        name="fold",
    )


def unfold_body(at_ref, b0, b1, b2, b3, kv_ref, w_ref, grad_ref, gkv_ref, rows_ref):
    for n in range(4):
        at = n * HEAD
        for away, ref in zip((0, 3, 1, 2), (b0, b1, b2, b3)):
            image = (at_ref[2] + away) & 3
            rows_ref[image] = ref[n * CAP : (n + 1) * CAP, :]
        rows = rows_ref[...].reshape(64, 2048)
        grad_ref[:, at : at + HEAD] = dot(rows, kv_ref[:, at : at + HEAD], 0, 0, BF)
        gkv_ref[:, at : at + HEAD] = dot(rows, w_ref[:, at : at + HEAD], 1, 0, BF)


def unfold(place, back, kv, weights, order=()):
    slot = pl.BlockSpec((64, 2048), lambda j: (0, 0))
    return kernel(
        unfold_body,
        (shape((2048, 512)), shape((64, 512))),
        (place, *back, kv, out_of(weights)),
        order,
        in_specs=[SCALAR]
        + [slot] * 4
        + [
            pl.BlockSpec((64, 512), lambda j: (0, 0)),
            pl.BlockSpec((2048, 512), lambda j: (0, 2)),
        ],
        out_specs=(
            pl.BlockSpec((2048, 512), lambda j: (0, 0)),
            pl.BlockSpec((64, 512), lambda j: (0, 0)),
        ),
        grid=(1,),
        scratch_shapes=[pltpu.VMEM((4, CAP, 2048), BF)],
        name="unfold",
    )


def slots_of(refs, part):
    return jnp.concatenate([ref[i, part, :] for ref in refs for i in range(4)], 0)


def middle_body(length_ref, *refs):
    x, parts, slots = refs[0], refs[1:6], refs[6:8]
    n2_ref, i2_ref, p2_ref, x3_ref, n3_ref, i3_ref = refs[8:]
    x2 = x[...].astype(F32) + total_of(parts)
    normed, inverse = stats(x2)
    low = normed.astype(BF)
    n2_ref[...] = low
    i2_ref[...] = inverse
    m, n = slots_of(slots, slice(0, 32)), slots_of(slots, slice(32, 64))
    s = (dot(m, low, 1, 1) * SCALE).reshape(16, CAP, 128)
    live = lax.broadcasted_iota(jnp.int32, (1, CAP, 1), 1) < length_ref[0]
    s = jnp.where(live, s, -1e30)
    e = jnp.exp(s - jnp.max(s, 1, keepdims=True))
    p = (e / jnp.sum(e, 1, keepdims=True)).reshape(256, 128)
    p2_ref[...] = p
    x3 = x2 + dot(p.astype(BF), n, 0, 0)
    x3_ref[...] = x3
    normed, inverse = stats(x3)
    n3_ref[...] = normed.astype(BF)
    i3_ref[...] = inverse


def middle(length, x, parts, slots, order=()):
    column = shape((128, 1), F32)
    return kernel(
        middle_body,
        (
            shape((128, 2048)),
            column,
            shape((256, 128), F32),
            shape((128, 2048), F32),
            shape((128, 2048)),
            column,
        ),
        (length, x, *parts, *slots),
        order,
        in_specs=[SCALAR] + [WHOLE] * 8,
        name="middle",
    )


def middle_back_body(*refs):
    g3, parts, slots = refs[0], refs[1:6], refs[6:8]
    n2, i2, p2, n3, i3 = refs[8:13]
    g1_ref, low_ref, keep_ref, send_ref = refs[13:]
    g2 = g3[...].astype(F32) + norm_back(total_of(parts), n3[...].astype(F32), i3[...])
    c = g2.astype(BF)
    m, n = slots_of(slots, slice(0, 32)), slots_of(slots, slice(32, 64))
    p = p2[...].reshape(16, CAP, 128)
    gp = dot(n, c, 1, 1).reshape(16, CAP, 128)
    gs = (p * (gp - jnp.sum(p * gp, 1, keepdims=True))).reshape(256, 128) * SCALE
    gs = gs.astype(BF)
    g1 = g2 + norm_back(dot(gs, m, 0, 0), n2[...].astype(F32), i2[...])
    g1_ref[...] = g1
    low_ref[...] = g1.astype(BF)
    gm = dot(gs, n2[...], 1, 0, BF)
    gn = dot(p2[...].astype(BF), c, 1, 0, BF)
    for out, at in ((keep_ref, 0), (send_ref, 128)):
        for i in range(4):
            rows = slice(at + 32 * i, at + 32 * (i + 1))
            out[i, :32, :] = gm[rows]
            out[i, 32:, :] = gn[rows]


def middle_back(g3, parts, slots, n2, i2, p2, n3, i3, order=()):
    slot = shape((4, 64, 2048))
    outs = (shape((128, 2048), F32), shape((128, 2048)), slot, slot)
    args = (g3, *parts, *slots, n2, i2, p2, n3, i3)
    return kernel(middle_back_body, outs, args, order, name="middle_back")


def last_body(*refs):
    g1, parts, x, out = refs[0], refs[1:6], refs[6], refs[7]
    normed, inverse = stats(x[...].astype(F32))
    out[...] = g1[...] + norm_back(total_of(parts), normed, inverse)


def last(g1, parts, x, order=()):
    return kernel(last_body, shape((128, 2048), F32), (g1, *parts, x), order, name="last")


def mix_features(value):
    n = value.shape[0]
    return value.reshape(n, 2, 16, 64).transpose(0, 2, 1, 3).reshape(n, 2048)


def unmix_features(value):
    n = value.shape[0]
    return value.reshape(n, 16, 2, 64).transpose(0, 2, 1, 3).reshape(n, 2048)


def per_device(
    image_tokens,
    caption_embed,
    caption_lengths,
    output_grad,
    norm_self,
    norm_cross,
    norm_feed,
    self_query,
    self_key,
    self_value,
    self_output,
    cross_query,
    cross_key,
    cross_value,
    cross_output,
    up_weight,
    down_weight,
):
    xh = lax.axis_index("xh")
    xl = lax.axis_index("xl")
    core = lax.axis_index("c")
    place = [lax.axis_index("y"), lax.axis_index("z"), 2 * xh + xl, core]
    place = jnp.stack(place).astype(jnp.int32)
    gain_one = norm_self.astype(F32)[:, None]
    gain_two = norm_cross.astype(F32)[:, None]
    gain_three = norm_feed.astype(F32)[:, None]

    def gained(weight, gain):
        return (weight.astype(F32) * gain).astype(BF)

    def halves(weight):
        n = weight.shape[1] // 2
        first, second = weight[:, :n], weight[:, n:]
        return jnp.where(xh == 0, first, second), jnp.where(xh == 0, second, first)

    def in_order(mine, theirs):
        return jnp.where(xh == 0, mine, theirs), jnp.where(xh == 0, theirs, mine)

    def exchange(weights):
        pairs = [halves(w) for w in weights]
        mine = jnp.concatenate([p[0] for p in pairs], 1)
        theirs = swap(jnp.concatenate([p[1] for p in pairs], 1), "xh")
        return jnp.stack(in_order(mine, theirs), 0)

    def home(first, second):
        keep = jnp.where(xh == 0, first, second)
        theirs = swap(jnp.where(xh == 0, second, first).astype(BF), "xh")
        return keep, theirs.astype(F32)

    def join(keep, theirs):
        return jnp.concatenate(in_order(keep, theirs), 1)

    pair = exchange(
        (
            gained(self_query, gain_one),
            gained(self_key, gain_one),
            gained(self_value, gain_one),
            self_output.T,
            gained(cross_query, gain_two),
            cross_output.T,
        )
    )
    first = lax.all_gather(pair.reshape(128, 1536), PLANE, axis=0, tiled=True)
    pair_late = exchange(
        (
            after(gained(up_weight, gain_three), pair),
            down_weight.T,
            cross_key[:64],
            cross_value[:64],
            cross_key[64:],
            cross_value[64:],
        )
    )
    pair_kv = jnp.stack([pair_late[:, :, 2048:2560], pair_late[:, :, 2560:]], 1)
    pair_kv = pair_kv.reshape(256, 512)
    resid = mix_features(image_tokens[0])
    normed_one, _ = stats(resid.astype(F32))
    grad_low = mix_features(output_grad[0])
    caption = after(caption_embed[0], pair)
    caption = lax.all_gather(caption, ("xh", "xl", "c"), axis=0, tiled=True)
    caption = caption.reshape(64, 2, 16, 128).transpose(2, 0, 1, 3).reshape(16, 64, 256)
    tokens = after(jnp.concatenate([normed_one.astype(BF), grad_low], 0), caption)
    pieces = [tokens, px(tokens, 1), px(tokens, -1)]
    pieces.append(jnp.concatenate(far_of(pieces[1], pieces[2]), 0))
    tokens = [side for piece in pieces for side in (piece, swap(piece, "c"))]
    feed_weight = pair_late[:, :, :2048].reshape(128, 2048)
    feed_weight = lax.all_gather(feed_weight, PLANE, axis=0, tiled=True)
    caption = lax.all_to_all(caption, PLANE, split_axis=0, concat_axis=0, tiled=True)
    caption = caption.reshape(1024, 256)
    kv = dot(caption, pair_kv, 1, 0, BF).reshape(16, 64, 512)
    kv = lax.all_to_all(kv, PLANE, split_axis=0, concat_axis=0, tiled=True)
    kv, both = fold(place, kv.reshape(16, 64, 512), first)
    kv_weight = lax.all_gather(after(pair_kv, kv), PLANE, axis=0, tiled=True)
    slots_come = [px(both[1], -1), px(both[2], 1), px(both[3], 2)]
    slots = jnp.stack([both[0], *slots_come], 0)
    slots = (slots, swap(slots, "c"))

    saved = attend(0, 2, tokens[:4], first)
    qkv, p1, o1, keep, send = attend(2, 2, tokens[4:], first, saved, slots_come)
    parts = reduce_tokens(keep, swap(send, "c"))
    length = jnp.where(xl == 0, caption_lengths[0, 0], caption_lengths[0, 1])[None]
    n2, i2, p2, x3, n3, i3 = middle(length, resid, parts, slots)

    theirs = swap(n3, "c")
    around = [px(n3, 1), px(n3, -1)]
    saved, keeps, others = None, [], []
    for i in range(4):
        if i == 0:
            mine = n3
        else:
            if i == 1:
                around = [hold(piece, keeps[:1]) for piece in around]
                across = far_of(*around)
            if i < 3:
                mine = around[i - 1]
            else:
                mine = jnp.concatenate([hold(piece, keeps[1:2]) for piece in across], 0)
            theirs = swap(mine, "c")
        *saved, keep, send = feed(
            i,
            mine,
            theirs,
            tokens[2 * i],
            tokens[2 * i + 1],
            feed_weight,
            saved and tuple(saved),
            others[:-1][-1:],
        )
        keeps.append(keep)
        others.append(swap(send, "c"))
    parts = reduce_tokens(keeps, others)
    act, grad, x3_all = saved
    total = feed_grad(x3_all, grad, act, tokens, others[-1:] + [kv_weight])
    g1, c1, keep_slots, send_slots = middle_back(
        grad_low, parts, slots, n2, i2, p2, n3, i3, [total]
    )
    total = lax.psum_scatter(hold(total, [c1], True), PLANE, scatter_dimension=0, tiled=True)
    own, their_ff = home(total[:64], total[64:])
    own = own.astype(F32)
    up_out = join(own[:, :1024], their_ff[:, :1024])
    down_out = join(own[:, 1024:], their_ff[:, 1024:])

    theirs = swap(c1, "c")
    around = [px(c1, 1), px(c1, -1)]
    slot_back = keep_slots.astype(F32) + swap(send_slots, "c").astype(F32)
    back, keeps, others = None, [], []
    for i in range(4):
        if i == 0:
            mine = c1
        else:
            if i == 1:
                around = [hold(piece, keeps[:1]) for piece in around]
                across = far_of(*around)
                slot_back = after(slot_back.astype(BF), around[1])
                slot_back = [
                    slot_back[0],
                    px(slot_back[1], 1),
                    px(slot_back[2], -1),
                    px(slot_back[3], 2),
                ]
            if i < 3:
                mine = around[i - 1]
            else:
                mine = jnp.concatenate([hold(piece, keeps[1:2]) for piece in across], 0)
            theirs = swap(mine, "c")
        order = others[:-1][-1:] + (slot_back[1:3] if i == 3 else [])
        *back, keep, send = attend_back(
            i, mine, theirs, first, qkv, p1, back and tuple(back), order
        )
        keeps.append(keep)
        others.append(swap(send, "c"))
    parts = reduce_tokens(keeps, others)
    cross_grad, grad_kv = unfold(place, slot_back, kv, first)
    more = more_grad(*back, o1, cross_grad, tokens, keeps[-1:])
    more = hold(more, [total], True)
    rest = lax.psum_scatter(more, PLANE, scatter_dimension=0, tiled=True)
    y_keep, y_send = feed_out(act, feed_weight, [more])
    y_parts = reduce_tokens(y_keep, swap(y_send, "c"))
    block_out = x3
    for part in y_parts:
        block_out = block_out + part.astype(F32)
    grad_kv = after(grad_kv, more)
    kv_all = lax.all_to_all(
        jnp.broadcast_to(grad_kv[None], (16, 64, 512)), PLANE, split_axis=0, concat_axis=0, tiled=True
    ).reshape(1024, 512)
    kv_grad = dot(caption, kv_all, 0, 0)
    ck_own, ck_their = home(kv_grad[:128], kv_grad[128:])
    ck_out = join(ck_own[:, :256], ck_their[:, :256])
    cv_out = join(ck_own[:, 256:], ck_their[:, 256:])
    cap_grad = dot(grad_kv, kv_weight, 1, 1, BF).reshape(4, 16, 4096)
    keep = jnp.where(core == 0, cap_grad[:, :8], cap_grad[:, 8:])
    send = jnp.where(core == 0, cap_grad[:, 8:], cap_grad[:, :8])
    send = swap(send, "c")
    low_cap = (keep.astype(F32) + send.astype(F32)).astype(BF)
    near_image = [pick(low_cap, place[2] + n) for n in range(4)]
    cap_out = near_image[0].astype(F32)
    for n in (1, 2, 3):
        cap_out = cap_out + px(near_image[n], n).astype(F32)
    cap_out = cap_out.reshape(8, 16, 2, 128).transpose(0, 2, 1, 3).reshape(1, 8, 4096)
    for part in y_parts[2:]:
        rest = after(rest, part)
    own, their = home(rest[:64], rest[64:])
    own = own.astype(F32)
    outs = [join(own[:, at : at + 256], their[:, at : at + 256]) for at in range(0, 1536, 256)]
    so_out, cq_out, co_out = outs[3:]

    image_grad = unmix_features(last(g1, parts, resid))[None]

    first_gain = (
        jnp.sum(outs[0] * self_query.astype(F32), 1)
        + jnp.sum(outs[1] * self_key.astype(F32), 1)
        + jnp.sum(outs[2] * self_value.astype(F32), 1)
    )
    terms = jnp.stack(
        [
            first_gain,
            jnp.sum(cq_out * cross_query.astype(F32), 1),
            jnp.sum(up_out * up_weight.astype(F32), 1),
        ],
        0,
    )
    terms = terms + swap(terms, "xl")
    terms = terms + swap(terms, "c")

    return (
        unmix_features(block_out.astype(BF))[None],
        image_grad,
        cap_out,
        terms[0],
        terms[1],
        terms[2],
        outs[0] * gain_one,
        outs[1] * gain_one,
        outs[2] * gain_one,
        so_out.T,
        cq_out * gain_two,
        ck_out,
        cv_out,
        co_out.T,
        up_out * gain_three,
        down_out.T,
    )


def solution(mesh):
    names = ("xh", "y", "z", "xl", "c")
    fine = Mesh(mesh.devices.reshape(2, 4, 4, 2, 2), names)
    rows, text = ("xh", "y", "z"), ("xl", "c")
    tokens = P(rows, text, None)
    by_row = P(rows, text)
    by_text = P(text, rows)
    weights = (by_row, by_row, by_row, by_text, by_row, by_row, by_row, by_text, by_row, by_text)
    in_specs = (tokens, tokens, P(rows, None), tokens) + (P(rows),) * 3 + weights
    out_specs = (tokens,) * 3 + (P(rows),) * 3 + weights
    return jax.shard_map(
        per_device, mesh=fine, in_specs=in_specs, out_specs=out_specs, check_vma=False
    )
```

```python
import functools

import jax
import jax.numpy as jnp
from jax import lax
from jax.experimental import pallas as pl
from jax.experimental.pallas import tpu as pltpu
from jax.sharding import Mesh, PartitionSpec as P

HEAD = 128
CAP = 16
EPSILON = 1e-05
SCALE = HEAD ** (-0.5)
BF = jnp.bfloat16
F32 = jnp.float32
RING = ("xh", "xl")
PLANE = ("y", "z")
WHOLE = pl.BlockSpec(memory_space=pltpu.VMEM)
HBM = pl.BlockSpec(memory_space=pltpu.MemorySpace.HBM)
ANY = pl.BlockSpec(memory_space=pl.ANY)
SCALAR = pl.BlockSpec(memory_space=pltpu.SMEM)


def shape(dims, dtype=BF):
    return jax.ShapeDtypeStruct(dims, dtype)


def out_of(value):
    return pltpu.with_memory_space_constraint(value, pltpu.MemorySpace.HBM)


def far(dims, dtype=BF):
    return pltpu.MemorySpace.HBM(dims, dtype)


def kernel(body, outs, args, order=(), vmem=16, in_specs=None, out_specs=None, **more):
    n, outer = len(order), body
    if in_specs is None:
        in_specs = [WHOLE] * len(args)
    if out_specs is None:
        out_specs = jax.tree.map(lambda _: WHOLE, outs)
    spec = more.pop("grid_spec", None)
    if n:
        m = len(args)

        def outer(*refs):
            body(*refs[:m], *refs[m + n :])

    specs = dict(in_specs=list(in_specs) + [HBM] * n, out_specs=out_specs)
    if spec is not None:
        scalars, grid, scratch = spec
        specs = dict(
            grid_spec=pltpu.PrefetchScalarGridSpec(
                num_scalar_prefetch=scalars, grid=grid, scratch_shapes=scratch, **specs
            )
        )
    return pl.pallas_call(
        outer,
        out_shape=outs,
        compiler_params=pltpu.CompilerParams(vmem_limit_bytes=vmem * 2**20),
        cost_estimate=pl.CostEstimate(flops=1000, bytes_accessed=1000, transcendentals=0),
        **specs,
        **more,
    )(*args, *order)


def hold_body(value, out):
    pass


def hold(value, order, away=False):
    return kernel(
        hold_body,
        far(value.shape, value.dtype) if away else shape(value.shape, value.dtype),
        (out_of(value) if away else value,),
        order,
        vmem=4,
        in_specs=[ANY],
        out_specs=ANY,
        input_output_aliases={0: 0},
        name="hold",
    )


def dot(a, b, ca, cb, out=F32):
    return lax.dot_general(a, b, (((ca,), (cb,)), ((), ())), preferred_element_type=F32).astype(out)


def px(value, step):
    return lax.ppermute(value, RING, [(i, (i + step) % 4) for i in range(4)])


def pp(value, axis, step):
    return lax.ppermute(value, axis, [(i, (i + step) % 4) for i in range(4)])


def swap(value, axis):
    return lax.ppermute(value, axis, [(0, 1), (1, 0)])


def after(value, dep):
    first = dep[(slice(0, 1),) * dep.ndim].reshape((1,) * value.ndim).astype(F32)
    return (value.astype(F32) + first * 0.0).astype(value.dtype)


def far_of(left, right):
    half = left.shape[0] // 2
    return [px(left[:half], 1), px(right[half:], -1)]


def pick(value, at):
    return lax.dynamic_index_in_dim(value, at & 3, 0, False, allow_negative_indices=False)


def reduce_tokens(keep, other):
    low = [(keep[i].astype(F32) + other[i].astype(F32)).astype(BF) for i in range(1, 4)]
    return [keep[0], other[0], px(low[0], -1), px(low[1], 1), px(low[2], 2)], low


def stats(resid):
    mean = jnp.mean(resid, -1, keepdims=True)
    centered = resid - mean
    inverse = lax.rsqrt(jnp.mean(centered * centered, -1, keepdims=True) + EPSILON)
    return centered * inverse, inverse


def norm_back(scaled, normed, inverse):
    return inverse * (
        scaled
        - jnp.mean(scaled, -1, keepdims=True)
        - normed * jnp.mean(scaled * normed, -1, keepdims=True)
    )


def total_of(refs):
    total = refs[0][...].astype(F32)
    for ref in refs[1:]:
        total = total + ref[...].astype(F32)
    return total


def rows_of(refs, part=slice(None)):
    return jnp.concatenate([ref[part, :] for ref in refs], 0)


def attend_body(first, count, *refs):
    pieces, w_ref = refs[: 2 * count], refs[2 * count]
    qkv_ref, p_ref, o_ref, keep_ref, send_ref = refs[-5:]
    for i in range(count):
        rows = slice(256 * (first + i), 256 * (first + i + 1))
        x = rows_of(pieces[2 * i : 2 * i + 2], slice(0, 128))
        qkv_ref[rows, :] = dot(x, w_ref[:, :768], 1, 0, BF)
        for h in range(2):
            at = h * HEAD
            q = qkv_ref[rows, at : at + HEAD]
            k = qkv_ref[rows, 256 + at : 256 + at + HEAD]
            v = qkv_ref[rows, 512 + at : 512 + at + HEAD]
            s = dot(q, k, 1, 1) * SCALE
            e = jnp.exp(s - jnp.max(s, -1, keepdims=True))
            p = (e / jnp.sum(e, -1, keepdims=True)).astype(BF)
            p_ref[first + i, h] = p
            o_ref[rows, at : at + HEAD] = dot(p, v, 1, 0, BF)
        part = dot(o_ref[rows, :], w_ref[:, 768:1024], 1, 1, BF)
        keep_ref[i] = part[:128]
        send_ref[i] = part[128:]


def attend(first, count, pieces, weights, saved=(), order=()):
    return kernel(
        functools.partial(attend_body, first, count),
        (
            shape((1024, 768)),
            shape((4, 2, 256, 256)),
            shape((1024, 256)),
            shape((count, 128, 2048)),
            shape((count, 128, 2048)),
        ),
        (*pieces, weights, *saved),
        order,
        input_output_aliases={2 * count + 1 + n: n for n in range(3)} if saved else {},
        name="attend",
    )


def attend_back_body(i, ca, cb, qkv_ref, p_ref, w_ref, *refs):
    g_ref, all_ref, keep_ref, send_ref = refs[-4:]
    rows = slice(256 * i, 256 * (i + 1))
    c = rows_of((ca, cb))
    all_ref[rows, :] = c
    go = dot(c, w_ref[:, 768:1024], 1, 0, BF)
    for h in range(2):
        at = h * HEAD
        q = qkv_ref[rows, at : at + HEAD]
        k = qkv_ref[rows, 256 + at : 256 + at + HEAD]
        v = qkv_ref[rows, 512 + at : 512 + at + HEAD]
        low = p_ref[i, h]
        g = go[:, at : at + HEAD]
        g_ref[rows, 512 + at : 512 + at + HEAD] = dot(low, g, 0, 0, BF)
        gp = dot(g, v, 1, 1)
        p = low.astype(F32)
        gs = (p * (gp - jnp.sum(p * gp, -1, keepdims=True))).astype(BF)
        g_ref[rows, at : at + HEAD] = (dot(gs, k, 1, 0) * SCALE).astype(BF)
        g_ref[rows, 256 + at : 256 + at + HEAD] = (dot(gs, q, 0, 0) * SCALE).astype(BF)
    part = dot(g_ref[rows, :], w_ref[:, :768], 1, 1, BF)
    keep_ref[...] = part[:128]
    send_ref[...] = part[128:]


def attend_back(i, ca, cb, weights, qkv, p, saved, order=()):
    more = () if saved is None else saved
    return kernel(
        functools.partial(attend_back_body, i),
        (shape((1024, 768)), shape((1024, 2048)), shape((128, 2048)), shape((128, 2048))),
        (ca, cb, qkv, p, weights, *more),
        order,
        input_output_aliases={5: 0, 6: 1} if more else {},
        name="attend_back",
    )


def feed_body(i, xa, xb, ga, gb, w_ref, *refs):
    act_ref, g_ref, all_ref, keep_ref, send_ref = refs[-5:]
    rows = slice(256 * i, 256 * (i + 1))
    x = rows_of((xa, xb))
    all_ref[rows, :] = x
    final = rows_of((ga, gb), slice(128, 256))
    for at in range(0, 1024, 256):
        u = dot(x, w_ref[:, at : at + 256], 1, 0)
        ga_hidden = dot(final, w_ref[:, 1024 + at : 1280 + at], 1, 0)
        phi = 0.5 + 0.5 * lax.erf(u * 0.5**0.5)
        act_ref[rows, at : at + 256] = (u * phi).astype(BF)
        slope = phi + u * jnp.exp(-0.5 * u * u) * (0.5 / jnp.pi) ** 0.5
        g_ref[rows, at : at + 256] = (ga_hidden * slope).astype(BF)
    part = dot(g_ref[rows, :], w_ref[:, :1024], 1, 1, BF)
    keep_ref[...] = part[:128]
    send_ref[...] = part[128:]


def feed(i, xa, xb, ga, gb, weights, saved, order=()):
    more = () if saved is None else saved
    return kernel(
        functools.partial(feed_body, i),
        (
            shape((1024, 1024)),
            shape((1024, 1024)),
            shape((1024, 2048)),
            shape((128, 2048)),
            shape((128, 2048)),
        ),
        (xa, xb, ga, gb, weights, *more),
        order,
        input_output_aliases={5: 0, 6: 1, 7: 2} if more else {},
        name="feed",
    )


def feed_out_body(act_ref, down_ref, keep_ref, send_ref):
    part = dot(act_ref[...], down_ref[...], 1, 1, BF)
    for i in range(4):
        keep_ref[i] = part[256 * i : 256 * i + 128]
        send_ref[i] = part[256 * i + 128 : 256 * (i + 1)]


def feed_out(act, weights, order=()):
    out = pl.BlockSpec((4, 128, 256), lambda j: (0, 0, j))
    return kernel(
        feed_out_body,
        (far((4, 128, 2048)), far((4, 128, 2048))),
        (out_of(act), out_of(weights)),
        order,
        grid=(8,),
        in_specs=[
            pl.BlockSpec((1024, 1024), lambda j: (0, 0)),
            pl.BlockSpec((256, 1024), lambda j: (j, 1)),
        ],
        out_specs=(out, out),
        name="feed_out",
    )


def feed_grad_body(x, g, act, *refs):
    gm, out = refs[:8], refs[8]
    columns = pl.ds(pl.multiple_of(pl.program_id(0) * 256, 256), 256)
    out[:, :1024] = dot(x[:, columns], g[...], 0, 0, BF)
    gm = jnp.concatenate([ref[128:, columns] for ref in gm], 0)
    out[:, 1024:] = dot(gm, act[...], 0, 0, BF)


def feed_grad(x, g, act, pieces, order=()):
    return kernel(
        feed_grad_body,
        far((2048, 2048)),
        (x, g, act, *pieces),
        order,
        grid=(8,),
        out_specs=pl.BlockSpec((256, 2048), lambda j: (j, 0)),
        name="feed_grad",
    )


def more_grad_body(g, c, o, cross, *refs):
    x, out = refs[:8], refs[8]
    start = pl.multiple_of(pl.program_id(0) * 256, 256)
    columns = pl.ds(start, 256)
    x = jnp.concatenate([ref[:128, columns] for ref in x], 0)
    out[:, :768] = dot(x, g[...], 0, 0, BF)
    out[:, 768:1024] = dot(c[:, columns], o[...], 0, 0, BF)
    out[:, 1024:] = cross[columns, :]


def more_grad(g, c, o, cross, pieces, order=()):
    return kernel(
        more_grad_body,
        far((2048, 1536)),
        (g, c, o, cross, *pieces),
        order,
        grid=(8,),
        out_specs=pl.BlockSpec((256, 1536), lambda j: (j, 0)),
        name="more_grad",
    )


def fold_body(at_ref, kv_ref, w_ref, kv_out, both_ref):
    kv = jnp.sum(kv_ref[...].astype(F32), 0).astype(BF)
    kv_out[...] = kv
    for n in range(4):
        at = n * HEAD
        part = dot(kv[:, at : at + HEAD], w_ref[:, at : at + HEAD], 1, 1, BF)
        for i in range(4):
            away = (i + 4 - at_ref[2]) & 3
            away = jnp.where(away == 0, 0, jnp.where(away == 3, 1, away + 1))
            both_ref[away, n * CAP : (n + 1) * CAP, :] = part[i * CAP : (i + 1) * CAP]


def fold(place, kv, weights, order=()):
    outs = (shape((64, 512)), shape((4, 64, 2048)))
    return kernel(
        fold_body,
        outs,
        (place, kv, out_of(weights)),
        order,
        in_specs=[
            SCALAR,
            pl.BlockSpec((16, 64, 512), lambda j: (0, 0, 0)),
            pl.BlockSpec((2048, 512), lambda j: (0, 2)),
        ],
        out_specs=(
            pl.BlockSpec((64, 512), lambda j: (0, 0)),
            pl.BlockSpec((4, 64, 2048), lambda j: (0, 0, 0)),
        ),
        grid=(1,),
        name="fold",
    )


def unfold_body(at_ref, b0, b1, b2, b3, kv_ref, w_ref, grad_ref, gkv_ref, rows_ref):
    for n in range(4):
        at = n * HEAD
        for away, ref in zip((0, 3, 1, 2), (b0, b1, b2, b3)):
            image = (at_ref[2] + away) & 3
            rows_ref[image] = ref[n * CAP : (n + 1) * CAP, :]
        rows = rows_ref[...].reshape(64, 2048)
        grad_ref[:, at : at + HEAD] = dot(rows, kv_ref[:, at : at + HEAD], 0, 0, BF)
        gkv_ref[:, at : at + HEAD] = dot(rows, w_ref[:, at : at + HEAD], 1, 0, BF)


def unfold(place, back, kv, weights, order=()):
    slot = pl.BlockSpec((64, 2048), lambda j: (0, 0))
    return kernel(
        unfold_body,
        (shape((2048, 512)), shape((64, 512))),
        (place, *back, kv, out_of(weights)),
        order,
        in_specs=[SCALAR]
        + [slot] * 4
        + [
            pl.BlockSpec((64, 512), lambda j: (0, 0)),
            pl.BlockSpec((2048, 512), lambda j: (0, 2)),
        ],
        out_specs=(
            pl.BlockSpec((2048, 512), lambda j: (0, 0)),
            pl.BlockSpec((64, 512), lambda j: (0, 0)),
        ),
        grid=(1,),
        scratch_shapes=[pltpu.VMEM((4, CAP, 2048), BF)],
        name="unfold",
    )


def slots_of(refs, part):
    return jnp.concatenate([ref[i, part, :] for ref in refs for i in range(4)], 0)


def middle_body(length_ref, *refs):
    x, parts, slots = refs[0], refs[1:6], refs[6:8]
    n2_ref, i2_ref, p2_ref, x3_ref, n3_ref, i3_ref = refs[8:]
    x2 = x[...].astype(F32) + total_of(parts)
    normed, inverse = stats(x2)
    low = normed.astype(BF)
    n2_ref[...] = low
    i2_ref[...] = inverse
    m, n = slots_of(slots, slice(0, 32)), slots_of(slots, slice(32, 64))
    s = (dot(m, low, 1, 1) * SCALE).reshape(16, CAP, 128)
    live = lax.broadcasted_iota(jnp.int32, (1, CAP, 1), 1) < length_ref[0]
    s = jnp.where(live, s, -1e30)
    e = jnp.exp(s - jnp.max(s, 1, keepdims=True))
    p = (e / jnp.sum(e, 1, keepdims=True)).reshape(256, 128)
    p2_ref[...] = p
    x3 = x2 + dot(p.astype(BF), n, 0, 0)
    x3_ref[...] = x3
    normed, inverse = stats(x3)
    n3_ref[...] = normed.astype(BF)
    i3_ref[...] = inverse


def middle(length, x, parts, slots, order=()):
    column = shape((128, 1), F32)
    return kernel(
        middle_body,
        (
            shape((128, 2048)),
            column,
            shape((256, 128), F32),
            shape((128, 2048), F32),
            shape((128, 2048)),
            column,
        ),
        (length, x, *parts, *slots),
        order,
        in_specs=[SCALAR] + [WHOLE] * 8,
        name="middle",
    )


def middle_back_body(*refs):
    g3, parts, slots = refs[0], refs[1:6], refs[6:8]
    n2, i2, p2, n3, i3 = refs[8:13]
    g1_ref, low_ref, keep_ref, send_ref = refs[13:]
    g2 = g3[...].astype(F32) + norm_back(total_of(parts), n3[...].astype(F32), i3[...])
    c = g2.astype(BF)
    m, n = slots_of(slots, slice(0, 32)), slots_of(slots, slice(32, 64))
    p = p2[...].reshape(16, CAP, 128)
    gp = dot(n, c, 1, 1).reshape(16, CAP, 128)
    gs = (p * (gp - jnp.sum(p * gp, 1, keepdims=True))).reshape(256, 128) * SCALE
    gs = gs.astype(BF)
    g1 = g2 + norm_back(dot(gs, m, 0, 0), n2[...].astype(F32), i2[...])
    g1_ref[...] = g1
    low_ref[...] = g1.astype(BF)
    gm = dot(gs, n2[...], 1, 0, BF)
    gn = dot(p2[...].astype(BF), c, 1, 0, BF)
    for out, at in ((keep_ref, 0), (send_ref, 128)):
        for i in range(4):
            rows = slice(at + 32 * i, at + 32 * (i + 1))
            out[i, :32, :] = gm[rows]
            out[i, 32:, :] = gn[rows]


def middle_back(g3, parts, slots, n2, i2, p2, n3, i3, order=()):
    slot = shape((4, 64, 2048))
    outs = (shape((128, 2048), F32), shape((128, 2048)), slot, slot)
    args = (g3, *parts, *slots, n2, i2, p2, n3, i3)
    return kernel(middle_back_body, outs, args, order, name="middle_back")


def last_body(*refs):
    g1, parts, x, out = refs[0], refs[1:6], refs[6], refs[7]
    normed, inverse = stats(x[...].astype(F32))
    out[...] = g1[...] + norm_back(total_of(parts), normed, inverse)


def last(g1, parts, x, order=()):
    return kernel(last_body, shape((128, 2048), F32), (g1, *parts, x), order, name="last")


def mix_features(value):
    n = value.shape[0]
    return value.reshape(n, 2, 16, 64).transpose(0, 2, 1, 3).reshape(n, 2048)


def unmix_features(value):
    n = value.shape[0]
    return value.reshape(n, 16, 2, 64).transpose(0, 2, 1, 3).reshape(n, 2048)


def per_device(
    image_tokens,
    caption_embed,
    caption_lengths,
    output_grad,
    norm_self,
    norm_cross,
    norm_feed,
    self_query,
    self_key,
    self_value,
    self_output,
    cross_query,
    cross_key,
    cross_value,
    cross_output,
    up_weight,
    down_weight,
):
    xh = lax.axis_index("xh")
    xl = lax.axis_index("xl")
    core = lax.axis_index("c")
    place = [lax.axis_index("y"), lax.axis_index("z"), 2 * xh + xl, core]
    place = jnp.stack(place).astype(jnp.int32)
    gain_one = norm_self.astype(F32)[:, None]
    gain_two = norm_cross.astype(F32)[:, None]
    gain_three = norm_feed.astype(F32)[:, None]

    def gained(weight, gain):
        return (weight.astype(F32) * gain).astype(BF)

    def halves(weight):
        n = weight.shape[1] // 2
        first, second = weight[:, :n], weight[:, n:]
        return jnp.where(xh == 0, first, second), jnp.where(xh == 0, second, first)

    def in_order(mine, theirs):
        return jnp.where(xh == 0, mine, theirs), jnp.where(xh == 0, theirs, mine)

    def exchange(weights):
        pairs = [halves(w) for w in weights]
        mine = jnp.concatenate([p[0] for p in pairs], 1)
        theirs = swap(jnp.concatenate([p[1] for p in pairs], 1), "xh")
        return jnp.stack(in_order(mine, theirs), 0)

    def home(first, second):
        keep = jnp.where(xh == 0, first, second)
        theirs = swap(jnp.where(xh == 0, second, first).astype(BF), "xh")
        return keep, theirs.astype(F32)

    def join(keep, theirs):
        return jnp.concatenate(in_order(keep, theirs), 1)

    pair = exchange(
        (
            gained(self_query, gain_one),
            gained(self_key, gain_one),
            gained(self_value, gain_one),
            self_output.T,
            gained(cross_query, gain_two),
            cross_output.T,
        )
    )
    first = lax.all_gather(pair.reshape(128, 1536), PLANE, axis=0, tiled=True)
    pair_late = exchange(
        (
            after(gained(up_weight, gain_three), pair),
            down_weight.T,
            cross_key[:64],
            cross_value[:64],
            cross_key[64:],
            cross_value[64:],
        )
    )
    pair_kv = jnp.stack([pair_late[:, :, 2048:2560], pair_late[:, :, 2560:]], 1)
    pair_kv = pair_kv.reshape(256, 512)
    resid = mix_features(image_tokens[0])
    normed_one, _ = stats(resid.astype(F32))
    grad_low = mix_features(output_grad[0])
    caption = after(caption_embed[0], pair)
    caption = lax.all_gather(caption, ("xh", "xl", "c"), axis=0, tiled=True)
    caption = caption.reshape(64, 2, 16, 128).transpose(2, 0, 1, 3).reshape(16, 64, 256)
    tokens = after(jnp.concatenate([normed_one.astype(BF), grad_low], 0), caption)
    pieces = [tokens, px(tokens, 1), px(tokens, -1)]
    across = far_of(pieces[1], pieces[2])
    tokens = [side for piece in pieces[:2] for side in (piece, swap(piece, "c"))]
    *saved, keep, send = attend(0, 2, tokens, first, (), across)
    pieces.append(jnp.concatenate(across, 0))
    tokens += [side for piece in pieces[2:] for side in (piece, swap(piece, "c"))]
    other = swap(send, "c")
    feed_weight = pair_late[:, :, :2048].reshape(128, 2048)
    feed_weight = lax.all_gather(feed_weight, PLANE, axis=0, tiled=True)
    caption = lax.all_to_all(caption, PLANE, split_axis=0, concat_axis=0, tiled=True)
    caption = caption.reshape(1024, 256)
    kv = dot(caption, pair_kv, 1, 0, BF).reshape(16, 64, 512)
    kv = lax.all_to_all(kv, PLANE, split_axis=0, concat_axis=0, tiled=True)
    kv, both = fold(place, kv.reshape(16, 64, 512), first, [keep])
    kv_weight = lax.all_gather(after(pair_kv, kv), PLANE, axis=0, tiled=True)
    slots_come = [px(both[1], -1), px(both[2], 1), px(both[3], 2)]
    slots = jnp.stack([both[0], *slots_come], 0)
    slots = (slots, swap(slots, "c"))

    qkv, p1, o1, keep_more, send = attend(2, 2, tokens[4:], first, saved, [*slots_come, other])
    more = swap(send, "c")
    parts, _ = reduce_tokens([*keep, *keep_more], [*other, *more])
    length = jnp.where(xl == 0, caption_lengths[0, 0], caption_lengths[0, 1])[None]
    n2, i2, p2, x3, n3, i3 = middle(length, resid, parts, slots)

    theirs = swap(n3, "c")
    around = [px(n3, 1), px(n3, -1)]
    saved, keeps, others = None, [], []
    for i in range(4):
        if i == 0:
            mine = n3
        else:
            if i == 1:
                around = [hold(piece, keeps[:1]) for piece in around]
                across = far_of(*around)
            if i < 3:
                mine = around[i - 1]
            else:
                mine = jnp.concatenate([hold(piece, keeps[1:2]) for piece in across], 0)
            theirs = swap(mine, "c")
        *saved, keep, send = feed(
            i,
            mine,
            theirs,
            tokens[2 * i],
            tokens[2 * i + 1],
            feed_weight,
            saved and tuple(saved),
            others[:-1][-1:],
        )
        keeps.append(keep)
        others.append(swap(send, "c"))
    parts, low = reduce_tokens(keeps, others)
    act, grad, x3_all = saved
    total = feed_grad(x3_all, grad, act, tokens, low + [kv_weight])
    total = hold(total, parts[2:], True)
    g1, c1, keep_slots, send_slots = middle_back(
        grad_low, parts, slots, n2, i2, p2, n3, i3, [total]
    )
    total = lax.psum_scatter(total, PLANE, scatter_dimension=0, tiled=True)
    own, their_ff = home(total[:64], total[64:])
    own = own.astype(F32)
    up_out = join(own[:, :1024], their_ff[:, :1024])
    down_out = join(own[:, 1024:], their_ff[:, 1024:])

    theirs = swap(c1, "c")
    around = [px(c1, 1), px(c1, -1)]
    slot_back = keep_slots.astype(F32) + swap(send_slots, "c").astype(F32)
    back, keeps, others = None, [], []
    for i in range(4):
        if i == 0:
            mine = c1
        else:
            if i == 1:
                around = [hold(piece, keeps[:1]) for piece in around]
                across = far_of(*around)
                slot_back = after(slot_back.astype(BF), around[1])
                slot_back = [
                    slot_back[0],
                    px(slot_back[1], 1),
                    px(slot_back[2], -1),
                    px(slot_back[3], 2),
                ]
            if i < 3:
                mine = around[i - 1]
            else:
                mine = jnp.concatenate([hold(piece, keeps[1:2]) for piece in across], 0)
            theirs = swap(mine, "c")
        order = others[:-1][-1:] + (slot_back[1:] if i == 3 else [])
        *back, keep, send = attend_back(
            i, mine, theirs, first, qkv, p1, back and tuple(back), order
        )
        keeps.append(keep)
        others.append(swap(send, "c"))
    parts, low = reduce_tokens(keeps, others)
    cross_grad, grad_kv = unfold(place, slot_back, kv, first)
    more = more_grad(*back, o1, cross_grad, tokens, keeps[-1:])
    y_keep, y_send = feed_out(act, feed_weight, low[-1:])
    more = hold(more, [total, y_keep], True)
    rest = lax.psum_scatter(more, PLANE, scatter_dimension=0, tiled=True)
    y_parts, _ = reduce_tokens(y_keep, swap(y_send, "c"))
    block_out = x3
    for part in y_parts:
        block_out = block_out + part.astype(F32)
    grad_kv = after(grad_kv, more)
    kv_all = lax.all_to_all(
        jnp.broadcast_to(grad_kv[None], (16, 64, 512)), PLANE, split_axis=0, concat_axis=0, tiled=True
    ).reshape(1024, 512)
    kv_grad = dot(caption, kv_all, 0, 0)
    ck_own, ck_their = home(kv_grad[:128], kv_grad[128:])
    ck_out = join(ck_own[:, :256], ck_their[:, :256])
    cv_out = join(ck_own[:, 256:], ck_their[:, 256:])
    cap_grad = dot(grad_kv, kv_weight, 1, 1, BF).reshape(4, 16, 4096)
    keep = jnp.where(core == 0, cap_grad[:, :8], cap_grad[:, 8:])
    send = jnp.where(core == 0, cap_grad[:, 8:], cap_grad[:, :8])
    send = swap(send, "c")
    low_cap = (keep.astype(F32) + send.astype(F32)).astype(BF)
    near_image = [pick(low_cap, place[2] + n) for n in range(4)]
    cap_out = near_image[0].astype(F32)
    for n in (1, 2, 3):
        cap_out = cap_out + px(near_image[n], n).astype(F32)
    cap_out = cap_out.reshape(8, 16, 2, 128).transpose(0, 2, 1, 3).reshape(1, 8, 4096)
    rest = hold(rest, y_parts[2:], True)
    own, their = home(rest[:64], rest[64:])
    own = own.astype(F32)
    outs = [join(own[:, at : at + 256], their[:, at : at + 256]) for at in range(0, 1536, 256)]
    so_out, cq_out, co_out = outs[3:]

    image_grad = unmix_features(last(g1, parts, resid))[None]

    first_gain = (
        jnp.sum(outs[0] * self_query.astype(F32), 1)
        + jnp.sum(outs[1] * self_key.astype(F32), 1)
        + jnp.sum(outs[2] * self_value.astype(F32), 1)
    )
    terms = jnp.stack(
        [
            first_gain,
            jnp.sum(cq_out * cross_query.astype(F32), 1),
            jnp.sum(up_out * up_weight.astype(F32), 1),
        ],
        0,
    )
    terms = terms + swap(terms, "xl")
    terms = terms + swap(terms, "c")

    return (
        unmix_features(block_out.astype(BF))[None],
        image_grad,
        cap_out,
        terms[0],
        terms[1],
        terms[2],
        outs[0] * gain_one,
        outs[1] * gain_one,
        outs[2] * gain_one,
        so_out.T,
        cq_out * gain_two,
        ck_out,
        cv_out,
        co_out.T,
        up_out * gain_three,
        down_out.T,
    )


def solution(mesh):
    names = ("xh", "y", "z", "xl", "c")
    fine = Mesh(mesh.devices.reshape(2, 4, 4, 2, 2), names)
    rows, text = ("xh", "y", "z"), ("xl", "c")
    tokens = P(rows, text, None)
    by_row = P(rows, text)
    by_text = P(text, rows)
    weights = (by_row, by_row, by_row, by_text, by_row, by_row, by_row, by_text, by_row, by_text)
    in_specs = (tokens, tokens, P(rows, None), tokens) + (P(rows),) * 3 + weights
    out_specs = (tokens,) * 3 + (P(rows),) * 3 + weights
    return jax.shard_map(
        per_device, mesh=fine, in_specs=in_specs, out_specs=out_specs, check_vma=False
    )
```

```python
import functools

import jax
import jax.numpy as jnp
from jax import lax
from jax.experimental import pallas as pl
from jax.experimental.pallas import tpu as pltpu
from jax.sharding import Mesh, PartitionSpec as P

HEAD = 128
CAP = 16
EPSILON = 1e-05
SCALE = HEAD ** (-0.5)
BF = jnp.bfloat16
F32 = jnp.float32
RING = ("xh", "xl")
PLANE = ("y", "z")
WHOLE = pl.BlockSpec(memory_space=pltpu.VMEM)
HBM = pl.BlockSpec(memory_space=pltpu.MemorySpace.HBM)
ANY = pl.BlockSpec(memory_space=pl.ANY)
SCALAR = pl.BlockSpec(memory_space=pltpu.SMEM)


def shape(dims, dtype=BF):
    return jax.ShapeDtypeStruct(dims, dtype)


def out_of(value):
    return pltpu.with_memory_space_constraint(value, pltpu.MemorySpace.HBM)


def far(dims, dtype=BF):
    return pltpu.MemorySpace.HBM(dims, dtype)


def kernel(body, outs, args, order=(), vmem=12, in_specs=None, out_specs=None, **more):
    order = [out_of(dep) if dep.size >= 2**20 else dep for dep in order]
    n, outer = len(order), body
    if in_specs is None:
        in_specs = [WHOLE] * len(args)
    if out_specs is None:
        out_specs = jax.tree.map(lambda _: WHOLE, outs)
    spec = more.pop("grid_spec", None)
    if n:
        m = len(args)

        def outer(*refs):
            body(*refs[:m], *refs[m + n :])

    specs = dict(in_specs=list(in_specs) + [HBM] * n, out_specs=out_specs)
    if spec is not None:
        scalars, grid, scratch = spec
        specs = dict(
            grid_spec=pltpu.PrefetchScalarGridSpec(
                num_scalar_prefetch=scalars, grid=grid, scratch_shapes=scratch, **specs
            )
        )
    return pl.pallas_call(
        outer,
        out_shape=outs,
        compiler_params=pltpu.CompilerParams(vmem_limit_bytes=vmem * 2**20),
        cost_estimate=pl.CostEstimate(flops=1000, bytes_accessed=1000, transcendentals=0),
        **specs,
        **more,
    )(*args, *order)


def hold_body(value, out):
    pass


def hold(value, order, away=False):
    return kernel(
        hold_body,
        far(value.shape, value.dtype) if away else shape(value.shape, value.dtype),
        (out_of(value) if away else value,),
        order,
        vmem=4,
        in_specs=[ANY],
        out_specs=ANY,
        input_output_aliases={0: 0},
        name="hold",
    )


def dot(a, b, ca, cb, out=F32):
    return lax.dot_general(a, b, (((ca,), (cb,)), ((), ())), preferred_element_type=F32).astype(out)


def px(value, step):
    return lax.ppermute(value, RING, [(i, (i + step) % 4) for i in range(4)])


def pp(value, axis, step):
    return lax.ppermute(value, axis, [(i, (i + step) % 4) for i in range(4)])


def swap(value, axis):
    return lax.ppermute(value, axis, [(0, 1), (1, 0)])


def after(value, dep):
    first = dep[(slice(0, 1),) * dep.ndim].reshape((1,) * value.ndim).astype(F32)
    return (value.astype(F32) + first * 0.0).astype(value.dtype)


def far_of(left, right):
    half = left.shape[0] // 2
    return [px(left[:half], 1), px(right[half:], -1)]


def pick(value, at):
    return lax.dynamic_index_in_dim(value, at & 3, 0, False, allow_negative_indices=False)


def reduce_tokens(keep, other):
    low = [(keep[i].astype(F32) + other[i].astype(F32)).astype(BF) for i in range(1, 4)]
    return [keep[0], other[0], px(low[0], -1), px(low[1], 1), px(low[2], 2)], low


def stats(resid):
    mean = jnp.mean(resid, -1, keepdims=True)
    centered = resid - mean
    inverse = lax.rsqrt(jnp.mean(centered * centered, -1, keepdims=True) + EPSILON)
    return centered * inverse, inverse


def norm_back(scaled, normed, inverse):
    return inverse * (
        scaled
        - jnp.mean(scaled, -1, keepdims=True)
        - normed * jnp.mean(scaled * normed, -1, keepdims=True)
    )


def total_of(refs):
    total = refs[0][...].astype(F32)
    for ref in refs[1:]:
        total = total + ref[...].astype(F32)
    return total


def rows_of(refs, part=slice(None)):
    return jnp.concatenate([ref[part, :] for ref in refs], 0)


def attend_body(first, count, *refs):
    pieces, w_ref = refs[: 2 * count], refs[2 * count]
    qkv_ref, p_ref, o_ref, keep_ref, send_ref = refs[-5:]
    for i in range(count):
        rows = slice(256 * (first + i), 256 * (first + i + 1))
        x = rows_of(pieces[2 * i : 2 * i + 2], slice(0, 128))
        qkv_ref[rows, :] = dot(x, w_ref[:, :768], 1, 0, BF)
        for h in range(2):
            at = h * HEAD
            q = qkv_ref[rows, at : at + HEAD]
            k = qkv_ref[rows, 256 + at : 256 + at + HEAD]
            v = qkv_ref[rows, 512 + at : 512 + at + HEAD]
            s = dot(q, k, 1, 1) * SCALE
            e = jnp.exp(s - jnp.max(s, -1, keepdims=True))
            p = (e / jnp.sum(e, -1, keepdims=True)).astype(BF)
            p_ref[first + i, h] = p
            o_ref[rows, at : at + HEAD] = dot(p, v, 1, 0, BF)
        part = dot(o_ref[rows, :], w_ref[:, 768:1024], 1, 1, BF)
        keep_ref[i] = part[:128]
        send_ref[i] = part[128:]


def attend(first, count, pieces, weights, saved=(), order=()):
    return kernel(
        functools.partial(attend_body, first, count),
        (
            shape((1024, 768)),
            shape((4, 2, 256, 256)),
            shape((1024, 256)),
            shape((count, 128, 2048)),
            shape((count, 128, 2048)),
        ),
        (*pieces, weights, *saved),
        order,
        input_output_aliases={2 * count + 1 + n: n for n in range(3)} if saved else {},
        name="attend",
    )


def attend_back_body(i, ca, cb, qkv_ref, p_ref, w_ref, *refs):
    g_ref, all_ref, keep_ref, send_ref = refs[-4:]
    rows = slice(256 * i, 256 * (i + 1))
    c = rows_of((ca, cb))
    all_ref[rows, :] = c
    go = dot(c, w_ref[:, 768:1024], 1, 0, BF)
    for h in range(2):
        at = h * HEAD
        q = qkv_ref[rows, at : at + HEAD]
        k = qkv_ref[rows, 256 + at : 256 + at + HEAD]
        v = qkv_ref[rows, 512 + at : 512 + at + HEAD]
        low = p_ref[i, h]
        g = go[:, at : at + HEAD]
        g_ref[rows, 512 + at : 512 + at + HEAD] = dot(low, g, 0, 0, BF)
        gp = dot(g, v, 1, 1)
        p = low.astype(F32)
        gs = (p * (gp - jnp.sum(p * gp, -1, keepdims=True))).astype(BF)
        g_ref[rows, at : at + HEAD] = (dot(gs, k, 1, 0) * SCALE).astype(BF)
        g_ref[rows, 256 + at : 256 + at + HEAD] = (dot(gs, q, 0, 0) * SCALE).astype(BF)
    part = dot(g_ref[rows, :], w_ref[:, :768], 1, 1, BF)
    keep_ref[...] = part[:128]
    send_ref[...] = part[128:]


def attend_back(i, ca, cb, weights, qkv, p, saved, order=()):
    more = () if saved is None else saved
    return kernel(
        functools.partial(attend_back_body, i),
        (shape((1024, 768)), shape((1024, 2048)), shape((128, 2048)), shape((128, 2048))),
        (ca, cb, qkv, p, weights, *more),
        order,
        input_output_aliases={5: 0, 6: 1} if more else {},
        name="attend_back",
    )


def feed_body(i, xa, xb, ga, gb, w_ref, *refs):
    act_ref, g_ref, all_ref, keep_ref, send_ref = refs[-5:]
    rows = slice(256 * i, 256 * (i + 1))
    x = rows_of((xa, xb))
    all_ref[rows, :] = x
    final = rows_of((ga, gb), slice(128, 256))
    for at in range(0, 1024, 256):
        u = dot(x, w_ref[:, at : at + 256], 1, 0)
        ga_hidden = dot(final, w_ref[:, 1024 + at : 1280 + at], 1, 0)
        phi = 0.5 + 0.5 * lax.erf(u * 0.5**0.5)
        act_ref[rows, at : at + 256] = (u * phi).astype(BF)
        slope = phi + u * jnp.exp(-0.5 * u * u) * (0.5 / jnp.pi) ** 0.5
        g_ref[rows, at : at + 256] = (ga_hidden * slope).astype(BF)
    part = dot(g_ref[rows, :], w_ref[:, :1024], 1, 1, BF)
    keep_ref[...] = part[:128]
    send_ref[...] = part[128:]


def feed(i, xa, xb, ga, gb, weights, saved, order=()):
    more = () if saved is None else saved
    return kernel(
        functools.partial(feed_body, i),
        (
            shape((1024, 1024)),
            shape((1024, 1024)),
            shape((1024, 2048)),
            shape((128, 2048)),
            shape((128, 2048)),
        ),
        (xa, xb, ga, gb, weights, *more),
        order,
        input_output_aliases={5: 0, 6: 1, 7: 2} if more else {},
        name="feed",
    )


def feed_out_body(act_ref, down_ref, keep_ref, send_ref):
    part = dot(act_ref[...], down_ref[...], 1, 1, BF)
    for i in range(4):
        keep_ref[i] = part[256 * i : 256 * i + 128]
        send_ref[i] = part[256 * i + 128 : 256 * (i + 1)]


def feed_out(act, weights, order=()):
    out = pl.BlockSpec((4, 128, 256), lambda j: (0, 0, j))
    return kernel(
        feed_out_body,
        (far((4, 128, 2048)), far((4, 128, 2048))),
        (out_of(act), out_of(weights)),
        order,
        grid=(8,),
        in_specs=[
            pl.BlockSpec((1024, 1024), lambda j: (0, 0)),
            pl.BlockSpec((256, 1024), lambda j: (j, 1)),
        ],
        out_specs=(out, out),
        name="feed_out",
    )


def feed_grad_body(x, g, act, *refs):
    gm, out = refs[:8], refs[8]
    columns = pl.ds(pl.multiple_of(pl.program_id(0) * 256, 256), 256)
    out[:, :1024] = dot(x[:, columns], g[...], 0, 0, BF)
    out[:, 1024:] = dot(rows_of(gm), act[...], 0, 0, BF)


def feed_grad(x, g, act, pieces, order=()):
    return kernel(
        feed_grad_body,
        far((2048, 2048)),
        (x, g, act, *map(out_of, pieces)),
        order,
        grid=(8,),
        in_specs=[WHOLE] * 3 + [pl.BlockSpec((128, 256), lambda j: (1, j))] * 8,
        out_specs=pl.BlockSpec((256, 2048), lambda j: (j, 0)),
        name="feed_grad",
    )


def more_grad_body(g, c, o, cross, *refs):
    x, out = refs[:8], refs[8]
    start = pl.multiple_of(pl.program_id(0) * 256, 256)
    columns = pl.ds(start, 256)
    out[:, :768] = dot(rows_of(x), g[...], 0, 0, BF)
    out[:, 768:1024] = dot(c[:, columns], o[...], 0, 0, BF)
    out[:, 1024:] = cross[columns, :]


def more_grad(g, c, o, cross, pieces, order=()):
    return kernel(
        more_grad_body,
        far((2048, 1536)),
        (g, c, o, cross, *map(out_of, pieces)),
        order,
        grid=(8,),
        in_specs=[WHOLE] * 4 + [pl.BlockSpec((128, 256), lambda j: (0, j))] * 8,
        out_specs=pl.BlockSpec((256, 1536), lambda j: (j, 0)),
        name="more_grad",
    )


def fold_body(at_ref, kv_ref, w_ref, kv_out, both_ref):
    kv = jnp.sum(kv_ref[...].astype(F32), 0).astype(BF)
    kv_out[...] = kv
    for n in range(4):
        at = n * HEAD
        part = dot(kv[:, at : at + HEAD], w_ref[:, at : at + HEAD], 1, 1, BF)
        for i in range(4):
            away = (i + 4 - at_ref[2]) & 3
            away = jnp.where(away == 0, 0, jnp.where(away == 3, 1, away + 1))
            both_ref[away, n * CAP : (n + 1) * CAP, :] = part[i * CAP : (i + 1) * CAP]


def fold(place, kv, weights, order=()):
    outs = (shape((64, 512)), shape((4, 64, 2048)))
    return kernel(
        fold_body,
        outs,
        (place, kv, out_of(weights)),
        order,
        in_specs=[
            SCALAR,
            pl.BlockSpec((16, 64, 512), lambda j: (0, 0, 0)),
            pl.BlockSpec((2048, 512), lambda j: (0, 2)),
        ],
        out_specs=(
            pl.BlockSpec((64, 512), lambda j: (0, 0)),
            pl.BlockSpec((4, 64, 2048), lambda j: (0, 0, 0)),
        ),
        grid=(1,),
        name="fold",
    )


def unfold_body(at_ref, b0, b1, b2, b3, kv_ref, w_ref, grad_ref, gkv_ref, rows_ref):
    for n in range(4):
        at = n * HEAD
        for away, ref in zip((0, 3, 1, 2), (b0, b1, b2, b3)):
            image = (at_ref[2] + away) & 3
            rows_ref[image] = ref[n * CAP : (n + 1) * CAP, :]
        rows = rows_ref[...].reshape(64, 2048)
        grad_ref[:, at : at + HEAD] = dot(rows, kv_ref[:, at : at + HEAD], 0, 0, BF)
        gkv_ref[:, at : at + HEAD] = dot(rows, w_ref[:, at : at + HEAD], 1, 0, BF)


def unfold(place, back, kv, weights, order=()):
    slot = pl.BlockSpec((64, 2048), lambda j: (0, 0))
    return kernel(
        unfold_body,
        (shape((2048, 512)), shape((64, 512))),
        (place, *back, kv, out_of(weights)),
        order,
        in_specs=[SCALAR]
        + [slot] * 4
        + [
            pl.BlockSpec((64, 512), lambda j: (0, 0)),
            pl.BlockSpec((2048, 512), lambda j: (0, 2)),
        ],
        out_specs=(
            pl.BlockSpec((2048, 512), lambda j: (0, 0)),
            pl.BlockSpec((64, 512), lambda j: (0, 0)),
        ),
        grid=(1,),
        scratch_shapes=[pltpu.VMEM((4, CAP, 2048), BF)],
        name="unfold",
    )


def slots_of(refs, part):
    return jnp.concatenate([ref[i, part, :] for ref in refs for i in range(4)], 0)


def middle_body(length_ref, *refs):
    x, parts, slots = refs[0], refs[1:6], refs[6:8]
    n2_ref, i2_ref, p2_ref, x3_ref, n3_ref, i3_ref = refs[8:]
    x2 = x[...].astype(F32) + total_of(parts)
    normed, inverse = stats(x2)
    low = normed.astype(BF)
    n2_ref[...] = low
    i2_ref[...] = inverse
    m, n = slots_of(slots, slice(0, 32)), slots_of(slots, slice(32, 64))
    s = (dot(m, low, 1, 1) * SCALE).reshape(16, CAP, 128)
    live = lax.broadcasted_iota(jnp.int32, (1, CAP, 1), 1) < length_ref[0]
    s = jnp.where(live, s, -1e30)
    e = jnp.exp(s - jnp.max(s, 1, keepdims=True))
    p = (e / jnp.sum(e, 1, keepdims=True)).reshape(256, 128)
    p2_ref[...] = p
    x3 = x2 + dot(p.astype(BF), n, 0, 0)
    x3_ref[...] = x3
    normed, inverse = stats(x3)
    n3_ref[...] = normed.astype(BF)
    i3_ref[...] = inverse


def middle(length, x, parts, slots, order=()):
    column = shape((128, 1), F32)
    return kernel(
        middle_body,
        (
            shape((128, 2048)),
            column,
            shape((256, 128), F32),
            shape((128, 2048), F32),
            shape((128, 2048)),
            column,
        ),
        (length, x, *parts, *slots),
        order,
        vmem=16,
        in_specs=[SCALAR] + [WHOLE] * 8,
        name="middle",
    )


def middle_back_body(*refs):
    g3, parts, slots = refs[0], refs[1:6], refs[6:8]
    n2, i2, p2, n3, i3 = refs[8:13]
    g1_ref, low_ref, keep_ref, send_ref = refs[13:]
    g2 = g3[...].astype(F32) + norm_back(total_of(parts), n3[...].astype(F32), i3[...])
    c = g2.astype(BF)
    m, n = slots_of(slots, slice(0, 32)), slots_of(slots, slice(32, 64))
    p = p2[...].reshape(16, CAP, 128)
    gp = dot(n, c, 1, 1).reshape(16, CAP, 128)
    gs = (p * (gp - jnp.sum(p * gp, 1, keepdims=True))).reshape(256, 128) * SCALE
    gs = gs.astype(BF)
    g1 = g2 + norm_back(dot(gs, m, 0, 0), n2[...].astype(F32), i2[...])
    g1_ref[...] = g1
    low_ref[...] = g1.astype(BF)
    gm = dot(gs, n2[...], 1, 0, BF)
    gn = dot(p2[...].astype(BF), c, 1, 0, BF)
    for out, at in ((keep_ref, 0), (send_ref, 128)):
        for i in range(4):
            rows = slice(at + 32 * i, at + 32 * (i + 1))
            out[i, :32, :] = gm[rows]
            out[i, 32:, :] = gn[rows]


def middle_back(g3, parts, slots, n2, i2, p2, n3, i3, order=()):
    slot = shape((4, 64, 2048))
    outs = (shape((128, 2048), F32), shape((128, 2048)), slot, slot)
    args = (g3, *parts, *slots, n2, i2, p2, n3, i3)
    return kernel(middle_back_body, outs, args, order, vmem=16, name="middle_back")


def last_body(*refs):
    g1, parts, x, out = refs[0], refs[1:6], refs[6], refs[7]
    normed, inverse = stats(x[...].astype(F32))
    out[...] = g1[...] + norm_back(total_of(parts), normed, inverse)


def last(g1, parts, x, order=()):
    return kernel(last_body, shape((128, 2048), F32), (g1, *parts, x), order, name="last")


def mix_features(value):
    n = value.shape[0]
    return value.reshape(n, 2, 16, 64).transpose(0, 2, 1, 3).reshape(n, 2048)


def unmix_features(value):
    n = value.shape[0]
    return value.reshape(n, 16, 2, 64).transpose(0, 2, 1, 3).reshape(n, 2048)


def per_device(
    image_tokens,
    caption_embed,
    caption_lengths,
    output_grad,
    norm_self,
    norm_cross,
    norm_feed,
    self_query,
    self_key,
    self_value,
    self_output,
    cross_query,
    cross_key,
    cross_value,
    cross_output,
    up_weight,
    down_weight,
):
    xh = lax.axis_index("xh")
    xl = lax.axis_index("xl")
    core = lax.axis_index("c")
    place = [lax.axis_index("y"), lax.axis_index("z"), 2 * xh + xl, core]
    place = jnp.stack(place).astype(jnp.int32)
    gain_one = norm_self.astype(F32)[:, None]
    gain_two = norm_cross.astype(F32)[:, None]
    gain_three = norm_feed.astype(F32)[:, None]

    def gained(weight, gain):
        return (weight.astype(F32) * gain).astype(BF)

    def halves(weight):
        n = weight.shape[1] // 2
        first, second = weight[:, :n], weight[:, n:]
        return jnp.where(xh == 0, first, second), jnp.where(xh == 0, second, first)

    def in_order(mine, theirs):
        return jnp.where(xh == 0, mine, theirs), jnp.where(xh == 0, theirs, mine)

    def exchange(weights):
        pairs = [halves(w) for w in weights]
        mine = jnp.concatenate([p[0] for p in pairs], 1)
        theirs = swap(jnp.concatenate([p[1] for p in pairs], 1), "xh")
        return jnp.stack(in_order(mine, theirs), 0)

    def home(first, second):
        keep = jnp.where(xh == 0, first, second)
        theirs = swap(jnp.where(xh == 0, second, first).astype(BF), "xh")
        return keep, theirs.astype(F32)

    def join(keep, theirs):
        return jnp.concatenate(in_order(keep, theirs), 1)

    pair = exchange(
        (
            gained(self_query, gain_one),
            gained(self_key, gain_one),
            gained(self_value, gain_one),
            self_output.T,
            gained(cross_query, gain_two),
            cross_output.T,
        )
    )
    first = lax.all_gather(pair.reshape(128, 1536), PLANE, axis=0, tiled=True)
    resid = mix_features(image_tokens[0])
    normed_one, _ = stats(resid.astype(F32))
    grad_low = mix_features(output_grad[0])
    tokens = after(jnp.concatenate([normed_one.astype(BF), grad_low], 0), pair)
    pieces = [tokens, px(tokens, 1), px(tokens, -1)]
    caption = after(after(caption_embed[0], pieces[1]), pieces[2])
    caption = lax.all_gather(caption, ("xh", "xl", "c"), axis=0, tiled=True)
    caption = caption.reshape(64, 2, 16, 128).transpose(2, 0, 1, 3).reshape(16, 64, 256)
    pieces.append(jnp.concatenate(far_of(pieces[1], pieces[2]), 0))
    tokens = [side for piece in pieces for side in (piece, swap(piece, "c"))]
    pair_late = exchange(
        (
            after(gained(up_weight, gain_three), caption),
            down_weight.T,
            cross_key[:64],
            cross_value[:64],
            cross_key[64:],
            cross_value[64:],
        )
    )
    pair_kv = jnp.stack([pair_late[:, :, 2048:2560], pair_late[:, :, 2560:]], 1)
    pair_kv = pair_kv.reshape(256, 512)
    feed_weight = pair_late[:, :, :2048].reshape(128, 2048)
    feed_weight = lax.all_gather(feed_weight, PLANE, axis=0, tiled=True)
    caption = lax.all_to_all(caption, PLANE, split_axis=0, concat_axis=0, tiled=True)
    caption = caption.reshape(1024, 256)
    kv = dot(caption, pair_kv, 1, 0, BF).reshape(16, 64, 512)
    kv = lax.all_to_all(kv, PLANE, split_axis=0, concat_axis=0, tiled=True)
    qkv, p1, o1, keep, send = attend(0, 4, tokens, first)
    kv, both = fold(place, kv.reshape(16, 64, 512), first, [keep])
    kv_weight = lax.all_gather(after(pair_kv, kv), PLANE, axis=0, tiled=True)
    parts, low = reduce_tokens(keep, swap(send, "c"))
    both = hold(both, parts[2:4])
    slots_come = [px(both[1], -1), px(both[2], 1), px(both[3], 2)]
    slots = jnp.stack([both[0], *slots_come], 0)
    slots = (slots, swap(slots, "c"))

    length = jnp.where(xl == 0, caption_lengths[0, 0], caption_lengths[0, 1])[None]
    n2, i2, p2, x3, n3, i3 = middle(length, resid, parts, slots)

    theirs = swap(n3, "c")
    around = [px(n3, 1), px(n3, -1)]
    saved, keeps, others = None, [], []
    for i in range(4):
        if i == 0:
            mine = n3
        else:
            if i == 1:
                around = [hold(piece, keeps[:1]) for piece in around]
                across = far_of(*around)
            if i < 3:
                mine = around[i - 1]
            else:
                mine = jnp.concatenate([hold(piece, keeps[1:2]) for piece in across], 0)
            theirs = swap(mine, "c")
        *saved, keep, send = feed(
            i,
            mine,
            theirs,
            tokens[2 * i],
            tokens[2 * i + 1],
            feed_weight,
            saved and tuple(saved),
            others[:-1][-1:],
        )
        keeps.append(keep)
        others.append(swap(send, "c"))
    parts, low = reduce_tokens(keeps, others)
    act, grad, x3_all = saved
    total = feed_grad(x3_all, grad, act, tokens, low + [kv_weight])
    total = hold(total, parts[2:], True)
    g1, c1, keep_slots, send_slots = middle_back(
        grad_low, parts, slots, n2, i2, p2, n3, i3, [total]
    )
    total = lax.psum_scatter(total, PLANE, scatter_dimension=0, tiled=True)
    own, their_ff = home(total[:64], total[64:])
    own = own.astype(F32)
    up_out = join(own[:, :1024], their_ff[:, :1024])
    down_out = join(own[:, 1024:], their_ff[:, 1024:])

    theirs = swap(c1, "c")
    around = [px(c1, 1), px(c1, -1)]
    slot_back = keep_slots.astype(F32) + swap(send_slots, "c").astype(F32)
    back, keeps, others = None, [], []
    for i in range(4):
        if i == 0:
            mine = c1
        else:
            if i == 1:
                around = [hold(piece, keeps[:1]) for piece in around]
                across = far_of(*around)
                slot_back = after(slot_back.astype(BF), around[1])
                slot_back = [
                    slot_back[0],
                    px(slot_back[1], 1),
                    px(slot_back[2], -1),
                    px(slot_back[3], 2),
                ]
            if i < 3:
                mine = around[i - 1]
            else:
                mine = jnp.concatenate([hold(piece, keeps[1:2]) for piece in across], 0)
            theirs = swap(mine, "c")
        order = others[:-1][-1:] + (slot_back[1:] if i == 3 else [])
        *back, keep, send = attend_back(
            i, mine, theirs, first, qkv, p1, back and tuple(back), order
        )
        keeps.append(keep)
        others.append(swap(send, "c"))
    parts, low = reduce_tokens(keeps, others)
    cross_grad, grad_kv = unfold(place, slot_back, kv, first)
    more = more_grad(*back, o1, cross_grad, tokens, keeps[-1:])
    kv_all = lax.all_to_all(
        jnp.broadcast_to(grad_kv[None], (16, 64, 512)),
        PLANE,
        split_axis=0,
        concat_axis=0,
        tiled=True,
    ).reshape(1024, 512)
    kv_grad = dot(caption, kv_all, 0, 0)
    ck_own, ck_their = home(kv_grad[:128], kv_grad[128:])
    ck_out = join(ck_own[:, :256], ck_their[:, :256])
    cv_out = join(ck_own[:, 256:], ck_their[:, 256:])
    more = hold(more, [total, ck_their, low[-1]], True)
    y_keep, y_send = feed_out(act, feed_weight, [more])
    rest = lax.psum_scatter(more, PLANE, scatter_dimension=0, tiled=True)
    y_parts, _ = reduce_tokens(y_keep, swap(y_send, "c"))
    block_out = x3
    for part in y_parts:
        block_out = block_out + part.astype(F32)
    grad_kv = after(grad_kv, more)
    cap_grad = dot(grad_kv, kv_weight, 1, 1, BF).reshape(4, 16, 4096)
    keep = jnp.where(core == 0, cap_grad[:, :8], cap_grad[:, 8:])
    send = jnp.where(core == 0, cap_grad[:, 8:], cap_grad[:, :8])
    send = swap(send, "c")
    low_cap = (keep.astype(F32) + send.astype(F32)).astype(BF)
    near_image = [pick(low_cap, place[2] + n) for n in range(4)]
    cap_out = near_image[0].astype(F32)
    for n in (1, 2, 3):
        cap_out = cap_out + px(near_image[n], n).astype(F32)
    cap_out = cap_out.reshape(8, 16, 2, 128).transpose(0, 2, 1, 3).reshape(1, 8, 4096)
    rest = hold(rest, y_parts[2:], True)
    own, their = home(rest[:64], rest[64:])
    own = own.astype(F32)
    outs = [join(own[:, at : at + 256], their[:, at : at + 256]) for at in range(0, 1536, 256)]
    so_out, cq_out, co_out = outs[3:]

    image_grad = unmix_features(last(g1, parts, resid))[None]

    first_gain = (
        jnp.sum(outs[0] * self_query.astype(F32), 1)
        + jnp.sum(outs[1] * self_key.astype(F32), 1)
        + jnp.sum(outs[2] * self_value.astype(F32), 1)
    )
    terms = jnp.stack(
        [
            first_gain,
            jnp.sum(cq_out * cross_query.astype(F32), 1),
            jnp.sum(up_out * up_weight.astype(F32), 1),
        ],
        0,
    )
    terms = terms + swap(terms, "xl")
    terms = terms + swap(terms, "c")

    return (
        unmix_features(block_out.astype(BF))[None],
        image_grad,
        cap_out,
        terms[0],
        terms[1],
        terms[2],
        outs[0] * gain_one,
        outs[1] * gain_one,
        outs[2] * gain_one,
        so_out.T,
        cq_out * gain_two,
        ck_out,
        cv_out,
        co_out.T,
        up_out * gain_three,
        down_out.T,
    )


def solution(mesh):
    names = ("xh", "y", "z", "xl", "c")
    fine = Mesh(mesh.devices.reshape(2, 4, 4, 2, 2), names)
    rows, text = ("xh", "y", "z"), ("xl", "c")
    tokens = P(rows, text, None)
    by_row = P(rows, text)
    by_text = P(text, rows)
    weights = (by_row, by_row, by_row, by_text, by_row, by_row, by_row, by_text, by_row, by_text)
    in_specs = (tokens, tokens, P(rows, None), tokens) + (P(rows),) * 3 + weights
    out_specs = (tokens,) * 3 + (P(rows),) * 3 + weights
    return jax.shard_map(
        per_device, mesh=fine, in_specs=in_specs, out_specs=out_specs, check_vma=False
    )
```

```python
import functools

import jax
import jax.numpy as jnp
from jax import lax
from jax.experimental import pallas as pl
from jax.experimental.pallas import tpu as pltpu
from jax.sharding import Mesh, PartitionSpec as P

HEAD = 128
CAP = 16
EPSILON = 1e-05
SCALE = HEAD ** (-0.5)
BF = jnp.bfloat16
F32 = jnp.float32
RING = ("xh", "xl")
PLANE = ("y", "z")
WHOLE = pl.BlockSpec(memory_space=pltpu.VMEM)
HBM = pl.BlockSpec(memory_space=pltpu.MemorySpace.HBM)
ANY = pl.BlockSpec(memory_space=pl.ANY)
SCALAR = pl.BlockSpec(memory_space=pltpu.SMEM)


def shape(dims, dtype=BF):
    return jax.ShapeDtypeStruct(dims, dtype)


def out_of(value):
    return pltpu.with_memory_space_constraint(value, pltpu.MemorySpace.HBM)


def far(dims, dtype=BF):
    return pltpu.MemorySpace.HBM(dims, dtype)


def kernel(body, outs, args, order=(), vmem=12, in_specs=None, out_specs=None, **more):
    order = [out_of(dep) if dep.size >= 2**20 else dep for dep in order]
    n, outer = len(order), body
    if in_specs is None:
        in_specs = [WHOLE] * len(args)
    if out_specs is None:
        out_specs = jax.tree.map(lambda _: WHOLE, outs)
    spec = more.pop("grid_spec", None)
    if n:
        m = len(args)

        def outer(*refs):
            body(*refs[:m], *refs[m + n :])

    specs = dict(in_specs=list(in_specs) + [HBM] * n, out_specs=out_specs)
    if spec is not None:
        scalars, grid, scratch = spec
        specs = dict(
            grid_spec=pltpu.PrefetchScalarGridSpec(
                num_scalar_prefetch=scalars, grid=grid, scratch_shapes=scratch, **specs
            )
        )
    return pl.pallas_call(
        outer,
        out_shape=outs,
        compiler_params=pltpu.CompilerParams(vmem_limit_bytes=vmem * 2**20),
        cost_estimate=pl.CostEstimate(flops=1000, bytes_accessed=1000, transcendentals=0),
        **specs,
        **more,
    )(*args, *order)


def hold_body(value, out):
    pass


def hold(value, order, away=False):
    return kernel(
        hold_body,
        far(value.shape, value.dtype) if away else shape(value.shape, value.dtype),
        (out_of(value) if away else value,),
        order,
        vmem=4,
        in_specs=[ANY],
        out_specs=ANY,
        input_output_aliases={0: 0},
        name="hold",
    )


def dot(a, b, ca, cb, out=F32):
    return lax.dot_general(a, b, (((ca,), (cb,)), ((), ())), preferred_element_type=F32).astype(out)


def px(value, step):
    return lax.ppermute(value, RING, [(i, (i + step) % 4) for i in range(4)])


def pp(value, axis, step):
    return lax.ppermute(value, axis, [(i, (i + step) % 4) for i in range(4)])


def swap(value, axis):
    return lax.ppermute(value, axis, [(0, 1), (1, 0)])


def after(value, dep):
    first = dep[(slice(0, 1),) * dep.ndim].reshape((1,) * value.ndim).astype(F32)
    return (value.astype(F32) + first * 0.0).astype(value.dtype)


def far_of(left, right):
    half = left.shape[0] // 2
    return [px(left[:half], 1), px(right[half:], -1)]


def pick(value, at):
    return lax.dynamic_index_in_dim(value, at & 3, 0, False, allow_negative_indices=False)


def reduce_tokens(keep, other):
    low = [(keep[i].astype(F32) + other[i].astype(F32)).astype(BF) for i in range(1, 4)]
    return [keep[0], other[0], px(low[0], -1), px(low[1], 1), px(low[2], 2)], low


def stats(resid):
    mean = jnp.mean(resid, -1, keepdims=True)
    centered = resid - mean
    inverse = lax.rsqrt(jnp.mean(centered * centered, -1, keepdims=True) + EPSILON)
    return centered * inverse, inverse


def norm_back(scaled, normed, inverse):
    return inverse * (
        scaled
        - jnp.mean(scaled, -1, keepdims=True)
        - normed * jnp.mean(scaled * normed, -1, keepdims=True)
    )


def total_of(refs):
    total = refs[0][...].astype(F32)
    for ref in refs[1:]:
        total = total + ref[...].astype(F32)
    return total


def rows_of(refs, part=slice(None)):
    return jnp.concatenate([ref[part, :] for ref in refs], 0)


def attend_body(first, count, *refs):
    pieces, w_ref = refs[: 2 * count], refs[2 * count]
    qkv_ref, p_ref, o_ref, keep_ref, send_ref = refs[-5:]
    for i in range(count):
        rows = slice(256 * (first + i), 256 * (first + i + 1))
        x = rows_of(pieces[2 * i : 2 * i + 2], slice(0, 128))
        qkv_ref[rows, :] = dot(x, w_ref[:, :768], 1, 0, BF)
        for h in range(2):
            at = h * HEAD
            q = qkv_ref[rows, at : at + HEAD]
            k = qkv_ref[rows, 256 + at : 256 + at + HEAD]
            v = qkv_ref[rows, 512 + at : 512 + at + HEAD]
            s = dot(q, k, 1, 1) * SCALE
            e = jnp.exp(s - jnp.max(s, -1, keepdims=True))
            p = (e / jnp.sum(e, -1, keepdims=True)).astype(BF)
            p_ref[first + i, h] = p
            o_ref[rows, at : at + HEAD] = dot(p, v, 1, 0, BF)
        part = dot(o_ref[rows, :], w_ref[:, 768:1024], 1, 1, BF)
        keep_ref[i] = part[:128]
        send_ref[i] = part[128:]


def attend(first, count, pieces, weights, saved=(), order=()):
    return kernel(
        functools.partial(attend_body, first, count),
        (
            shape((1024, 768)),
            shape((4, 2, 256, 256)),
            shape((1024, 256)),
            shape((count, 128, 2048)),
            shape((count, 128, 2048)),
        ),
        (*pieces, weights, *saved),
        order,
        input_output_aliases={2 * count + 1 + n: n for n in range(3)} if saved else {},
        name="attend",
    )


def attend_back_body(i, ca, cb, qkv_ref, p_ref, w_ref, *refs):
    g_ref, all_ref, keep_ref, send_ref = refs[-4:]
    rows = slice(256 * i, 256 * (i + 1))
    c = rows_of((ca, cb))
    all_ref[rows, :] = c
    go = dot(c, w_ref[:, 768:1024], 1, 0, BF)
    for h in range(2):
        at = h * HEAD
        q = qkv_ref[rows, at : at + HEAD]
        k = qkv_ref[rows, 256 + at : 256 + at + HEAD]
        v = qkv_ref[rows, 512 + at : 512 + at + HEAD]
        low = p_ref[i, h]
        g = go[:, at : at + HEAD]
        g_ref[rows, 512 + at : 512 + at + HEAD] = dot(low, g, 0, 0, BF)
        gp = dot(g, v, 1, 1)
        p = low.astype(F32)
        gs = (p * (gp - jnp.sum(p * gp, -1, keepdims=True))).astype(BF)
        g_ref[rows, at : at + HEAD] = (dot(gs, k, 1, 0) * SCALE).astype(BF)
        g_ref[rows, 256 + at : 256 + at + HEAD] = (dot(gs, q, 0, 0) * SCALE).astype(BF)
    part = dot(g_ref[rows, :], w_ref[:, :768], 1, 1, BF)
    keep_ref[...] = part[:128]
    send_ref[...] = part[128:]


def attend_back(i, ca, cb, weights, qkv, p, saved, order=()):
    more = () if saved is None else saved
    return kernel(
        functools.partial(attend_back_body, i),
        (shape((1024, 768)), shape((1024, 2048)), shape((128, 2048)), shape((128, 2048))),
        (ca, cb, qkv, p, weights, *more),
        order,
        input_output_aliases={5: 0, 6: 1} if more else {},
        name="attend_back",
    )


def feed_body(i, xa, xb, ga, gb, w_ref, *refs):
    act_ref, g_ref, all_ref, keep_ref, send_ref = refs[-5:]
    rows = slice(256 * i, 256 * (i + 1))
    x = rows_of((xa, xb))
    all_ref[rows, :] = x
    final = rows_of((ga, gb), slice(128, 256))
    for at in range(0, 1024, 256):
        u = dot(x, w_ref[:, at : at + 256], 1, 0)
        ga_hidden = dot(final, w_ref[:, 1024 + at : 1280 + at], 1, 0)
        phi = 0.5 + 0.5 * lax.erf(u * 0.5**0.5)
        act_ref[rows, at : at + 256] = (u * phi).astype(BF)
        slope = phi + u * jnp.exp(-0.5 * u * u) * (0.5 / jnp.pi) ** 0.5
        g_ref[rows, at : at + 256] = (ga_hidden * slope).astype(BF)
    part = dot(g_ref[rows, :], w_ref[:, :1024], 1, 1, BF)
    keep_ref[...] = part[:128]
    send_ref[...] = part[128:]


def feed(i, xa, xb, ga, gb, weights, saved, order=()):
    more = () if saved is None else saved
    return kernel(
        functools.partial(feed_body, i),
        (
            shape((1024, 1024)),
            shape((1024, 1024)),
            shape((1024, 2048)),
            shape((128, 2048)),
            shape((128, 2048)),
        ),
        (xa, xb, ga, gb, weights, *more),
        order,
        input_output_aliases={5: 0, 6: 1, 7: 2} if more else {},
        name="feed",
    )


def feed_out_body(act_ref, down_ref, keep_ref, send_ref):
    part = dot(act_ref[...], down_ref[...], 1, 1, BF)
    for i in range(4):
        keep_ref[i] = part[256 * i : 256 * i + 128]
        send_ref[i] = part[256 * i + 128 : 256 * (i + 1)]


def feed_out(act, weights, order=()):
    out = pl.BlockSpec((4, 128, 256), lambda j: (0, 0, j))
    return kernel(
        feed_out_body,
        (far((4, 128, 2048)), far((4, 128, 2048))),
        (out_of(act), out_of(weights)),
        order,
        grid=(8,),
        in_specs=[
            pl.BlockSpec((1024, 1024), lambda j: (0, 0)),
            pl.BlockSpec((256, 1024), lambda j: (j, 1)),
        ],
        out_specs=(out, out),
        name="feed_out",
    )


def feed_grad_body(x, g, act, *refs):
    gm, out = refs[:8], refs[8]
    columns = pl.ds(pl.multiple_of(pl.program_id(0) * 256, 256), 256)
    out[:, :1024] = dot(x[:, columns], g[...], 0, 0, BF)
    out[:, 1024:] = dot(rows_of(gm), act[...], 0, 0, BF)


def feed_grad(x, g, act, pieces, order=()):
    return kernel(
        feed_grad_body,
        far((2048, 2048)),
        (x, g, act, *map(out_of, pieces)),
        order,
        grid=(8,),
        in_specs=[WHOLE] * 3 + [pl.BlockSpec((128, 256), lambda j: (1, j))] * 8,
        out_specs=pl.BlockSpec((256, 2048), lambda j: (j, 0)),
        name="feed_grad",
    )


def more_grad_body(g, c, o, cross, *refs):
    x, out = refs[:8], refs[8]
    start = pl.multiple_of(pl.program_id(0) * 256, 256)
    columns = pl.ds(start, 256)
    out[:, :768] = dot(rows_of(x), g[...], 0, 0, BF)
    out[:, 768:1024] = dot(c[:, columns], o[...], 0, 0, BF)
    out[:, 1024:] = cross[columns, :]


def more_grad(g, c, o, cross, pieces, order=()):
    return kernel(
        more_grad_body,
        far((2048, 1536)),
        (g, c, o, cross, *map(out_of, pieces)),
        order,
        grid=(8,),
        in_specs=[WHOLE] * 4 + [pl.BlockSpec((128, 256), lambda j: (0, j))] * 8,
        out_specs=pl.BlockSpec((256, 1536), lambda j: (j, 0)),
        name="more_grad",
    )


def fold_body(at_ref, kv_ref, w_ref, kv_out, both_ref):
    kv = jnp.sum(kv_ref[...].astype(F32), 0).astype(BF)
    kv_out[...] = kv
    for n in range(4):
        at = n * HEAD
        part = dot(kv[:, at : at + HEAD], w_ref[:, at : at + HEAD], 1, 1, BF)
        for i in range(4):
            away = (i + 4 - at_ref[2]) & 3
            away = jnp.where(away == 0, 0, jnp.where(away == 3, 1, away + 1))
            both_ref[away, n * CAP : (n + 1) * CAP, :] = part[i * CAP : (i + 1) * CAP]


def fold(place, kv, weights, order=()):
    outs = (shape((64, 512)), shape((4, 64, 2048)))
    return kernel(
        fold_body,
        outs,
        (place, kv, out_of(weights)),
        order,
        in_specs=[
            SCALAR,
            pl.BlockSpec((16, 64, 512), lambda j: (0, 0, 0)),
            pl.BlockSpec((2048, 512), lambda j: (0, 2)),
        ],
        out_specs=(
            pl.BlockSpec((64, 512), lambda j: (0, 0)),
            pl.BlockSpec((4, 64, 2048), lambda j: (0, 0, 0)),
        ),
        grid=(1,),
        name="fold",
    )


def unfold_body(at_ref, b0, b1, b2, b3, kv_ref, w_ref, grad_ref, gkv_ref, rows_ref):
    for n in range(4):
        at = n * HEAD
        for away, ref in zip((0, 3, 1, 2), (b0, b1, b2, b3)):
            image = (at_ref[2] + away) & 3
            rows_ref[image] = ref[n * CAP : (n + 1) * CAP, :]
        rows = rows_ref[...].reshape(64, 2048)
        grad_ref[:, at : at + HEAD] = dot(rows, kv_ref[:, at : at + HEAD], 0, 0, BF)
        gkv_ref[:, at : at + HEAD] = dot(rows, w_ref[:, at : at + HEAD], 1, 0, BF)


def unfold(place, back, kv, weights, order=()):
    slot = pl.BlockSpec((64, 2048), lambda j: (0, 0))
    return kernel(
        unfold_body,
        (shape((2048, 512)), shape((64, 512))),
        (place, *back, kv, out_of(weights)),
        order,
        in_specs=[SCALAR]
        + [slot] * 4
        + [
            pl.BlockSpec((64, 512), lambda j: (0, 0)),
            pl.BlockSpec((2048, 512), lambda j: (0, 2)),
        ],
        out_specs=(
            pl.BlockSpec((2048, 512), lambda j: (0, 0)),
            pl.BlockSpec((64, 512), lambda j: (0, 0)),
        ),
        grid=(1,),
        scratch_shapes=[pltpu.VMEM((4, CAP, 2048), BF)],
        name="unfold",
    )


def slots_of(refs, part):
    return jnp.concatenate([ref[i, part, :] for ref in refs for i in range(4)], 0)


def middle_body(length_ref, *refs):
    x, parts, slots = refs[0], refs[1:6], refs[6:8]
    n2_ref, i2_ref, p2_ref, x3_ref, n3_ref, i3_ref = refs[8:]
    x2 = x[...].astype(F32) + total_of(parts)
    normed, inverse = stats(x2)
    low = normed.astype(BF)
    n2_ref[...] = low
    i2_ref[...] = inverse
    m, n = slots_of(slots, slice(0, 32)), slots_of(slots, slice(32, 64))
    s = (dot(m, low, 1, 1) * SCALE).reshape(16, CAP, 128)
    live = lax.broadcasted_iota(jnp.int32, (1, CAP, 1), 1) < length_ref[0]
    s = jnp.where(live, s, -1e30)
    e = jnp.exp(s - jnp.max(s, 1, keepdims=True))
    p = (e / jnp.sum(e, 1, keepdims=True)).reshape(256, 128)
    p2_ref[...] = p
    x3 = x2 + dot(p.astype(BF), n, 0, 0)
    x3_ref[...] = x3
    normed, inverse = stats(x3)
    n3_ref[...] = normed.astype(BF)
    i3_ref[...] = inverse


def middle(length, x, parts, slots, order=()):
    column = shape((128, 1), F32)
    return kernel(
        middle_body,
        (
            shape((128, 2048)),
            column,
            shape((256, 128), F32),
            shape((128, 2048), F32),
            shape((128, 2048)),
            column,
        ),
        (length, x, *parts, *slots),
        order,
        vmem=16,
        in_specs=[SCALAR] + [WHOLE] * 8,
        name="middle",
    )


def middle_back_body(*refs):
    g3, parts, slots = refs[0], refs[1:6], refs[6:8]
    n2, i2, p2, n3, i3 = refs[8:13]
    g1_ref, low_ref, keep_ref, send_ref = refs[13:]
    g2 = g3[...].astype(F32) + norm_back(total_of(parts), n3[...].astype(F32), i3[...])
    c = g2.astype(BF)
    m, n = slots_of(slots, slice(0, 32)), slots_of(slots, slice(32, 64))
    p = p2[...].reshape(16, CAP, 128)
    gp = dot(n, c, 1, 1).reshape(16, CAP, 128)
    gs = (p * (gp - jnp.sum(p * gp, 1, keepdims=True))).reshape(256, 128) * SCALE
    gs = gs.astype(BF)
    g1 = g2 + norm_back(dot(gs, m, 0, 0), n2[...].astype(F32), i2[...])
    g1_ref[...] = g1
    low_ref[...] = g1.astype(BF)
    gm = dot(gs, n2[...], 1, 0, BF)
    gn = dot(p2[...].astype(BF), c, 1, 0, BF)
    for out, at in ((keep_ref, 0), (send_ref, 128)):
        for i in range(4):
            rows = slice(at + 32 * i, at + 32 * (i + 1))
            out[i, :32, :] = gm[rows]
            out[i, 32:, :] = gn[rows]


def middle_back(g3, parts, slots, n2, i2, p2, n3, i3, order=()):
    slot = shape((4, 64, 2048))
    outs = (shape((128, 2048), F32), shape((128, 2048)), slot, slot)
    args = (g3, *parts, *slots, n2, i2, p2, n3, i3)
    return kernel(middle_back_body, outs, args, order, vmem=16, name="middle_back")


def last_body(*refs):
    g1, parts, x, out = refs[0], refs[1:6], refs[6], refs[7]
    normed, inverse = stats(x[...].astype(F32))
    out[...] = g1[...] + norm_back(total_of(parts), normed, inverse)


def last(g1, parts, x, order=()):
    return kernel(last_body, shape((128, 2048), F32), (g1, *parts, x), order, name="last")


def mix_features(value):
    n = value.shape[0]
    return value.reshape(n, 2, 16, 64).transpose(0, 2, 1, 3).reshape(n, 2048)


def unmix_features(value):
    n = value.shape[0]
    return value.reshape(n, 16, 2, 64).transpose(0, 2, 1, 3).reshape(n, 2048)


def per_device(
    image_tokens,
    caption_embed,
    caption_lengths,
    output_grad,
    norm_self,
    norm_cross,
    norm_feed,
    self_query,
    self_key,
    self_value,
    self_output,
    cross_query,
    cross_key,
    cross_value,
    cross_output,
    up_weight,
    down_weight,
):
    xh = lax.axis_index("xh")
    xl = lax.axis_index("xl")
    core = lax.axis_index("c")
    place = [lax.axis_index("y"), lax.axis_index("z"), 2 * xh + xl, core]
    place = jnp.stack(place).astype(jnp.int32)
    gain_one = norm_self.astype(F32)[:, None]
    gain_two = norm_cross.astype(F32)[:, None]
    gain_three = norm_feed.astype(F32)[:, None]

    def gained(weight, gain):
        return (weight.astype(F32) * gain).astype(BF)

    def halves(weight):
        n = weight.shape[1] // 2
        first, second = weight[:, :n], weight[:, n:]
        return jnp.where(xh == 0, first, second), jnp.where(xh == 0, second, first)

    def in_order(mine, theirs):
        return jnp.where(xh == 0, mine, theirs), jnp.where(xh == 0, theirs, mine)

    def exchange(weights):
        pairs = [halves(w) for w in weights]
        mine = jnp.concatenate([p[0] for p in pairs], 1)
        return mine, swap(jnp.concatenate([p[1] for p in pairs], 1), "xh")

    def both_of(mine, theirs):
        return jnp.stack(in_order(mine, theirs), 0)

    def home(first, second):
        keep = jnp.where(xh == 0, first, second)
        theirs = swap(jnp.where(xh == 0, second, first).astype(BF), "xh")
        return keep, theirs.astype(F32)

    def join(keep, theirs):
        return jnp.concatenate(in_order(keep, theirs), 1)

    pair = both_of(*exchange(
        (
            gained(self_query, gain_one),
            gained(self_key, gain_one),
            gained(self_value, gain_one),
            self_output.T,
            gained(cross_query, gain_two),
            cross_output.T,
        )
    ))
    first = lax.all_gather(pair.reshape(128, 1536), PLANE, axis=0, tiled=True)
    mine_late, theirs_late = exchange(
        (
            gained(up_weight, gain_three),
            down_weight.T,
            cross_key[:64],
            cross_value[:64],
            cross_key[64:],
            cross_value[64:],
        )
    )
    resid = mix_features(image_tokens[0])
    normed_one, _ = stats(resid.astype(F32))
    grad_low = mix_features(output_grad[0])
    caption = after(caption_embed[0], pair)
    caption = lax.all_gather(caption, ("xh", "xl", "c"), axis=0, tiled=True)
    caption = caption.reshape(64, 2, 16, 128).transpose(2, 0, 1, 3).reshape(16, 64, 256)
    tokens = after(jnp.concatenate([normed_one.astype(BF), grad_low], 0), caption)
    pieces = [tokens, px(tokens, 1), px(tokens, -1)]
    caption = lax.all_to_all(caption, PLANE, split_axis=0, concat_axis=0, tiled=True)
    caption = caption.reshape(1024, 256)
    across = far_of(after(pieces[1], caption), after(pieces[2], caption))
    pieces.append(jnp.concatenate(across, 0))
    tokens = [side for piece in pieces for side in (piece, swap(piece, "c"))]
    pair_kv = both_of(mine_late[:, 2048:], theirs_late[:, 2048:])
    pair_kv = jnp.stack([pair_kv[:, :, :512], pair_kv[:, :, 512:]], 1).reshape(256, 512)
    kv = dot(caption, pair_kv, 1, 0, BF)
    pair_late = both_of(mine_late[:, :2048], hold(theirs_late, [*across, kv])[:, :2048])
    feed_weight = pair_late.reshape(128, 2048)
    feed_weight = lax.all_gather(feed_weight, PLANE, axis=0, tiled=True)
    kv = lax.all_to_all(kv.reshape(16, 64, 512), PLANE, split_axis=0, concat_axis=0, tiled=True)
    qkv, p1, o1, keep, send = attend(0, 4, tokens, first)
    kv, both = fold(place, kv.reshape(16, 64, 512), first, [keep])
    kv_weight = lax.all_gather(after(pair_kv, kv), PLANE, axis=0, tiled=True)
    slots_come = [px(both[1], -1), px(both[2], 1), px(both[3], 2)]
    slots = jnp.stack([both[0], *slots_come], 0)
    slots = (slots, swap(slots, "c"))

    parts, _ = reduce_tokens(keep, swap(send, "c"))
    length = jnp.where(xl == 0, caption_lengths[0, 0], caption_lengths[0, 1])[None]
    n2, i2, p2, x3, n3, i3 = middle(length, resid, parts, slots)

    theirs = swap(n3, "c")
    around = [px(n3, 1), px(n3, -1)]
    saved, keeps, others = None, [], []
    for i in range(4):
        if i == 0:
            mine = n3
        else:
            if i == 1:
                around = [hold(piece, keeps[:1]) for piece in around]
                across = far_of(*around)
            if i < 3:
                mine = around[i - 1]
            else:
                mine = jnp.concatenate([hold(piece, keeps[1:2]) for piece in across], 0)
            theirs = swap(mine, "c")
        *saved, keep, send = feed(
            i,
            mine,
            theirs,
            tokens[2 * i],
            tokens[2 * i + 1],
            feed_weight,
            saved and tuple(saved),
            others[:-1][-1:],
        )
        keeps.append(keep)
        others.append(swap(send, "c"))
    parts, low = reduce_tokens(keeps, others)
    act, grad, x3_all = saved
    total = feed_grad(x3_all, grad, act, tokens, low + [kv_weight])
    total = hold(total, parts[2:], True)
    g1, c1, keep_slots, send_slots = middle_back(
        grad_low, parts, slots, n2, i2, p2, n3, i3, [total]
    )
    total = lax.psum_scatter(total, PLANE, scatter_dimension=0, tiled=True)
    own, their_ff = home(total[:64], total[64:])
    own = own.astype(F32)
    up_out = join(own[:, :1024], their_ff[:, :1024])
    down_out = join(own[:, 1024:], their_ff[:, 1024:])

    theirs = swap(c1, "c")
    around = [px(c1, 1), px(c1, -1)]
    slot_back = keep_slots.astype(F32) + swap(send_slots, "c").astype(F32)
    back, keeps, others = None, [], []
    for i in range(4):
        if i == 0:
            mine = c1
        else:
            if i == 1:
                around = [hold(piece, keeps[:1]) for piece in around]
                across = far_of(*around)
                slot_back = after(slot_back.astype(BF), around[1])
                slot_back = [
                    slot_back[0],
                    px(slot_back[1], 1),
                    px(slot_back[2], -1),
                    px(slot_back[3], 2),
                ]
            if i < 3:
                mine = around[i - 1]
            else:
                mine = jnp.concatenate([hold(piece, keeps[1:2]) for piece in across], 0)
            theirs = swap(mine, "c")
        order = others[:-1][-1:] + (slot_back[1:] if i == 3 else [])
        *back, keep, send = attend_back(
            i, mine, theirs, first, qkv, p1, back and tuple(back), order
        )
        keeps.append(keep)
        others.append(swap(send, "c"))
    parts, low = reduce_tokens(keeps, others)
    cross_grad, grad_kv = unfold(place, slot_back, kv, first, keeps[-1:])
    more = more_grad(*back, o1, cross_grad, tokens, keeps[-1:])
    kv_all = lax.all_to_all(
        jnp.broadcast_to(grad_kv[None], (16, 64, 512)),
        PLANE,
        split_axis=0,
        concat_axis=0,
        tiled=True,
    ).reshape(1024, 512)
    kv_grad = dot(caption, kv_all, 0, 0)
    ck_own, ck_their = home(kv_grad[:128], kv_grad[128:])
    ck_out = join(ck_own[:, :256], ck_their[:, :256])
    cv_out = join(ck_own[:, 256:], ck_their[:, 256:])
    more = hold(more, [total, ck_their, low[-1]], True)
    y_keep, y_send = feed_out(act, feed_weight, [more])
    rest = lax.psum_scatter(more, PLANE, scatter_dimension=0, tiled=True)
    y_parts, _ = reduce_tokens(y_keep, swap(y_send, "c"))
    block_out = x3
    for part in y_parts:
        block_out = block_out + part.astype(F32)
    grad_kv = after(grad_kv, more)
    cap_grad = dot(grad_kv, kv_weight, 1, 1, BF).reshape(4, 16, 4096)
    keep = jnp.where(core == 0, cap_grad[:, :8], cap_grad[:, 8:])
    send = jnp.where(core == 0, cap_grad[:, 8:], cap_grad[:, :8])
    send = swap(send, "c")
    low_cap = (keep.astype(F32) + send.astype(F32)).astype(BF)
    near_image = [pick(low_cap, place[2] + n) for n in range(4)]
    cap_out = near_image[0].astype(F32)
    for n in (1, 2, 3):
        cap_out = cap_out + px(near_image[n], n).astype(F32)
    cap_out = cap_out.reshape(8, 16, 2, 128).transpose(0, 2, 1, 3).reshape(1, 8, 4096)
    rest = hold(rest, y_parts[2:], True)
    own, their = home(rest[:64], rest[64:])
    own = own.astype(F32)
    outs = [join(own[:, at : at + 256], their[:, at : at + 256]) for at in range(0, 1536, 256)]
    so_out, cq_out, co_out = outs[3:]

    image_grad = unmix_features(last(g1, parts, resid))[None]

    first_gain = (
        jnp.sum(outs[0] * self_query.astype(F32), 1)
        + jnp.sum(outs[1] * self_key.astype(F32), 1)
        + jnp.sum(outs[2] * self_value.astype(F32), 1)
    )
    terms = jnp.stack(
        [
            first_gain,
            jnp.sum(cq_out * cross_query.astype(F32), 1),
            jnp.sum(up_out * up_weight.astype(F32), 1),
        ],
        0,
    )
    terms = terms + swap(terms, "xl")
    terms = terms + swap(terms, "c")

    return (
        unmix_features(block_out.astype(BF))[None],
        image_grad,
        cap_out,
        terms[0],
        terms[1],
        terms[2],
        outs[0] * gain_one,
        outs[1] * gain_one,
        outs[2] * gain_one,
        so_out.T,
        cq_out * gain_two,
        ck_out,
        cv_out,
        co_out.T,
        up_out * gain_three,
        down_out.T,
    )


def solution(mesh):
    names = ("xh", "y", "z", "xl", "c")
    fine = Mesh(mesh.devices.reshape(2, 4, 4, 2, 2), names)
    rows, text = ("xh", "y", "z"), ("xl", "c")
    tokens = P(rows, text, None)
    by_row = P(rows, text)
    by_text = P(text, rows)
    weights = (by_row, by_row, by_row, by_text, by_row, by_row, by_row, by_text, by_row, by_text)
    in_specs = (tokens, tokens, P(rows, None), tokens) + (P(rows),) * 3 + weights
    out_specs = (tokens,) * 3 + (P(rows),) * 3 + weights
    return jax.shard_map(
        per_device, mesh=fine, in_specs=in_specs, out_specs=out_specs, check_vma=False
    )
```

```python
import functools

import jax
import jax.numpy as jnp
from jax import lax
from jax.experimental import pallas as pl
from jax.experimental.pallas import tpu as pltpu
from jax.sharding import Mesh, PartitionSpec as P

HEAD = 128
CAP = 16
EPSILON = 1e-05
SCALE = HEAD ** (-0.5)
BF = jnp.bfloat16
F32 = jnp.float32
RING = ("xh", "xl")
PLANE = ("y", "z")
WHOLE = pl.BlockSpec(memory_space=pltpu.VMEM)
HBM = pl.BlockSpec(memory_space=pltpu.MemorySpace.HBM)
ANY = pl.BlockSpec(memory_space=pl.ANY)
SCALAR = pl.BlockSpec(memory_space=pltpu.SMEM)


def shape(dims, dtype=BF):
    return jax.ShapeDtypeStruct(dims, dtype)


def out_of(value):
    return pltpu.with_memory_space_constraint(value, pltpu.MemorySpace.HBM)


def far(dims, dtype=BF):
    return pltpu.MemorySpace.HBM(dims, dtype)


def kernel(body, outs, args, order=(), vmem=12, in_specs=None, out_specs=None, **more):
    order = [out_of(dep) if dep.size >= 2**20 else dep for dep in order]
    n, outer = len(order), body
    if in_specs is None:
        in_specs = [WHOLE] * len(args)
    if out_specs is None:
        out_specs = jax.tree.map(lambda _: WHOLE, outs)
    spec = more.pop("grid_spec", None)
    if n:
        m = len(args)

        def outer(*refs):
            body(*refs[:m], *refs[m + n :])

    specs = dict(in_specs=list(in_specs) + [HBM] * n, out_specs=out_specs)
    if spec is not None:
        scalars, grid, scratch = spec
        specs = dict(
            grid_spec=pltpu.PrefetchScalarGridSpec(
                num_scalar_prefetch=scalars, grid=grid, scratch_shapes=scratch, **specs
            )
        )
    return pl.pallas_call(
        outer,
        out_shape=outs,
        compiler_params=pltpu.CompilerParams(vmem_limit_bytes=vmem * 2**20),
        cost_estimate=pl.CostEstimate(flops=1000, bytes_accessed=1000, transcendentals=0),
        **specs,
        **more,
    )(*args, *order)


def hold_body(value, out):
    pass


def hold(value, order, away=False):
    return kernel(
        hold_body,
        far(value.shape, value.dtype) if away else shape(value.shape, value.dtype),
        (out_of(value) if away else value,),
        order,
        vmem=4,
        in_specs=[ANY],
        out_specs=ANY,
        input_output_aliases={0: 0},
        name="hold",
    )


def dot(a, b, ca, cb, out=F32):
    return lax.dot_general(a, b, (((ca,), (cb,)), ((), ())), preferred_element_type=F32).astype(out)


def px(value, step):
    return lax.ppermute(value, RING, [(i, (i + step) % 4) for i in range(4)])


def pp(value, axis, step):
    return lax.ppermute(value, axis, [(i, (i + step) % 4) for i in range(4)])


def swap(value, axis):
    return lax.ppermute(value, axis, [(0, 1), (1, 0)])


def after(value, dep):
    first = dep[(slice(0, 1),) * dep.ndim].reshape((1,) * value.ndim).astype(F32)
    return (value.astype(F32) + first * 0.0).astype(value.dtype)


def far_of(left, right):
    half = left.shape[0] // 2
    return [px(left[:half], 1), px(right[half:], -1)]


def pick(value, at):
    return lax.dynamic_index_in_dim(value, at & 3, 0, False, allow_negative_indices=False)


def reduce_tokens(keep, other):
    low = [(keep[i].astype(F32) + other[i].astype(F32)).astype(BF) for i in range(1, 4)]
    return [keep[0], other[0], px(low[0], -1), px(low[1], 1), px(low[2], 2)], low


def stats(resid):
    mean = jnp.mean(resid, -1, keepdims=True)
    centered = resid - mean
    inverse = lax.rsqrt(jnp.mean(centered * centered, -1, keepdims=True) + EPSILON)
    return centered * inverse, inverse


def norm_back(scaled, normed, inverse):
    return inverse * (
        scaled
        - jnp.mean(scaled, -1, keepdims=True)
        - normed * jnp.mean(scaled * normed, -1, keepdims=True)
    )


def total_of(refs):
    total = refs[0][...].astype(F32)
    for ref in refs[1:]:
        total = total + ref[...].astype(F32)
    return total


def rows_of(refs, part=slice(None)):
    return jnp.concatenate([ref[part, :] for ref in refs], 0)


def attend_body(first, count, *refs):
    pieces, w_ref = refs[: 2 * count], refs[2 * count]
    qkv_ref, p_ref, o_ref, keep_ref, send_ref = refs[-5:]
    for i in range(count):
        rows = slice(256 * (first + i), 256 * (first + i + 1))
        x = rows_of(pieces[2 * i : 2 * i + 2], slice(0, 128))
        qkv_ref[rows, :] = dot(x, w_ref[:, :768], 1, 0, BF)
        for h in range(2):
            at = h * HEAD
            q = qkv_ref[rows, at : at + HEAD]
            k = qkv_ref[rows, 256 + at : 256 + at + HEAD]
            v = qkv_ref[rows, 512 + at : 512 + at + HEAD]
            s = dot(q, k, 1, 1) * SCALE
            e = jnp.exp(s - jnp.max(s, -1, keepdims=True))
            p = (e / jnp.sum(e, -1, keepdims=True)).astype(BF)
            p_ref[first + i, h] = p
            o_ref[rows, at : at + HEAD] = dot(p, v, 1, 0, BF)
        part = dot(o_ref[rows, :], w_ref[:, 768:1024], 1, 1, BF)
        keep_ref[i] = part[:128]
        send_ref[i] = part[128:]


def attend(first, count, pieces, weights, saved=(), order=()):
    return kernel(
        functools.partial(attend_body, first, count),
        (
            shape((1024, 768)),
            shape((4, 2, 256, 256)),
            shape((1024, 256)),
            shape((count, 128, 2048)),
            shape((count, 128, 2048)),
        ),
        (*pieces, weights, *saved),
        order,
        input_output_aliases={2 * count + 1 + n: n for n in range(3)} if saved else {},
        name="attend",
    )


def attend_back_body(i, ca, cb, qkv_ref, p_ref, w_ref, *refs):
    g_ref, all_ref, keep_ref, send_ref = refs[-4:]
    rows = slice(256 * i, 256 * (i + 1))
    c = rows_of((ca, cb))
    all_ref[rows, :] = c
    go = dot(c, w_ref[:, 768:1024], 1, 0, BF)
    for h in range(2):
        at = h * HEAD
        q = qkv_ref[rows, at : at + HEAD]
        k = qkv_ref[rows, 256 + at : 256 + at + HEAD]
        v = qkv_ref[rows, 512 + at : 512 + at + HEAD]
        low = p_ref[i, h]
        g = go[:, at : at + HEAD]
        g_ref[rows, 512 + at : 512 + at + HEAD] = dot(low, g, 0, 0, BF)
        gp = dot(g, v, 1, 1)
        p = low.astype(F32)
        gs = (p * (gp - jnp.sum(p * gp, -1, keepdims=True))).astype(BF)
        g_ref[rows, at : at + HEAD] = (dot(gs, k, 1, 0) * SCALE).astype(BF)
        g_ref[rows, 256 + at : 256 + at + HEAD] = (dot(gs, q, 0, 0) * SCALE).astype(BF)
    part = dot(g_ref[rows, :], w_ref[:, :768], 1, 1, BF)
    keep_ref[...] = part[:128]
    send_ref[...] = part[128:]


def attend_back(i, ca, cb, weights, qkv, p, saved, order=()):
    more = () if saved is None else saved
    return kernel(
        functools.partial(attend_back_body, i),
        (shape((1024, 768)), shape((1024, 2048)), shape((128, 2048)), shape((128, 2048))),
        (ca, cb, qkv, p, weights, *more),
        order,
        input_output_aliases={5: 0, 6: 1} if more else {},
        name="attend_back",
    )


def feed_body(i, xa, xb, ga, gb, w_ref, *refs):
    act_ref, g_ref, all_ref, keep_ref, send_ref = refs[-5:]
    rows = slice(256 * i, 256 * (i + 1))
    x = rows_of((xa, xb))
    all_ref[rows, :] = x
    final = rows_of((ga, gb), slice(128, 256))
    for at in range(0, 1024, 256):
        u = dot(x, w_ref[:, at : at + 256], 1, 0)
        ga_hidden = dot(final, w_ref[:, 1024 + at : 1280 + at], 1, 0)
        phi = 0.5 + 0.5 * lax.erf(u * 0.5**0.5)
        act_ref[rows, at : at + 256] = (u * phi).astype(BF)
        slope = phi + u * jnp.exp(-0.5 * u * u) * (0.5 / jnp.pi) ** 0.5
        g_ref[rows, at : at + 256] = (ga_hidden * slope).astype(BF)
    part = dot(g_ref[rows, :], w_ref[:, :1024], 1, 1, BF)
    keep_ref[...] = part[:128]
    send_ref[...] = part[128:]


def feed(i, xa, xb, ga, gb, weights, saved, order=()):
    more = () if saved is None else saved
    return kernel(
        functools.partial(feed_body, i),
        (
            shape((1024, 1024)),
            shape((1024, 1024)),
            shape((1024, 2048)),
            shape((128, 2048)),
            shape((128, 2048)),
        ),
        (xa, xb, ga, gb, weights, *more),
        order,
        input_output_aliases={5: 0, 6: 1, 7: 2} if more else {},
        name="feed",
    )


def feed_out_body(act_ref, down_ref, keep_ref, send_ref):
    part = dot(act_ref[...], down_ref[...], 1, 1, BF)
    for i in range(4):
        keep_ref[i] = part[256 * i : 256 * i + 128]
        send_ref[i] = part[256 * i + 128 : 256 * (i + 1)]


def feed_out(act, weights, order=()):
    out = pl.BlockSpec((4, 128, 256), lambda j: (0, 0, j))
    return kernel(
        feed_out_body,
        (far((4, 128, 2048)), far((4, 128, 2048))),
        (out_of(act), out_of(weights)),
        order,
        grid=(8,),
        in_specs=[
            pl.BlockSpec((1024, 1024), lambda j: (0, 0)),
            pl.BlockSpec((256, 1024), lambda j: (j, 1)),
        ],
        out_specs=(out, out),
        name="feed_out",
    )


def feed_grad_body(x, g, act, *refs):
    gm, out = refs[:8], refs[8]
    columns = pl.ds(pl.multiple_of(pl.program_id(0) * 256, 256), 256)
    out[:, :1024] = dot(x[:, columns], g[...], 0, 0, BF)
    out[:, 1024:] = dot(rows_of(gm), act[...], 0, 0, BF)


def feed_grad(x, g, act, pieces, order=()):
    return kernel(
        feed_grad_body,
        far((2048, 2048)),
        (x, g, act, *map(out_of, pieces)),
        order,
        grid=(8,),
        in_specs=[WHOLE] * 3 + [pl.BlockSpec((128, 256), lambda j: (1, j))] * 8,
        out_specs=pl.BlockSpec((256, 2048), lambda j: (j, 0)),
        name="feed_grad",
    )


def more_grad_body(g, c, o, cross, *refs):
    x, out = refs[:8], refs[8]
    start = pl.multiple_of(pl.program_id(0) * 256, 256)
    columns = pl.ds(start, 256)
    out[:, :768] = dot(rows_of(x), g[...], 0, 0, BF)
    out[:, 768:1024] = dot(c[:, columns], o[...], 0, 0, BF)
    out[:, 1024:] = cross[columns, :]


def more_grad(g, c, o, cross, pieces, order=()):
    return kernel(
        more_grad_body,
        far((2048, 1536)),
        (g, c, o, cross, *map(out_of, pieces)),
        order,
        grid=(8,),
        in_specs=[WHOLE] * 4 + [pl.BlockSpec((128, 256), lambda j: (0, j))] * 8,
        out_specs=pl.BlockSpec((256, 1536), lambda j: (j, 0)),
        name="more_grad",
    )


def fold_body(at_ref, kv_ref, w_ref, kv_out, both_ref):
    kv = jnp.sum(kv_ref[...].astype(F32), 0).astype(BF)
    kv_out[...] = kv
    for n in range(4):
        at = n * HEAD
        part = dot(kv[:, at : at + HEAD], w_ref[:, at : at + HEAD], 1, 1, BF)
        for i in range(4):
            away = (i + 4 - at_ref[2]) & 3
            away = jnp.where(away == 0, 0, jnp.where(away == 3, 1, away + 1))
            both_ref[away, n * CAP : (n + 1) * CAP, :] = part[i * CAP : (i + 1) * CAP]


def fold(place, kv, weights, order=()):
    outs = (shape((64, 512)), shape((4, 64, 2048)))
    return kernel(
        fold_body,
        outs,
        (place, kv, out_of(weights)),
        order,
        in_specs=[
            SCALAR,
            pl.BlockSpec((16, 64, 512), lambda j: (0, 0, 0)),
            pl.BlockSpec((2048, 512), lambda j: (0, 2)),
        ],
        out_specs=(
            pl.BlockSpec((64, 512), lambda j: (0, 0)),
            pl.BlockSpec((4, 64, 2048), lambda j: (0, 0, 0)),
        ),
        grid=(1,),
        name="fold",
    )


def unfold_body(at_ref, b0, b1, b2, b3, kv_ref, w_ref, grad_ref, gkv_ref, rows_ref):
    for n in range(4):
        at = n * HEAD
        for away, ref in zip((0, 3, 1, 2), (b0, b1, b2, b3)):
            image = (at_ref[2] + away) & 3
            rows_ref[image] = ref[n * CAP : (n + 1) * CAP, :]
        rows = rows_ref[...].reshape(64, 2048)
        grad_ref[:, at : at + HEAD] = dot(rows, kv_ref[:, at : at + HEAD], 0, 0, BF)
        gkv_ref[:, at : at + HEAD] = dot(rows, w_ref[:, at : at + HEAD], 1, 0, BF)


def unfold(place, back, kv, weights, order=()):
    slot = pl.BlockSpec((64, 2048), lambda j: (0, 0))
    return kernel(
        unfold_body,
        (shape((2048, 512)), shape((64, 512))),
        (place, *back, kv, out_of(weights)),
        order,
        in_specs=[SCALAR]
        + [slot] * 4
        + [
            pl.BlockSpec((64, 512), lambda j: (0, 0)),
            pl.BlockSpec((2048, 512), lambda j: (0, 2)),
        ],
        out_specs=(
            pl.BlockSpec((2048, 512), lambda j: (0, 0)),
            pl.BlockSpec((64, 512), lambda j: (0, 0)),
        ),
        grid=(1,),
        scratch_shapes=[pltpu.VMEM((4, CAP, 2048), BF)],
        name="unfold",
    )


def slots_of(refs, part):
    return jnp.concatenate([ref[i, part, :] for ref in refs for i in range(4)], 0)


def middle_body(length_ref, *refs):
    x, parts, slots = refs[0], refs[1:6], refs[6:8]
    n2_ref, i2_ref, p2_ref, x3_ref, n3_ref, i3_ref = refs[8:]
    x2 = x[...].astype(F32) + total_of(parts)
    normed, inverse = stats(x2)
    low = normed.astype(BF)
    n2_ref[...] = low
    i2_ref[...] = inverse
    m, n = slots_of(slots, slice(0, 32)), slots_of(slots, slice(32, 64))
    s = (dot(m, low, 1, 1) * SCALE).reshape(16, CAP, 128)
    live = lax.broadcasted_iota(jnp.int32, (1, CAP, 1), 1) < length_ref[0]
    s = jnp.where(live, s, -1e30)
    e = jnp.exp(s - jnp.max(s, 1, keepdims=True))
    p = (e / jnp.sum(e, 1, keepdims=True)).reshape(256, 128)
    p2_ref[...] = p
    x3 = x2 + dot(p.astype(BF), n, 0, 0)
    x3_ref[...] = x3
    normed, inverse = stats(x3)
    n3_ref[...] = normed.astype(BF)
    i3_ref[...] = inverse


def middle(length, x, parts, slots, order=()):
    column = shape((128, 1), F32)
    return kernel(
        middle_body,
        (
            shape((128, 2048)),
            column,
            shape((256, 128), F32),
            shape((128, 2048), F32),
            shape((128, 2048)),
            column,
        ),
        (length, x, *parts, *slots),
        order,
        vmem=16,
        in_specs=[SCALAR] + [WHOLE] * 8,
        name="middle",
    )


def middle_back_body(*refs):
    g3, parts, slots = refs[0], refs[1:6], refs[6:8]
    n2, i2, p2, n3, i3 = refs[8:13]
    g1_ref, low_ref, keep_ref, send_ref = refs[13:]
    g2 = g3[...].astype(F32) + norm_back(total_of(parts), n3[...].astype(F32), i3[...])
    c = g2.astype(BF)
    m, n = slots_of(slots, slice(0, 32)), slots_of(slots, slice(32, 64))
    p = p2[...].reshape(16, CAP, 128)
    gp = dot(n, c, 1, 1).reshape(16, CAP, 128)
    gs = (p * (gp - jnp.sum(p * gp, 1, keepdims=True))).reshape(256, 128) * SCALE
    gs = gs.astype(BF)
    g1 = g2 + norm_back(dot(gs, m, 0, 0), n2[...].astype(F32), i2[...])
    g1_ref[...] = g1
    low_ref[...] = g1.astype(BF)
    gm = dot(gs, n2[...], 1, 0, BF)
    gn = dot(p2[...].astype(BF), c, 1, 0, BF)
    for out, at in ((keep_ref, 0), (send_ref, 128)):
        for i in range(4):
            rows = slice(at + 32 * i, at + 32 * (i + 1))
            out[i, :32, :] = gm[rows]
            out[i, 32:, :] = gn[rows]


def middle_back(g3, parts, slots, n2, i2, p2, n3, i3, order=()):
    slot = shape((4, 64, 2048))
    outs = (shape((128, 2048), F32), shape((128, 2048)), slot, slot)
    args = (g3, *parts, *slots, n2, i2, p2, n3, i3)
    return kernel(middle_back_body, outs, args, order, vmem=16, name="middle_back")


def last_body(*refs):
    g1, parts, x, out = refs[0], refs[1:6], refs[6], refs[7]
    normed, inverse = stats(x[...].astype(F32))
    out[...] = g1[...] + norm_back(total_of(parts), normed, inverse)


def last(g1, parts, x, order=()):
    return kernel(last_body, shape((128, 2048), F32), (g1, *parts, x), order, name="last")


def mix_features(value):
    n = value.shape[0]
    return value.reshape(n, 2, 16, 64).transpose(0, 2, 1, 3).reshape(n, 2048)


def unmix_features(value):
    n = value.shape[0]
    return value.reshape(n, 16, 2, 64).transpose(0, 2, 1, 3).reshape(n, 2048)


def per_device(
    image_tokens,
    caption_embed,
    caption_lengths,
    output_grad,
    norm_self,
    norm_cross,
    norm_feed,
    self_query,
    self_key,
    self_value,
    self_output,
    cross_query,
    cross_key,
    cross_value,
    cross_output,
    up_weight,
    down_weight,
):
    xh = lax.axis_index("xh")
    xl = lax.axis_index("xl")
    core = lax.axis_index("c")
    place = [lax.axis_index("y"), lax.axis_index("z"), 2 * xh + xl, core]
    place = jnp.stack(place).astype(jnp.int32)
    gain_one = norm_self.astype(F32)[:, None]
    gain_two = norm_cross.astype(F32)[:, None]
    gain_three = norm_feed.astype(F32)[:, None]

    def gained(weight, gain):
        return (weight.astype(F32) * gain).astype(BF)

    def halves(weight):
        n = weight.shape[1] // 2
        first, second = weight[:, :n], weight[:, n:]
        return jnp.where(xh == 0, first, second), jnp.where(xh == 0, second, first)

    def in_order(mine, theirs):
        return jnp.where(xh == 0, mine, theirs), jnp.where(xh == 0, theirs, mine)

    def exchange(weights):
        pairs = [halves(w) for w in weights]
        mine = jnp.concatenate([p[0] for p in pairs], 1)
        return mine, swap(jnp.concatenate([p[1] for p in pairs], 1), "xh")

    def both_of(mine, theirs):
        return jnp.stack(in_order(mine, theirs), 0)

    def home(first, second):
        keep = jnp.where(xh == 0, first, second)
        theirs = swap(jnp.where(xh == 0, second, first).astype(BF), "xh")
        return keep, theirs.astype(F32)

    def join(keep, theirs):
        return jnp.concatenate(in_order(keep, theirs), 1)

    pair = both_of(*exchange(
        (
            gained(self_query, gain_one),
            gained(self_key, gain_one),
            gained(self_value, gain_one),
            self_output.T,
            gained(cross_query, gain_two),
            cross_output.T,
        )
    ))
    first = lax.all_gather(pair.reshape(128, 1536), PLANE, axis=0, tiled=True)
    mine_late, theirs_late = exchange(
        (
            gained(up_weight, gain_three),
            down_weight.T,
            cross_key[:64],
            cross_value[:64],
            cross_key[64:],
            cross_value[64:],
        )
    )
    resid = mix_features(image_tokens[0])
    normed_one, _ = stats(resid.astype(F32))
    grad_low = mix_features(output_grad[0])
    tokens = after(jnp.concatenate([normed_one.astype(BF), grad_low], 0), pair)
    pieces = [tokens, px(tokens, 1), px(tokens, -1)]
    caption = after(caption_embed[0], pair)
    caption = lax.all_gather(caption, ("xh", "xl", "c"), axis=0, tiled=True)
    caption = caption.reshape(64, 2, 16, 128).transpose(2, 0, 1, 3).reshape(16, 64, 256)
    caption = after(after(caption, pieces[1]), pieces[2])
    caption = lax.all_to_all(caption, PLANE, split_axis=0, concat_axis=0, tiled=True)
    caption = caption.reshape(1024, 256)
    across = far_of(pieces[1], pieces[2])
    pieces.append(jnp.concatenate(across, 0))
    tokens = [side for piece in pieces for side in (piece, swap(piece, "c"))]
    pair_kv = both_of(mine_late[:, 2048:], theirs_late[:, 2048:])
    pair_kv = jnp.stack([pair_kv[:, :, :512], pair_kv[:, :, 512:]], 1).reshape(256, 512)
    kv = dot(caption, pair_kv, 1, 0, BF)
    pair_late = both_of(mine_late[:, :2048], hold(theirs_late, [*across, kv])[:, :2048])
    feed_weight = pair_late.reshape(128, 2048)
    feed_weight = lax.all_gather(feed_weight, PLANE, axis=0, tiled=True)
    kv = lax.all_to_all(kv.reshape(16, 64, 512), PLANE, split_axis=0, concat_axis=0, tiled=True)
    qkv, p1, o1, keep, send = attend(0, 4, tokens, first)
    kv, both = fold(place, kv.reshape(16, 64, 512), first, [keep])
    kv_weight = lax.all_gather(after(pair_kv, kv), PLANE, axis=0, tiled=True)
    slots_come = [px(both[1], -1), px(both[2], 1), px(both[3], 2)]
    slots = jnp.stack([both[0], *slots_come], 0)
    slots = (slots, swap(slots, "c"))

    parts, _ = reduce_tokens(keep, swap(send, "c"))
    length = jnp.where(xl == 0, caption_lengths[0, 0], caption_lengths[0, 1])[None]
    n2, i2, p2, x3, n3, i3 = middle(length, resid, parts, slots, [feed_weight])

    theirs = swap(n3, "c")
    around = [px(n3, 1), px(n3, -1)]
    saved, keeps, others = None, [], []
    for i in range(4):
        if i == 0:
            mine = n3
        else:
            if i == 1:
                around = [hold(piece, keeps[:1]) for piece in around]
                across = far_of(*around)
            if i < 3:
                mine = around[i - 1]
            else:
                mine = jnp.concatenate([hold(piece, keeps[1:2]) for piece in across], 0)
            theirs = swap(mine, "c")
        *saved, keep, send = feed(
            i,
            mine,
            theirs,
            tokens[2 * i],
            tokens[2 * i + 1],
            feed_weight,
            saved and tuple(saved),
            others[:-1][-1:],
        )
        keeps.append(keep)
        others.append(swap(send, "c"))
    parts, low = reduce_tokens(keeps, others)
    act, grad, x3_all = saved
    total = feed_grad(x3_all, grad, act, tokens, low + [kv_weight])
    total = hold(total, parts[2:], True)
    g1, c1, keep_slots, send_slots = middle_back(
        grad_low, parts, slots, n2, i2, p2, n3, i3, [total]
    )
    total = lax.psum_scatter(total, PLANE, scatter_dimension=0, tiled=True)
    own, their_ff = home(total[:64], total[64:])
    own = own.astype(F32)
    up_out = join(own[:, :1024], their_ff[:, :1024])
    down_out = join(own[:, 1024:], their_ff[:, 1024:])

    theirs = swap(c1, "c")
    around = [px(c1, 1), px(c1, -1)]
    slot_back = keep_slots.astype(F32) + swap(send_slots, "c").astype(F32)
    back, keeps, others = None, [], []
    for i in range(4):
        if i == 0:
            mine = c1
        else:
            if i == 1:
                around = [hold(piece, keeps[:1]) for piece in around]
                across = far_of(*around)
                slot_back = after(slot_back.astype(BF), around[1])
                slot_back = [
                    slot_back[0],
                    px(slot_back[1], 1),
                    px(slot_back[2], -1),
                    px(slot_back[3], 2),
                ]
            if i < 3:
                mine = around[i - 1]
            else:
                mine = jnp.concatenate([hold(piece, keeps[1:2]) for piece in across], 0)
            theirs = swap(mine, "c")
        order = others[:-1][-1:] + (slot_back[1:] if i == 3 else [])
        *back, keep, send = attend_back(
            i, mine, theirs, first, qkv, p1, back and tuple(back), order
        )
        keeps.append(keep)
        others.append(swap(send, "c"))
    parts, low = reduce_tokens(keeps, others)
    cross_grad, grad_kv = unfold(place, slot_back, kv, first, keeps[-1:])
    more = more_grad(*back, o1, cross_grad, tokens, keeps[-1:])
    more = hold(more, [total, low[-1]], True)
    y_keep, y_send = feed_out(act, feed_weight, [more])
    rest = lax.psum_scatter(more, PLANE, scatter_dimension=0, tiled=True)
    y_parts, _ = reduce_tokens(y_keep, swap(y_send, "c"))
    block_out = x3
    for part in y_parts:
        block_out = block_out + part.astype(F32)
    grad_kv = after(grad_kv, more)
    kv_all = lax.all_to_all(
        jnp.broadcast_to(grad_kv[None], (16, 64, 512)),
        PLANE,
        split_axis=0,
        concat_axis=0,
        tiled=True,
    ).reshape(1024, 512)
    kv_grad = dot(caption, kv_all, 0, 0)
    ck_own, ck_their = home(kv_grad[:128], kv_grad[128:])
    ck_out = join(ck_own[:, :256], ck_their[:, :256])
    cv_out = join(ck_own[:, 256:], ck_their[:, 256:])
    cap_grad = dot(grad_kv, kv_weight, 1, 1, BF).reshape(4, 16, 4096)
    keep = jnp.where(core == 0, cap_grad[:, :8], cap_grad[:, 8:])
    send = jnp.where(core == 0, cap_grad[:, 8:], cap_grad[:, :8])
    send = swap(send, "c")
    low_cap = (keep.astype(F32) + send.astype(F32)).astype(BF)
    near_image = [pick(low_cap, place[2] + n) for n in range(4)]
    cap_out = near_image[0].astype(F32)
    for n in (1, 2, 3):
        cap_out = cap_out + px(near_image[n], n).astype(F32)
    cap_out = cap_out.reshape(8, 16, 2, 128).transpose(0, 2, 1, 3).reshape(1, 8, 4096)
    rest = hold(rest, y_parts[2:], True)
    own, their = home(rest[:64], rest[64:])
    own = own.astype(F32)
    outs = [join(own[:, at : at + 256], their[:, at : at + 256]) for at in range(0, 1536, 256)]
    so_out, cq_out, co_out = outs[3:]

    image_grad = unmix_features(last(g1, parts, resid, [y_keep]))[None]

    first_gain = (
        jnp.sum(outs[0] * self_query.astype(F32), 1)
        + jnp.sum(outs[1] * self_key.astype(F32), 1)
        + jnp.sum(outs[2] * self_value.astype(F32), 1)
    )
    terms = jnp.stack(
        [
            first_gain,
            jnp.sum(cq_out * cross_query.astype(F32), 1),
            jnp.sum(up_out * up_weight.astype(F32), 1),
        ],
        0,
    )
    terms = terms + swap(terms, "xl")
    terms = terms + swap(terms, "c")

    return (
        unmix_features(block_out.astype(BF))[None],
        image_grad,
        cap_out,
        terms[0],
        terms[1],
        terms[2],
        outs[0] * gain_one,
        outs[1] * gain_one,
        outs[2] * gain_one,
        so_out.T,
        cq_out * gain_two,
        ck_out,
        cv_out,
        co_out.T,
        up_out * gain_three,
        down_out.T,
    )


def solution(mesh):
    names = ("xh", "y", "z", "xl", "c")
    fine = Mesh(mesh.devices.reshape(2, 4, 4, 2, 2), names)
    rows, text = ("xh", "y", "z"), ("xl", "c")
    tokens = P(rows, text, None)
    by_row = P(rows, text)
    by_text = P(text, rows)
    weights = (by_row, by_row, by_row, by_text, by_row, by_row, by_row, by_text, by_row, by_text)
    in_specs = (tokens, tokens, P(rows, None), tokens) + (P(rows),) * 3 + weights
    out_specs = (tokens,) * 3 + (P(rows),) * 3 + weights
    return jax.shard_map(
        per_device, mesh=fine, in_specs=in_specs, out_specs=out_specs, check_vma=False
    )
```

```python
import functools

import jax
import jax.numpy as jnp
from jax import lax
from jax.experimental import pallas as pl
from jax.experimental.pallas import tpu as pltpu
from jax.sharding import Mesh, PartitionSpec as P

HEAD = 128
CAP = 16
EPSILON = 1e-05
SCALE = HEAD ** (-0.5)
BF = jnp.bfloat16
F32 = jnp.float32
RING = ("xh", "xl")
PLANE = ("y", "z")
WHOLE = pl.BlockSpec(memory_space=pltpu.VMEM)
HBM = pl.BlockSpec(memory_space=pltpu.MemorySpace.HBM)
ANY = pl.BlockSpec(memory_space=pl.ANY)
SCALAR = pl.BlockSpec(memory_space=pltpu.SMEM)


def shape(dims, dtype=BF):
    return jax.ShapeDtypeStruct(dims, dtype)


def out_of(value):
    return pltpu.with_memory_space_constraint(value, pltpu.MemorySpace.HBM)


def far(dims, dtype=BF):
    return pltpu.MemorySpace.HBM(dims, dtype)


def kernel(body, outs, args, order=(), vmem=12, in_specs=None, out_specs=None, **more):
    order = [out_of(dep) if dep.size >= 2**20 else dep for dep in order]
    n, outer = len(order), body
    if in_specs is None:
        in_specs = [WHOLE] * len(args)
    if out_specs is None:
        out_specs = jax.tree.map(lambda _: WHOLE, outs)
    spec = more.pop("grid_spec", None)
    if n:
        m = len(args)

        def outer(*refs):
            body(*refs[:m], *refs[m + n :])

    specs = dict(in_specs=list(in_specs) + [HBM] * n, out_specs=out_specs)
    if spec is not None:
        scalars, grid, scratch = spec
        specs = dict(
            grid_spec=pltpu.PrefetchScalarGridSpec(
                num_scalar_prefetch=scalars, grid=grid, scratch_shapes=scratch, **specs
            )
        )
    return pl.pallas_call(
        outer,
        out_shape=outs,
        compiler_params=pltpu.CompilerParams(vmem_limit_bytes=vmem * 2**20),
        cost_estimate=pl.CostEstimate(flops=1000, bytes_accessed=1000, transcendentals=0),
        **specs,
        **more,
    )(*args, *order)


def hold_body(value, out):
    pass


def hold(value, order, away=False):
    return kernel(
        hold_body,
        far(value.shape, value.dtype) if away else shape(value.shape, value.dtype),
        (out_of(value) if away else value,),
        order,
        vmem=4,
        in_specs=[ANY],
        out_specs=ANY,
        input_output_aliases={0: 0},
        name="hold",
    )


def dot(a, b, ca, cb, out=F32):
    return lax.dot_general(a, b, (((ca,), (cb,)), ((), ())), preferred_element_type=F32).astype(out)


def px(value, step):
    return lax.ppermute(value, RING, [(i, (i + step) % 4) for i in range(4)])


def pp(value, axis, step):
    return lax.ppermute(value, axis, [(i, (i + step) % 4) for i in range(4)])


def swap(value, axis):
    return lax.ppermute(value, axis, [(0, 1), (1, 0)])


def after(value, dep):
    first = dep[(slice(0, 1),) * dep.ndim].reshape((1,) * value.ndim).astype(F32)
    return (value.astype(F32) + first * 0.0).astype(value.dtype)


def far_of(left, right):
    half = left.shape[0] // 2
    return [px(left[:half], 1), px(right[half:], -1)]


def pick(value, at):
    return lax.dynamic_index_in_dim(value, at & 3, 0, False, allow_negative_indices=False)


def reduce_tokens(keep, other):
    low = [(keep[i].astype(F32) + other[i].astype(F32)).astype(BF) for i in range(1, 4)]
    return [keep[0], other[0], px(low[0], -1), px(low[1], 1), px(low[2], 2)], low


def stats(resid):
    mean = jnp.mean(resid, -1, keepdims=True)
    centered = resid - mean
    inverse = lax.rsqrt(jnp.mean(centered * centered, -1, keepdims=True) + EPSILON)
    return centered * inverse, inverse


def norm_back(scaled, normed, inverse):
    return inverse * (
        scaled
        - jnp.mean(scaled, -1, keepdims=True)
        - normed * jnp.mean(scaled * normed, -1, keepdims=True)
    )


def total_of(refs):
    total = refs[0][...].astype(F32)
    for ref in refs[1:]:
        total = total + ref[...].astype(F32)
    return total


def rows_of(refs, part=slice(None)):
    return jnp.concatenate([ref[part, :] for ref in refs], 0)


def attend_body(first, count, *refs):
    pieces, w_ref = refs[: 2 * count], refs[2 * count]
    qkv_ref, p_ref, o_ref, keep_ref, send_ref = refs[-5:]
    for i in range(count):
        rows = slice(256 * (first + i), 256 * (first + i + 1))
        x = rows_of(pieces[2 * i : 2 * i + 2], slice(0, 128))
        qkv_ref[rows, :] = dot(x, w_ref[:, :768], 1, 0, BF)
        for h in range(2):
            at = h * HEAD
            q = qkv_ref[rows, at : at + HEAD]
            k = qkv_ref[rows, 256 + at : 256 + at + HEAD]
            v = qkv_ref[rows, 512 + at : 512 + at + HEAD]
            s = dot(q, k, 1, 1) * SCALE
            e = jnp.exp(s - jnp.max(s, -1, keepdims=True))
            p = (e / jnp.sum(e, -1, keepdims=True)).astype(BF)
            p_ref[first + i, h] = p
            o_ref[rows, at : at + HEAD] = dot(p, v, 1, 0, BF)
        part = dot(o_ref[rows, :], w_ref[:, 768:1024], 1, 1, BF)
        keep_ref[i] = part[:128]
        send_ref[i] = part[128:]


def attend(first, count, pieces, weights, saved=(), order=()):
    return kernel(
        functools.partial(attend_body, first, count),
        (
            shape((1024, 768)),
            shape((4, 2, 256, 256)),
            shape((1024, 256)),
            shape((count, 128, 2048)),
            shape((count, 128, 2048)),
        ),
        (*pieces, weights, *saved),
        order,
        input_output_aliases={2 * count + 1 + n: n for n in range(3)} if saved else {},
        name="attend",
    )


def attend_back_body(i, ca, cb, qkv_ref, p_ref, w_ref, *refs):
    g_ref, all_ref, keep_ref, send_ref = refs[-4:]
    rows = slice(256 * i, 256 * (i + 1))
    c = rows_of((ca, cb))
    all_ref[rows, :] = c
    go = dot(c, w_ref[:, 768:1024], 1, 0, BF)
    for h in range(2):
        at = h * HEAD
        q = qkv_ref[rows, at : at + HEAD]
        k = qkv_ref[rows, 256 + at : 256 + at + HEAD]
        v = qkv_ref[rows, 512 + at : 512 + at + HEAD]
        low = p_ref[i, h]
        g = go[:, at : at + HEAD]
        g_ref[rows, 512 + at : 512 + at + HEAD] = dot(low, g, 0, 0, BF)
        gp = dot(g, v, 1, 1)
        p = low.astype(F32)
        gs = (p * (gp - jnp.sum(p * gp, -1, keepdims=True))).astype(BF)
        g_ref[rows, at : at + HEAD] = (dot(gs, k, 1, 0) * SCALE).astype(BF)
        g_ref[rows, 256 + at : 256 + at + HEAD] = (dot(gs, q, 0, 0) * SCALE).astype(BF)
    part = dot(g_ref[rows, :], w_ref[:, :768], 1, 1, BF)
    keep_ref[...] = part[:128]
    send_ref[...] = part[128:]


def attend_back(i, ca, cb, weights, qkv, p, saved, order=()):
    more = () if saved is None else saved
    return kernel(
        functools.partial(attend_back_body, i),
        (shape((1024, 768)), shape((1024, 2048)), shape((128, 2048)), shape((128, 2048))),
        (ca, cb, qkv, p, weights, *more),
        order,
        input_output_aliases={5: 0, 6: 1} if more else {},
        name="attend_back",
    )


def feed_body(i, xa, xb, ga, gb, w_ref, *refs):
    act_ref, g_ref, all_ref, keep_ref, send_ref = refs[-5:]
    rows = slice(256 * i, 256 * (i + 1))
    x = rows_of((xa, xb))
    all_ref[rows, :] = x
    final = rows_of((ga, gb), slice(128, 256))
    for at in range(0, 1024, 256):
        u = dot(x, w_ref[:, at : at + 256], 1, 0)
        ga_hidden = dot(final, w_ref[:, 1024 + at : 1280 + at], 1, 0)
        phi = 0.5 + 0.5 * lax.erf(u * 0.5**0.5)
        act_ref[rows, at : at + 256] = (u * phi).astype(BF)
        slope = phi + u * jnp.exp(-0.5 * u * u) * (0.5 / jnp.pi) ** 0.5
        g_ref[rows, at : at + 256] = (ga_hidden * slope).astype(BF)
    part = dot(g_ref[rows, :], w_ref[:, :1024], 1, 1, BF)
    keep_ref[...] = part[:128]
    send_ref[...] = part[128:]


def feed(i, xa, xb, ga, gb, weights, saved, order=()):
    more = () if saved is None else saved
    return kernel(
        functools.partial(feed_body, i),
        (
            shape((1024, 1024)),
            shape((1024, 1024)),
            shape((1024, 2048)),
            shape((128, 2048)),
            shape((128, 2048)),
        ),
        (xa, xb, ga, gb, weights, *more),
        order,
        input_output_aliases={5: 0, 6: 1, 7: 2} if more else {},
        name="feed",
    )


def feed_out_body(act_ref, down_ref, keep_ref, send_ref):
    part = dot(act_ref[...], down_ref[...], 1, 1, BF)
    for i in range(4):
        keep_ref[i] = part[256 * i : 256 * i + 128]
        send_ref[i] = part[256 * i + 128 : 256 * (i + 1)]


def feed_out(act, weights, order=()):
    out = pl.BlockSpec((4, 128, 256), lambda j: (0, 0, j))
    return kernel(
        feed_out_body,
        (far((4, 128, 2048)), far((4, 128, 2048))),
        (out_of(act), out_of(weights)),
        order,
        grid=(8,),
        in_specs=[
            pl.BlockSpec((1024, 1024), lambda j: (0, 0)),
            pl.BlockSpec((256, 1024), lambda j: (j, 1)),
        ],
        out_specs=(out, out),
        name="feed_out",
    )


def feed_grad_body(x, g, act, *refs):
    gm, out = refs[:8], refs[8]
    columns = pl.ds(pl.multiple_of(pl.program_id(0) * 256, 256), 256)
    out[:, :1024] = dot(x[:, columns], g[...], 0, 0, BF)
    out[:, 1024:] = dot(rows_of(gm), act[...], 0, 0, BF)


def feed_grad(x, g, act, pieces, order=()):
    return kernel(
        feed_grad_body,
        far((2048, 2048)),
        (x, g, act, *map(out_of, pieces)),
        order,
        grid=(8,),
        in_specs=[WHOLE] * 3 + [pl.BlockSpec((128, 256), lambda j: (1, j))] * 8,
        out_specs=pl.BlockSpec((256, 2048), lambda j: (j, 0)),
        name="feed_grad",
    )


def more_grad_body(g, c, o, cross, *refs):
    x, out = refs[:8], refs[8]
    start = pl.multiple_of(pl.program_id(0) * 256, 256)
    columns = pl.ds(start, 256)
    out[:, :768] = dot(rows_of(x), g[...], 0, 0, BF)
    out[:, 768:1024] = dot(c[:, columns], o[...], 0, 0, BF)
    out[:, 1024:] = cross[columns, :]


def more_grad(g, c, o, cross, pieces, order=()):
    return kernel(
        more_grad_body,
        far((2048, 1536)),
        (g, c, o, cross, *map(out_of, pieces)),
        order,
        grid=(8,),
        in_specs=[WHOLE] * 4 + [pl.BlockSpec((128, 256), lambda j: (0, j))] * 8,
        out_specs=pl.BlockSpec((256, 1536), lambda j: (j, 0)),
        name="more_grad",
    )


def fold_body(kv_ref, w_ref, kv_out, both_ref):
    kv = jnp.sum(kv_ref[...].astype(F32), 0).astype(BF)
    kv_out[...] = kv
    for n in range(4):
        at = n * HEAD
        part = dot(kv[:, at : at + HEAD], w_ref[:, at : at + HEAD], 1, 1, BF)
        for i in range(4):
            both_ref[i, n * CAP : (n + 1) * CAP, :] = part[i * CAP : (i + 1) * CAP]


def fold(kv, weights, order=()):
    outs = (shape((64, 512)), shape((4, 64, 2048)))
    return kernel(
        fold_body,
        outs,
        (kv, out_of(weights)),
        order,
        in_specs=[
            pl.BlockSpec((16, 64, 512), lambda j: (0, 0, 0)),
            pl.BlockSpec((2048, 512), lambda j: (0, 2)),
        ],
        out_specs=(
            pl.BlockSpec((64, 512), lambda j: (0, 0)),
            pl.BlockSpec((4, 64, 2048), lambda j: (0, 0, 0)),
        ),
        grid=(1,),
        name="fold",
    )


def unfold_body(b0, b1, b2, b3, kv_ref, w_ref, grad_ref, gkv_ref):
    for n in range(4):
        at = n * HEAD
        rows = rows_of((b0, b1, b2, b3), slice(n * CAP, (n + 1) * CAP))
        grad_ref[:, at : at + HEAD] = dot(rows, kv_ref[:, at : at + HEAD], 0, 0, BF)
        gkv_ref[:, at : at + HEAD] = dot(rows, w_ref[:, at : at + HEAD], 1, 0, BF)


def unfold(back, kv, weights, order=()):
    slot = pl.BlockSpec((64, 2048), lambda j: (0, 0))
    return kernel(
        unfold_body,
        (shape((2048, 512)), shape((64, 512))),
        (*back, kv, out_of(weights)),
        order,
        in_specs=[slot] * 4
        + [
            pl.BlockSpec((64, 512), lambda j: (0, 0)),
            pl.BlockSpec((2048, 512), lambda j: (0, 2)),
        ],
        out_specs=(
            pl.BlockSpec((2048, 512), lambda j: (0, 0)),
            pl.BlockSpec((64, 512), lambda j: (0, 0)),
        ),
        grid=(1,),
        name="unfold",
    )


def slots_of(refs, part):
    return jnp.concatenate([ref[i, part, :] for ref in refs for i in range(4)], 0)


def middle_body(length_ref, *refs):
    x, parts, slots = refs[0], refs[1:6], refs[6:8]
    n2_ref, i2_ref, p2_ref, x3_ref, n3_ref, i3_ref = refs[8:]
    x2 = x[...].astype(F32) + total_of(parts)
    normed, inverse = stats(x2)
    low = normed.astype(BF)
    n2_ref[...] = low
    i2_ref[...] = inverse
    m, n = slots_of(slots, slice(0, 32)), slots_of(slots, slice(32, 64))
    s = (dot(m, low, 1, 1) * SCALE).reshape(16, CAP, 128)
    live = lax.broadcasted_iota(jnp.int32, (1, CAP, 1), 1) < length_ref[0]
    s = jnp.where(live, s, -1e30)
    e = jnp.exp(s - jnp.max(s, 1, keepdims=True))
    p = (e / jnp.sum(e, 1, keepdims=True)).reshape(256, 128)
    p2_ref[...] = p
    x3 = x2 + dot(p.astype(BF), n, 0, 0)
    x3_ref[...] = x3
    normed, inverse = stats(x3)
    n3_ref[...] = normed.astype(BF)
    i3_ref[...] = inverse


def middle(length, x, parts, slots, order=()):
    column = shape((128, 1), F32)
    return kernel(
        middle_body,
        (
            shape((128, 2048)),
            column,
            shape((256, 128), F32),
            shape((128, 2048), F32),
            shape((128, 2048)),
            column,
        ),
        (length, x, *parts, *slots),
        order,
        vmem=16,
        in_specs=[SCALAR] + [WHOLE] * 8,
        name="middle",
    )


def middle_back_body(*refs):
    g3, parts, slots = refs[0], refs[1:6], refs[6:8]
    n2, i2, p2, n3, i3 = refs[8:13]
    g1_ref, low_ref, keep_ref, send_ref = refs[13:]
    g2 = g3[...].astype(F32) + norm_back(total_of(parts), n3[...].astype(F32), i3[...])
    c = g2.astype(BF)
    m, n = slots_of(slots, slice(0, 32)), slots_of(slots, slice(32, 64))
    p = p2[...].reshape(16, CAP, 128)
    gp = dot(n, c, 1, 1).reshape(16, CAP, 128)
    gs = (p * (gp - jnp.sum(p * gp, 1, keepdims=True))).reshape(256, 128) * SCALE
    gs = gs.astype(BF)
    g1 = g2 + norm_back(dot(gs, m, 0, 0), n2[...].astype(F32), i2[...])
    g1_ref[...] = g1
    low_ref[...] = g1.astype(BF)
    gm = dot(gs, n2[...], 1, 0, BF)
    gn = dot(p2[...].astype(BF), c, 1, 0, BF)
    for out, at in ((keep_ref, 0), (send_ref, 128)):
        for i in range(4):
            rows = slice(at + 32 * i, at + 32 * (i + 1))
            out[i, :32, :] = gm[rows]
            out[i, 32:, :] = gn[rows]


def middle_back(g3, parts, slots, n2, i2, p2, n3, i3, order=()):
    slot = shape((4, 64, 2048))
    outs = (shape((128, 2048), F32), shape((128, 2048)), slot, slot)
    args = (g3, *parts, *slots, n2, i2, p2, n3, i3)
    return kernel(middle_back_body, outs, args, order, vmem=16, name="middle_back")


def last_body(*refs):
    g1, parts, x, out = refs[0], refs[1:6], refs[6], refs[7]
    normed, inverse = stats(x[...].astype(F32))
    out[...] = g1[...] + norm_back(total_of(parts), normed, inverse)


def last(g1, parts, x, order=()):
    return kernel(last_body, shape((128, 2048), F32), (g1, *parts, x), order, name="last")


def mix_features(value):
    n = value.shape[0]
    return value.reshape(n, 2, 16, 64).transpose(0, 2, 1, 3).reshape(n, 2048)


def unmix_features(value):
    n = value.shape[0]
    return value.reshape(n, 16, 2, 64).transpose(0, 2, 1, 3).reshape(n, 2048)


def per_device(
    image_tokens,
    caption_embed,
    caption_lengths,
    output_grad,
    norm_self,
    norm_cross,
    norm_feed,
    self_query,
    self_key,
    self_value,
    self_output,
    cross_query,
    cross_key,
    cross_value,
    cross_output,
    up_weight,
    down_weight,
):
    xh = lax.axis_index("xh")
    xl = lax.axis_index("xl")
    core = lax.axis_index("c")
    place = [lax.axis_index("y"), lax.axis_index("z"), 2 * xh + xl, core]
    place = jnp.stack(place).astype(jnp.int32)
    gain_one = norm_self.astype(F32)[:, None]
    gain_two = norm_cross.astype(F32)[:, None]
    gain_three = norm_feed.astype(F32)[:, None]

    def gained(weight, gain):
        return (weight.astype(F32) * gain).astype(BF)

    def halves(weight):
        n = weight.shape[1] // 2
        first, second = weight[:, :n], weight[:, n:]
        return jnp.where(xh == 0, first, second), jnp.where(xh == 0, second, first)

    def in_order(mine, theirs):
        return jnp.where(xh == 0, mine, theirs), jnp.where(xh == 0, theirs, mine)

    def exchange(weights):
        pairs = [halves(w) for w in weights]
        mine = jnp.concatenate([p[0] for p in pairs], 1)
        return mine, swap(jnp.concatenate([p[1] for p in pairs], 1), "xh")

    def both_of(mine, theirs):
        return jnp.stack(in_order(mine, theirs), 0)

    def home(first, second):
        keep = jnp.where(xh == 0, first, second)
        theirs = swap(jnp.where(xh == 0, second, first).astype(BF), "xh")
        return keep, theirs.astype(F32)

    def join(keep, theirs):
        return jnp.concatenate(in_order(keep, theirs), 1)

    pair = both_of(*exchange(
        (
            gained(self_query, gain_one),
            gained(self_key, gain_one),
            gained(self_value, gain_one),
            self_output.T,
            gained(cross_query, gain_two),
            cross_output.T,
        )
    ))
    first = lax.all_gather(pair.reshape(128, 1536), PLANE, axis=0, tiled=True)
    mine_late, theirs_late = exchange(
        (
            gained(up_weight, gain_three),
            down_weight.T,
            cross_key[:64],
            cross_value[:64],
            cross_key[64:],
            cross_value[64:],
        )
    )
    resid = mix_features(image_tokens[0])
    normed_one, _ = stats(resid.astype(F32))
    grad_low = mix_features(output_grad[0])
    caption = after(caption_embed[0], pair)
    sibling = swap(caption, "c")
    caption = jnp.where(core == 0, jnp.stack([caption, sibling]), jnp.stack([sibling, caption]))
    tokens = after(jnp.concatenate([normed_one.astype(BF), grad_low], 0), caption)
    pieces = [tokens, px(tokens, 1), px(tokens, -1)]
    caption = jnp.stack([caption, px(caption, 1), px(caption, -1), px(caption, 2)])
    caption = caption.reshape(64, 2, 16, 128).transpose(2, 0, 1, 3).reshape(16, 64, 256)
    caption = lax.all_to_all(caption, PLANE, split_axis=0, concat_axis=0, tiled=True)
    caption = caption.reshape(1024, 256)
    across = far_of(pieces[1], pieces[2])
    pieces.append(jnp.concatenate(across, 0))
    tokens = [side for piece in pieces for side in (piece, swap(piece, "c"))]
    pair_kv = both_of(mine_late[:, 2048:], theirs_late[:, 2048:])
    pair_kv = jnp.stack([pair_kv[:, :, :512], pair_kv[:, :, 512:]], 1).reshape(256, 512)
    kv = dot(caption, pair_kv, 1, 0, BF)
    pair_late = both_of(mine_late[:, :2048], hold(theirs_late, [*across, kv])[:, :2048])
    feed_weight = pair_late.reshape(128, 2048)
    feed_weight = lax.all_gather(feed_weight, PLANE, axis=0, tiled=True)
    kv = lax.all_to_all(kv.reshape(16, 64, 512), PLANE, split_axis=0, concat_axis=0, tiled=True)
    qkv, p1, o1, keep, send = attend(0, 4, tokens, first)
    kv, both = fold(kv.reshape(16, 64, 512), first, [keep])
    kv_weight = lax.all_gather(after(pair_kv, kv), PLANE, axis=0, tiled=True)
    slots_come = [px(both[1], -1), px(both[2], 1), px(both[3], 2)]
    slots = jnp.stack([both[0], *slots_come], 0)
    slots = (slots, swap(slots, "c"))

    parts, _ = reduce_tokens(keep, swap(send, "c"))
    length = jnp.where(xl == 0, caption_lengths[0, 0], caption_lengths[0, 1])[None]
    n2, i2, p2, x3, n3, i3 = middle(length, resid, parts, slots, [feed_weight])

    theirs = swap(n3, "c")
    around = [px(n3, 1), px(n3, -1)]
    saved, keeps, others = None, [], []
    for i in range(4):
        if i == 0:
            mine = n3
        else:
            if i == 1:
                around = [hold(piece, keeps[:1]) for piece in around]
                across = far_of(*around)
            if i < 3:
                mine = around[i - 1]
            else:
                mine = jnp.concatenate([hold(piece, keeps[1:2]) for piece in across], 0)
            theirs = swap(mine, "c")
        *saved, keep, send = feed(
            i,
            mine,
            theirs,
            tokens[2 * i],
            tokens[2 * i + 1],
            feed_weight,
            saved and tuple(saved),
            others[:-1][-1:],
        )
        keeps.append(keep)
        others.append(swap(send, "c"))
    parts, low = reduce_tokens(keeps, others)
    act, grad, x3_all = saved
    total = feed_grad(x3_all, grad, act, tokens, low + [kv_weight])
    total = hold(total, parts[2:], True)
    g1, c1, keep_slots, send_slots = middle_back(
        grad_low, parts, slots, n2, i2, p2, n3, i3, [total]
    )
    total = lax.psum_scatter(total, PLANE, scatter_dimension=0, tiled=True)
    own, their_ff = home(total[:64], total[64:])
    own = own.astype(F32)
    up_out = join(own[:, :1024], their_ff[:, :1024])
    down_out = join(own[:, 1024:], their_ff[:, 1024:])

    theirs = swap(c1, "c")
    around = [px(c1, 1), px(c1, -1)]
    slot_back = keep_slots.astype(F32) + swap(send_slots, "c").astype(F32)
    back, keeps, others = None, [], []
    for i in range(4):
        if i == 0:
            mine = c1
        else:
            if i == 1:
                around = [hold(piece, keeps[:1]) for piece in around]
                across = far_of(*around)
                slot_back = after(slot_back.astype(BF), around[1])
                slot_back = [
                    slot_back[0],
                    px(slot_back[1], 1),
                    px(slot_back[2], -1),
                    px(slot_back[3], 2),
                ]
            if i < 3:
                mine = around[i - 1]
            else:
                mine = jnp.concatenate([hold(piece, keeps[1:2]) for piece in across], 0)
            theirs = swap(mine, "c")
        order = others[:-1][-1:] + (slot_back[1:] if i == 3 else [])
        *back, keep, send = attend_back(
            i, mine, theirs, first, qkv, p1, back and tuple(back), order
        )
        keeps.append(keep)
        others.append(swap(send, "c"))
    parts, low = reduce_tokens(keeps, others)
    cross_grad, grad_kv = unfold(slot_back, kv, first, keeps[-1:])
    more = more_grad(*back, o1, cross_grad, tokens, keeps[-1:])
    rest = lax.all_to_all(
        more.reshape(16, 128, 1536), PLANE, split_axis=0, concat_axis=0, tiled=True
    )
    y_keep, y_send = feed_out(act, feed_weight, [more, low[-1]])
    y_parts, _ = reduce_tokens(y_keep, swap(y_send, "c"))
    block_out = x3
    for part in y_parts:
        block_out = block_out + part.astype(F32)
    kv_all = hold(grad_kv, [total, more])
    kv_all = lax.all_gather(kv_all, PLANE, axis=0, tiled=True)
    kv_grad = dot(caption, kv_all, 0, 0)
    ck_own, ck_their = home(kv_grad[:128], kv_grad[128:])
    ck_out = join(ck_own[:, :256], ck_their[:, :256])
    cv_out = join(ck_own[:, 256:], ck_their[:, 256:])
    cap_grad = dot(grad_kv, kv_weight, 1, 1, BF).reshape(4, 16, 4096)
    keep = jnp.where(core == 0, cap_grad[:, :8], cap_grad[:, 8:])
    send = jnp.where(core == 0, cap_grad[:, 8:], cap_grad[:, :8])
    send = swap(send, "c")
    low_cap = (keep.astype(F32) + send.astype(F32)).astype(BF)
    cap_out = low_cap[0].astype(F32)
    for image, step in ((1, -1), (2, 1), (3, 2)):
        cap_out = cap_out + px(low_cap[image], step).astype(F32)
    cap_out = cap_out.reshape(8, 16, 2, 128).transpose(0, 2, 1, 3).reshape(1, 8, 4096)
    rest = hold(rest.reshape(2048, 1536), y_parts[2:] + [ck_their], True).reshape(16, 128, 1536)
    rest = jnp.sum(rest.astype(F32), 0)
    own, their = home(rest[:64], rest[64:])
    own = own.astype(F32)
    outs = [join(own[:, at : at + 256], their[:, at : at + 256]) for at in range(0, 1536, 256)]
    so_out, cq_out, co_out = outs[3:]

    image_grad = unmix_features(last(g1, parts, resid, [y_keep]))[None]

    first_gain = (
        jnp.sum(outs[0] * self_query.astype(F32), 1)
        + jnp.sum(outs[1] * self_key.astype(F32), 1)
        + jnp.sum(outs[2] * self_value.astype(F32), 1)
    )
    terms = jnp.stack(
        [
            first_gain,
            jnp.sum(cq_out * cross_query.astype(F32), 1),
            jnp.sum(up_out * up_weight.astype(F32), 1),
        ],
        0,
    )
    terms = terms + swap(terms, "xl")
    terms = terms + swap(terms, "c")

    return (
        unmix_features(block_out.astype(BF))[None],
        image_grad,
        cap_out,
        terms[0],
        terms[1],
        terms[2],
        outs[0] * gain_one,
        outs[1] * gain_one,
        outs[2] * gain_one,
        so_out.T,
        cq_out * gain_two,
        ck_out,
        cv_out,
        co_out.T,
        up_out * gain_three,
        down_out.T,
    )


def solution(mesh):
    names = ("xh", "y", "z", "xl", "c")
    fine = Mesh(mesh.devices.reshape(2, 4, 4, 2, 2), names)
    rows, text = ("xh", "y", "z"), ("xl", "c")
    tokens = P(rows, text, None)
    by_row = P(rows, text)
    by_text = P(text, rows)
    weights = (by_row, by_row, by_row, by_text, by_row, by_row, by_row, by_text, by_row, by_text)
    in_specs = (tokens, tokens, P(rows, None), tokens) + (P(rows),) * 3 + weights
    out_specs = (tokens,) * 3 + (P(rows),) * 3 + weights
    return jax.shard_map(
        per_device, mesh=fine, in_specs=in_specs, out_specs=out_specs, check_vma=False
    )
```

```python
import functools

import jax
import jax.numpy as jnp
from jax import lax
from jax.experimental import pallas as pl
from jax.experimental.pallas import tpu as pltpu
from jax.sharding import Mesh, PartitionSpec as P

HEAD = 128
CAP = 16
EPSILON = 1e-05
SCALE = HEAD ** (-0.5)
BF = jnp.bfloat16
F32 = jnp.float32
RING = ("xh", "xl")
PLANE = ("y", "z")
WHOLE = pl.BlockSpec(memory_space=pltpu.VMEM)
HBM = pl.BlockSpec(memory_space=pltpu.MemorySpace.HBM)
ANY = pl.BlockSpec(memory_space=pl.ANY)
SCALAR = pl.BlockSpec(memory_space=pltpu.SMEM)


def shape(dims, dtype=BF):
    return jax.ShapeDtypeStruct(dims, dtype)


def out_of(value):
    return pltpu.with_memory_space_constraint(value, pltpu.MemorySpace.HBM)


def far(dims, dtype=BF):
    return pltpu.MemorySpace.HBM(dims, dtype)


def kernel(body, outs, args, order=(), vmem=12, in_specs=None, out_specs=None, **more):
    order = [out_of(dep) if dep.size >= 2**20 else dep for dep in order]
    n, outer = len(order), body
    if in_specs is None:
        in_specs = [WHOLE] * len(args)
    if out_specs is None:
        out_specs = jax.tree.map(lambda _: WHOLE, outs)
    spec = more.pop("grid_spec", None)
    if n:
        m = len(args)

        def outer(*refs):
            body(*refs[:m], *refs[m + n :])

    specs = dict(in_specs=list(in_specs) + [HBM] * n, out_specs=out_specs)
    if spec is not None:
        scalars, grid, scratch = spec
        specs = dict(
            grid_spec=pltpu.PrefetchScalarGridSpec(
                num_scalar_prefetch=scalars, grid=grid, scratch_shapes=scratch, **specs
            )
        )
    return pl.pallas_call(
        outer,
        out_shape=outs,
        compiler_params=pltpu.CompilerParams(vmem_limit_bytes=vmem * 2**20),
        cost_estimate=pl.CostEstimate(flops=1000, bytes_accessed=1000, transcendentals=0),
        **specs,
        **more,
    )(*args, *order)


def hold_body(value, out):
    pass


def hold(value, order, away=False):
    return kernel(
        hold_body,
        far(value.shape, value.dtype) if away else shape(value.shape, value.dtype),
        (out_of(value) if away else value,),
        order,
        vmem=4,
        in_specs=[ANY],
        out_specs=ANY,
        input_output_aliases={0: 0},
        name="hold",
    )


def dot(a, b, ca, cb, out=F32):
    return lax.dot_general(a, b, (((ca,), (cb,)), ((), ())), preferred_element_type=F32).astype(out)


def px(value, step):
    return lax.ppermute(value, RING, [(i, (i + step) % 4) for i in range(4)])


def pp(value, axis, step):
    return lax.ppermute(value, axis, [(i, (i + step) % 4) for i in range(4)])


def swap(value, axis):
    return lax.ppermute(value, axis, [(0, 1), (1, 0)])


def after(value, dep):
    first = dep[(slice(0, 1),) * dep.ndim].reshape((1,) * value.ndim).astype(F32)
    return (value.astype(F32) + first * 0.0).astype(value.dtype)


def far_of(left, right):
    half = left.shape[0] // 2
    return [px(left[:half], 1), px(right[half:], -1)]


def pick(value, at):
    return lax.dynamic_index_in_dim(value, at & 3, 0, False, allow_negative_indices=False)


def reduce_tokens(keep, other):
    low = [(keep[i].astype(F32) + other[i].astype(F32)).astype(BF) for i in range(1, 4)]
    return [keep[0], other[0], px(low[0], -1), px(low[1], 1), px(low[2], 2)], low


def stats(resid):
    mean = jnp.mean(resid, -1, keepdims=True)
    centered = resid - mean
    inverse = lax.rsqrt(jnp.mean(centered * centered, -1, keepdims=True) + EPSILON)
    return centered * inverse, inverse


def norm_back(scaled, normed, inverse):
    return inverse * (
        scaled
        - jnp.mean(scaled, -1, keepdims=True)
        - normed * jnp.mean(scaled * normed, -1, keepdims=True)
    )


def total_of(refs):
    total = refs[0][...].astype(F32)
    for ref in refs[1:]:
        total = total + ref[...].astype(F32)
    return total


def rows_of(refs, part=slice(None)):
    return jnp.concatenate([ref[part, :] for ref in refs], 0)


def attend_body(first, count, *refs):
    pieces, w_ref = refs[: 2 * count], refs[2 * count]
    qkv_ref, p_ref, o_ref, keep_ref, send_ref = refs[-5:]
    for i in range(count):
        rows = slice(256 * (first + i), 256 * (first + i + 1))
        x = rows_of(pieces[2 * i : 2 * i + 2], slice(0, 128))
        qkv_ref[rows, :] = dot(x, w_ref[:, :768], 1, 0, BF)
        for h in range(2):
            at = h * HEAD
            q = qkv_ref[rows, at : at + HEAD]
            k = qkv_ref[rows, 256 + at : 256 + at + HEAD]
            v = qkv_ref[rows, 512 + at : 512 + at + HEAD]
            s = dot(q, k, 1, 1) * SCALE
            e = jnp.exp(s - jnp.max(s, -1, keepdims=True))
            p = (e / jnp.sum(e, -1, keepdims=True)).astype(BF)
            p_ref[first + i, h] = p
            o_ref[rows, at : at + HEAD] = dot(p, v, 1, 0, BF)
        part = dot(o_ref[rows, :], w_ref[:, 768:1024], 1, 1, BF)
        keep_ref[i] = part[:128]
        send_ref[i] = part[128:]


def attend(first, count, pieces, weights, saved=(), order=()):
    return kernel(
        functools.partial(attend_body, first, count),
        (
            shape((1024, 768)),
            shape((4, 2, 256, 256)),
            shape((1024, 256)),
            shape((count, 128, 2048)),
            shape((count, 128, 2048)),
        ),
        (*pieces, weights, *saved),
        order,
        input_output_aliases={2 * count + 1 + n: n for n in range(3)} if saved else {},
        name="attend",
    )


def attend_back_body(i, ca, cb, qkv_ref, p_ref, w_ref, *refs):
    g_ref, all_ref, keep_ref, send_ref = refs[-4:]
    rows = slice(256 * i, 256 * (i + 1))
    c = rows_of((ca, cb))
    all_ref[rows, :] = c
    go = dot(c, w_ref[:, 768:1024], 1, 0, BF)
    for h in range(2):
        at = h * HEAD
        q = qkv_ref[rows, at : at + HEAD]
        k = qkv_ref[rows, 256 + at : 256 + at + HEAD]
        v = qkv_ref[rows, 512 + at : 512 + at + HEAD]
        low = p_ref[i, h]
        g = go[:, at : at + HEAD]
        g_ref[rows, 512 + at : 512 + at + HEAD] = dot(low, g, 0, 0, BF)
        gp = dot(g, v, 1, 1)
        p = low.astype(F32)
        gs = (p * (gp - jnp.sum(p * gp, -1, keepdims=True))).astype(BF)
        g_ref[rows, at : at + HEAD] = (dot(gs, k, 1, 0) * SCALE).astype(BF)
        g_ref[rows, 256 + at : 256 + at + HEAD] = (dot(gs, q, 0, 0) * SCALE).astype(BF)
    part = dot(g_ref[rows, :], w_ref[:, :768], 1, 1, BF)
    keep_ref[...] = part[:128]
    send_ref[...] = part[128:]


def attend_back(i, ca, cb, weights, qkv, p, saved, order=()):
    more = () if saved is None else saved
    return kernel(
        functools.partial(attend_back_body, i),
        (shape((1024, 768)), shape((1024, 2048)), shape((128, 2048)), shape((128, 2048))),
        (ca, cb, qkv, p, weights, *more),
        order,
        input_output_aliases={5: 0, 6: 1} if more else {},
        name="attend_back",
    )


def feed_body(i, xa, xb, ga, gb, w_ref, *refs):
    act_ref, g_ref, all_ref, keep_ref, send_ref = refs[-5:]
    rows = slice(256 * i, 256 * (i + 1))
    x = rows_of((xa, xb))
    all_ref[rows, :] = x
    final = rows_of((ga, gb), slice(128, 256))
    for at in range(0, 1024, 256):
        u = dot(x, w_ref[:, at : at + 256], 1, 0)
        ga_hidden = dot(final, w_ref[:, 1024 + at : 1280 + at], 1, 0)
        phi = 0.5 + 0.5 * lax.erf(u * 0.5**0.5)
        act_ref[rows, at : at + 256] = (u * phi).astype(BF)
        slope = phi + u * jnp.exp(-0.5 * u * u) * (0.5 / jnp.pi) ** 0.5
        g_ref[rows, at : at + 256] = (ga_hidden * slope).astype(BF)
    part = dot(g_ref[rows, :], w_ref[:, :1024], 1, 1, BF)
    keep_ref[...] = part[:128]
    send_ref[...] = part[128:]


def feed(i, xa, xb, ga, gb, weights, saved, order=()):
    more = () if saved is None else saved
    return kernel(
        functools.partial(feed_body, i),
        (
            shape((1024, 1024)),
            shape((1024, 1024)),
            shape((1024, 2048)),
            shape((128, 2048)),
            shape((128, 2048)),
        ),
        (xa, xb, ga, gb, weights, *more),
        order,
        input_output_aliases={5: 0, 6: 1, 7: 2} if more else {},
        name="feed",
    )


def feed_out_body(act_ref, down_ref, keep_ref, send_ref):
    part = dot(act_ref[...], down_ref[...], 1, 1, BF)
    for i in range(4):
        keep_ref[i] = part[256 * i : 256 * i + 128]
        send_ref[i] = part[256 * i + 128 : 256 * (i + 1)]


def feed_out(act, weights, order=()):
    out = pl.BlockSpec((4, 128, 256), lambda j: (0, 0, j))
    return kernel(
        feed_out_body,
        (far((4, 128, 2048)), far((4, 128, 2048))),
        (out_of(act), out_of(weights)),
        order,
        grid=(8,),
        in_specs=[
            pl.BlockSpec((1024, 1024), lambda j: (0, 0)),
            pl.BlockSpec((256, 1024), lambda j: (j, 1)),
        ],
        out_specs=(out, out),
        name="feed_out",
    )


def feed_grad_body(x, g, act, *refs):
    gm, out = refs[:8], refs[8]
    columns = pl.ds(pl.multiple_of(pl.program_id(0) * 256, 256), 256)
    out[:, :1024] = dot(x[:, columns], g[...], 0, 0, BF)
    out[:, 1024:] = dot(rows_of(gm), act[...], 0, 0, BF)


def feed_grad(x, g, act, pieces, order=()):
    return kernel(
        feed_grad_body,
        far((2048, 2048)),
        (x, g, act, *map(out_of, pieces)),
        order,
        grid=(8,),
        in_specs=[WHOLE] * 3 + [pl.BlockSpec((128, 256), lambda j: (1, j))] * 8,
        out_specs=pl.BlockSpec((256, 2048), lambda j: (j, 0)),
        name="feed_grad",
    )


def more_grad_body(g, c, o, cross, *refs):
    x, out = refs[:8], refs[8]
    start = pl.multiple_of(pl.program_id(0) * 256, 256)
    columns = pl.ds(start, 256)
    out[:, :768] = dot(rows_of(x), g[...], 0, 0, BF)
    out[:, 768:1024] = dot(c[:, columns], o[...], 0, 0, BF)
    out[:, 1024:] = cross[columns, :]


def more_grad(g, c, o, cross, pieces, order=()):
    return kernel(
        more_grad_body,
        far((2048, 1536)),
        (g, c, o, cross, *map(out_of, pieces)),
        order,
        grid=(8,),
        in_specs=[WHOLE] * 4 + [pl.BlockSpec((128, 256), lambda j: (0, j))] * 8,
        out_specs=pl.BlockSpec((256, 1536), lambda j: (j, 0)),
        name="more_grad",
    )


def fold_body(kv_ref, w_ref, kv_out, both_ref):
    kv = jnp.sum(kv_ref[...].astype(F32), 0).astype(BF)
    kv_out[...] = kv
    for n in range(4):
        at = n * HEAD
        part = dot(kv[:, at : at + HEAD], w_ref[:, at : at + HEAD], 1, 1, BF)
        for i in range(4):
            both_ref[i, n * CAP : (n + 1) * CAP, :] = part[i * CAP : (i + 1) * CAP]


def fold(kv, weights, order=()):
    outs = (shape((64, 512)), shape((4, 64, 2048)))
    return kernel(
        fold_body,
        outs,
        (kv, out_of(weights)),
        order,
        in_specs=[
            pl.BlockSpec((16, 64, 512), lambda j: (0, 0, 0)),
            pl.BlockSpec((2048, 512), lambda j: (0, 2)),
        ],
        out_specs=(
            pl.BlockSpec((64, 512), lambda j: (0, 0)),
            pl.BlockSpec((4, 64, 2048), lambda j: (0, 0, 0)),
        ),
        grid=(1,),
        name="fold",
    )


def unfold_body(b0, b1, b2, b3, kv_ref, w_ref, grad_ref, gkv_ref):
    for n in range(4):
        at = n * HEAD
        rows = rows_of((b0, b1, b2, b3), slice(n * CAP, (n + 1) * CAP))
        grad_ref[:, at : at + HEAD] = dot(rows, kv_ref[:, at : at + HEAD], 0, 0, BF)
        gkv_ref[:, at : at + HEAD] = dot(rows, w_ref[:, at : at + HEAD], 1, 0, BF)


def unfold(back, kv, weights, order=()):
    slot = pl.BlockSpec((64, 2048), lambda j: (0, 0))
    return kernel(
        unfold_body,
        (shape((2048, 512)), shape((64, 512))),
        (*back, kv, out_of(weights)),
        order,
        in_specs=[slot] * 4
        + [
            pl.BlockSpec((64, 512), lambda j: (0, 0)),
            pl.BlockSpec((2048, 512), lambda j: (0, 2)),
        ],
        out_specs=(
            pl.BlockSpec((2048, 512), lambda j: (0, 0)),
            pl.BlockSpec((64, 512), lambda j: (0, 0)),
        ),
        grid=(1,),
        name="unfold",
    )


def slots_of(refs, part):
    return jnp.concatenate([ref[i, part, :] for ref in refs for i in range(4)], 0)


def middle_body(length_ref, *refs):
    x, parts, slots = refs[0], refs[1:6], refs[6:8]
    n2_ref, i2_ref, p2_ref, x3_ref, n3_ref, i3_ref = refs[8:]
    x2 = x[...].astype(F32) + total_of(parts)
    normed, inverse = stats(x2)
    low = normed.astype(BF)
    n2_ref[...] = low
    i2_ref[...] = inverse
    m, n = slots_of(slots, slice(0, 32)), slots_of(slots, slice(32, 64))
    s = (dot(m, low, 1, 1) * SCALE).reshape(16, CAP, 128)
    live = lax.broadcasted_iota(jnp.int32, (1, CAP, 1), 1) < length_ref[0]
    s = jnp.where(live, s, -1e30)
    e = jnp.exp(s - jnp.max(s, 1, keepdims=True))
    p = (e / jnp.sum(e, 1, keepdims=True)).reshape(256, 128)
    p2_ref[...] = p
    x3 = x2 + dot(p.astype(BF), n, 0, 0)
    x3_ref[...] = x3
    normed, inverse = stats(x3)
    n3_ref[...] = normed.astype(BF)
    i3_ref[...] = inverse


def middle(length, x, parts, slots, order=()):
    column = shape((128, 1), F32)
    return kernel(
        middle_body,
        (
            shape((128, 2048)),
            column,
            shape((256, 128), F32),
            shape((128, 2048), F32),
            shape((128, 2048)),
            column,
        ),
        (length, x, *parts, *slots),
        order,
        vmem=16,
        in_specs=[SCALAR] + [WHOLE] * 8,
        name="middle",
    )


def middle_back_body(*refs):
    g3, parts, slots = refs[0], refs[1:6], refs[6:8]
    n2, i2, p2, n3, i3 = refs[8:13]
    g1_ref, low_ref, keep_ref, send_ref = refs[13:]
    g2 = g3[...].astype(F32) + norm_back(total_of(parts), n3[...].astype(F32), i3[...])
    c = g2.astype(BF)
    m, n = slots_of(slots, slice(0, 32)), slots_of(slots, slice(32, 64))
    p = p2[...].reshape(16, CAP, 128)
    gp = dot(n, c, 1, 1).reshape(16, CAP, 128)
    gs = (p * (gp - jnp.sum(p * gp, 1, keepdims=True))).reshape(256, 128) * SCALE
    gs = gs.astype(BF)
    g1 = g2 + norm_back(dot(gs, m, 0, 0), n2[...].astype(F32), i2[...])
    g1_ref[...] = g1
    low_ref[...] = g1.astype(BF)
    gm = dot(gs, n2[...], 1, 0, BF)
    gn = dot(p2[...].astype(BF), c, 1, 0, BF)
    for out, at in ((keep_ref, 0), (send_ref, 128)):
        for i in range(4):
            rows = slice(at + 32 * i, at + 32 * (i + 1))
            out[i, :32, :] = gm[rows]
            out[i, 32:, :] = gn[rows]


def middle_back(g3, parts, slots, n2, i2, p2, n3, i3, order=()):
    slot = shape((4, 64, 2048))
    outs = (shape((128, 2048), F32), shape((128, 2048)), slot, slot)
    args = (g3, *parts, *slots, n2, i2, p2, n3, i3)
    return kernel(middle_back_body, outs, args, order, vmem=16, name="middle_back")


def last_body(*refs):
    g1, parts, x, out = refs[0], refs[1:6], refs[6], refs[7]
    normed, inverse = stats(x[...].astype(F32))
    out[...] = g1[...] + norm_back(total_of(parts), normed, inverse)


def last(g1, parts, x, order=()):
    return kernel(last_body, shape((128, 2048), F32), (g1, *parts, x), order, name="last")


def mix_features(value):
    n = value.shape[0]
    return value.reshape(n, 2, 16, 64).transpose(0, 2, 1, 3).reshape(n, 2048)


def unmix_features(value):
    n = value.shape[0]
    return value.reshape(n, 16, 2, 64).transpose(0, 2, 1, 3).reshape(n, 2048)


def per_device(
    image_tokens,
    caption_embed,
    caption_lengths,
    output_grad,
    norm_self,
    norm_cross,
    norm_feed,
    self_query,
    self_key,
    self_value,
    self_output,
    cross_query,
    cross_key,
    cross_value,
    cross_output,
    up_weight,
    down_weight,
):
    xh = lax.axis_index("xh")
    xl = lax.axis_index("xl")
    core = lax.axis_index("c")
    place = [lax.axis_index("y"), lax.axis_index("z"), 2 * xh + xl, core]
    place = jnp.stack(place).astype(jnp.int32)
    gain_one = norm_self.astype(F32)[:, None]
    gain_two = norm_cross.astype(F32)[:, None]
    gain_three = norm_feed.astype(F32)[:, None]

    def gained(weight, gain):
        return (weight.astype(F32) * gain).astype(BF)

    def halves(weight):
        n = weight.shape[1] // 2
        first, second = weight[:, :n], weight[:, n:]
        return jnp.where(xh == 0, first, second), jnp.where(xh == 0, second, first)

    def in_order(mine, theirs):
        return jnp.where(xh == 0, mine, theirs), jnp.where(xh == 0, theirs, mine)

    def exchange(weights):
        pairs = [halves(w) for w in weights]
        mine = jnp.concatenate([p[0] for p in pairs], 1)
        return mine, swap(jnp.concatenate([p[1] for p in pairs], 1), "xh")

    def both_of(mine, theirs):
        return jnp.stack(in_order(mine, theirs), 0)

    def home(first, second):
        keep = jnp.where(xh == 0, first, second)
        theirs = swap(jnp.where(xh == 0, second, first).astype(BF), "xh")
        return keep, theirs.astype(F32)

    def join(keep, theirs):
        return jnp.concatenate(in_order(keep, theirs), 1)

    pair = both_of(*exchange(
        (
            gained(self_query, gain_one),
            gained(self_key, gain_one),
            gained(self_value, gain_one),
            self_output.T,
            gained(cross_query, gain_two),
            cross_output.T,
        )
    ))
    first = lax.all_gather(pair.reshape(128, 1536), PLANE, axis=0, tiled=True)
    mine_late, theirs_late = exchange(
        (
            gained(up_weight, gain_three),
            down_weight.T,
            cross_key[:64],
            cross_value[:64],
            cross_key[64:],
            cross_value[64:],
        )
    )
    resid = mix_features(image_tokens[0])
    normed_one, _ = stats(resid.astype(F32))
    grad_low = mix_features(output_grad[0])
    caption = after(caption_embed[0], pair)
    sibling = swap(caption, "c")
    caption = jnp.where(core == 0, jnp.stack([caption, sibling]), jnp.stack([sibling, caption]))
    caption = jnp.stack([caption, px(caption, 1), px(caption, -1), px(caption, 2)])
    caption = caption.reshape(64, 2, 16, 128).transpose(2, 0, 1, 3).reshape(16, 64, 256)
    tokens = after(jnp.concatenate([normed_one.astype(BF), grad_low], 0), caption)
    pieces = [tokens, px(tokens, 1), px(tokens, -1)]
    caption = lax.all_to_all(caption, PLANE, split_axis=0, concat_axis=0, tiled=True)
    caption = caption.reshape(1024, 256)
    across = far_of(pieces[1], pieces[2])
    pieces.append(jnp.concatenate(across, 0))
    tokens = [side for piece in pieces for side in (piece, swap(piece, "c"))]
    pair_kv = both_of(mine_late[:, 2048:], theirs_late[:, 2048:])
    pair_kv = jnp.stack([pair_kv[:, :, :512], pair_kv[:, :, 512:]], 1).reshape(256, 512)
    kv = dot(caption, pair_kv, 1, 0, BF)
    pair_late = both_of(mine_late[:, :2048], hold(theirs_late, [*across, kv])[:, :2048])
    feed_weight = pair_late.reshape(128, 2048)
    feed_weight = lax.all_gather(feed_weight, PLANE, axis=0, tiled=True)
    kv = lax.all_to_all(kv.reshape(16, 64, 512), PLANE, split_axis=0, concat_axis=0, tiled=True)
    qkv, p1, o1, keep, send = attend(0, 4, tokens, first)
    kv, both = fold(kv.reshape(16, 64, 512), first, [keep])
    kv_weight = lax.all_gather(after(pair_kv, kv), PLANE, axis=0, tiled=True)
    slots_come = [px(both[1], -1), px(both[2], 1), px(both[3], 2)]
    slots = jnp.stack([both[0], *slots_come], 0)
    slots = (slots, swap(slots, "c"))

    parts, _ = reduce_tokens(keep, swap(send, "c"))
    length = jnp.where(xl == 0, caption_lengths[0, 0], caption_lengths[0, 1])[None]
    n2, i2, p2, x3, n3, i3 = middle(length, resid, parts, slots, [feed_weight])

    theirs = swap(n3, "c")
    around = [px(n3, 1), px(n3, -1)]
    saved, keeps, others = None, [], []
    for i in range(4):
        if i == 0:
            mine = n3
        else:
            if i == 1:
                around = [hold(piece, keeps[:1]) for piece in around]
                across = far_of(*around)
            if i < 3:
                mine = around[i - 1]
            else:
                mine = jnp.concatenate([hold(piece, keeps[1:2]) for piece in across], 0)
            theirs = swap(mine, "c")
        *saved, keep, send = feed(
            i,
            mine,
            theirs,
            tokens[2 * i],
            tokens[2 * i + 1],
            feed_weight,
            saved and tuple(saved),
            others[:-1][-1:],
        )
        keeps.append(keep)
        others.append(swap(send, "c"))
    parts, low = reduce_tokens(keeps, others)
    act, grad, x3_all = saved
    total = feed_grad(x3_all, grad, act, tokens, low + [kv_weight])
    total = hold(total, parts[2:], True)
    g1, c1, keep_slots, send_slots = middle_back(
        grad_low, parts, slots, n2, i2, p2, n3, i3, [total]
    )
    total = lax.psum_scatter(total, PLANE, scatter_dimension=0, tiled=True)
    own, their_ff = home(total[:64], total[64:])
    own = own.astype(F32)
    up_out = join(own[:, :1024], their_ff[:, :1024])
    down_out = join(own[:, 1024:], their_ff[:, 1024:])

    theirs = swap(c1, "c")
    around = [px(c1, 1), px(c1, -1)]
    slot_back = keep_slots.astype(F32) + swap(send_slots, "c").astype(F32)
    back, keeps, others = None, [], []
    for i in range(4):
        if i == 0:
            mine = c1
        else:
            if i == 1:
                around = [hold(piece, keeps[:1]) for piece in around]
                across = far_of(*around)
                slot_back = after(slot_back.astype(BF), around[1])
                slot_back = [
                    slot_back[0],
                    px(slot_back[1], 1),
                    px(slot_back[2], -1),
                    px(slot_back[3], 2),
                ]
            if i < 3:
                mine = around[i - 1]
            else:
                mine = jnp.concatenate([hold(piece, keeps[1:2]) for piece in across], 0)
            theirs = swap(mine, "c")
        order = others[:-1][-1:] + (slot_back[1:] if i == 3 else [])
        *back, keep, send = attend_back(
            i, mine, theirs, first, qkv, p1, back and tuple(back), order
        )
        keeps.append(keep)
        others.append(swap(send, "c"))
    parts, low = reduce_tokens(keeps, others)
    cross_grad, grad_kv = unfold(slot_back, kv, first, keeps[-1:])
    more = more_grad(*back, o1, cross_grad, tokens, keeps[-1:])
    more = hold(more, [total, low[-1]], True)
    y_keep, y_send = feed_out(act, feed_weight, [more])
    rest = lax.psum_scatter(more, PLANE, scatter_dimension=0, tiled=True)
    y_parts, _ = reduce_tokens(y_keep, swap(y_send, "c"))
    block_out = x3
    for part in y_parts:
        block_out = block_out + part.astype(F32)
    grad_kv = after(grad_kv, more)
    kv_all = lax.all_to_all(
        jnp.broadcast_to(grad_kv[None], (16, 64, 512)),
        PLANE,
        split_axis=0,
        concat_axis=0,
        tiled=True,
    ).reshape(1024, 512)
    kv_grad = dot(caption, kv_all, 0, 0)
    ck_own, ck_their = home(kv_grad[:128], kv_grad[128:])
    ck_out = join(ck_own[:, :256], ck_their[:, :256])
    cv_out = join(ck_own[:, 256:], ck_their[:, 256:])
    cap_grad = dot(grad_kv, kv_weight, 1, 1, BF).reshape(4, 16, 4096)
    keep = jnp.where(core == 0, cap_grad[:, :8], cap_grad[:, 8:])
    send = jnp.where(core == 0, cap_grad[:, 8:], cap_grad[:, :8])
    send = swap(send, "c")
    low_cap = (keep.astype(F32) + send.astype(F32)).astype(BF)
    cap_out = low_cap[0].astype(F32)
    for image, step in ((1, -1), (2, 1), (3, 2)):
        cap_out = cap_out + px(low_cap[image], step).astype(F32)
    cap_out = cap_out.reshape(8, 16, 2, 128).transpose(0, 2, 1, 3).reshape(1, 8, 4096)
    rest = hold(rest, y_parts[2:], True)
    own, their = home(rest[:64], rest[64:])
    own = own.astype(F32)
    outs = [join(own[:, at : at + 256], their[:, at : at + 256]) for at in range(0, 1536, 256)]
    so_out, cq_out, co_out = outs[3:]

    image_grad = unmix_features(last(g1, parts, resid, [y_keep]))[None]

    first_gain = (
        jnp.sum(outs[0] * self_query.astype(F32), 1)
        + jnp.sum(outs[1] * self_key.astype(F32), 1)
        + jnp.sum(outs[2] * self_value.astype(F32), 1)
    )
    terms = jnp.stack(
        [
            first_gain,
            jnp.sum(cq_out * cross_query.astype(F32), 1),
            jnp.sum(up_out * up_weight.astype(F32), 1),
        ],
        0,
    )
    terms = terms + swap(terms, "xl")
    terms = terms + swap(terms, "c")

    return (
        unmix_features(block_out.astype(BF))[None],
        image_grad,
        cap_out,
        terms[0],
        terms[1],
        terms[2],
        outs[0] * gain_one,
        outs[1] * gain_one,
        outs[2] * gain_one,
        so_out.T,
        cq_out * gain_two,
        ck_out,
        cv_out,
        co_out.T,
        up_out * gain_three,
        down_out.T,
    )


def solution(mesh):
    names = ("xh", "y", "z", "xl", "c")
    fine = Mesh(mesh.devices.reshape(2, 4, 4, 2, 2), names)
    rows, text = ("xh", "y", "z"), ("xl", "c")
    tokens = P(rows, text, None)
    by_row = P(rows, text)
    by_text = P(text, rows)
    weights = (by_row, by_row, by_row, by_text, by_row, by_row, by_row, by_text, by_row, by_text)
    in_specs = (tokens, tokens, P(rows, None), tokens) + (P(rows),) * 3 + weights
    out_specs = (tokens,) * 3 + (P(rows),) * 3 + weights
    return jax.shard_map(
        per_device, mesh=fine, in_specs=in_specs, out_specs=out_specs, check_vma=False
    )
```

```python
import functools

import jax
import jax.numpy as jnp
from jax import lax
from jax.experimental import pallas as pl
from jax.experimental.pallas import tpu as pltpu
from jax.sharding import Mesh, PartitionSpec as P

HEAD = 128
CAP = 16
EPSILON = 1e-05
SCALE = HEAD ** (-0.5)
BF = jnp.bfloat16
F32 = jnp.float32
RING = ("xh", "xl")
PLANE = ("y", "z")
WHOLE = pl.BlockSpec(memory_space=pltpu.VMEM)
HBM = pl.BlockSpec(memory_space=pltpu.MemorySpace.HBM)
ANY = pl.BlockSpec(memory_space=pl.ANY)
SCALAR = pl.BlockSpec(memory_space=pltpu.SMEM)


def shape(dims, dtype=BF):
    return jax.ShapeDtypeStruct(dims, dtype)


def out_of(value):
    return pltpu.with_memory_space_constraint(value, pltpu.MemorySpace.HBM)


def far(dims, dtype=BF):
    return pltpu.MemorySpace.HBM(dims, dtype)


def kernel(body, outs, args, order=(), vmem=12, in_specs=None, out_specs=None, **more):
    order = [out_of(dep) if dep.size >= 2**20 else dep for dep in order]
    n, outer = len(order), body
    if in_specs is None:
        in_specs = [WHOLE] * len(args)
    if out_specs is None:
        out_specs = jax.tree.map(lambda _: WHOLE, outs)
    spec = more.pop("grid_spec", None)
    if n:
        m = len(args)

        def outer(*refs):
            body(*refs[:m], *refs[m + n :])

    specs = dict(in_specs=list(in_specs) + [HBM] * n, out_specs=out_specs)
    if spec is not None:
        scalars, grid, scratch = spec
        specs = dict(
            grid_spec=pltpu.PrefetchScalarGridSpec(
                num_scalar_prefetch=scalars, grid=grid, scratch_shapes=scratch, **specs
            )
        )
    return pl.pallas_call(
        outer,
        out_shape=outs,
        compiler_params=pltpu.CompilerParams(vmem_limit_bytes=vmem * 2**20),
        cost_estimate=pl.CostEstimate(flops=1000, bytes_accessed=1000, transcendentals=0),
        **specs,
        **more,
    )(*args, *order)


def hold_body(value, out):
    pass


def hold(value, order, away=False):
    return kernel(
        hold_body,
        far(value.shape, value.dtype) if away else shape(value.shape, value.dtype),
        (out_of(value) if away else value,),
        order,
        vmem=4,
        in_specs=[ANY],
        out_specs=ANY,
        input_output_aliases={0: 0},
        name="hold",
    )


def dot(a, b, ca, cb, out=F32):
    return lax.dot_general(a, b, (((ca,), (cb,)), ((), ())), preferred_element_type=F32).astype(out)


def px(value, step):
    return lax.ppermute(value, RING, [(i, (i + step) % 4) for i in range(4)])


def pp(value, axis, step):
    return lax.ppermute(value, axis, [(i, (i + step) % 4) for i in range(4)])


def swap(value, axis):
    return lax.ppermute(value, axis, [(0, 1), (1, 0)])


def after(value, dep):
    first = dep[(slice(0, 1),) * dep.ndim].reshape((1,) * value.ndim).astype(F32)
    return (value.astype(F32) + first * 0.0).astype(value.dtype)


def far_of(left, right):
    half = left.shape[0] // 2
    return [px(left[:half], 1), px(right[half:], -1)]


def pick(value, at):
    return lax.dynamic_index_in_dim(value, at & 3, 0, False, allow_negative_indices=False)


def reduce_tokens(keep, other):
    low = [(keep[i].astype(F32) + other[i].astype(F32)).astype(BF) for i in range(1, 4)]
    return [keep[0], other[0], px(low[0], -1), px(low[1], 1), px(low[2], 2)], low


def stats(resid):
    mean = jnp.mean(resid, -1, keepdims=True)
    centered = resid - mean
    inverse = lax.rsqrt(jnp.mean(centered * centered, -1, keepdims=True) + EPSILON)
    return centered * inverse, inverse


def norm_back(scaled, normed, inverse):
    return inverse * (
        scaled
        - jnp.mean(scaled, -1, keepdims=True)
        - normed * jnp.mean(scaled * normed, -1, keepdims=True)
    )


def total_of(refs):
    total = refs[0][...].astype(F32)
    for ref in refs[1:]:
        total = total + ref[...].astype(F32)
    return total


def rows_of(refs, part=slice(None)):
    return jnp.concatenate([ref[part, :] for ref in refs], 0)


def attend_body(first, count, *refs):
    pieces, w_ref = refs[: 2 * count], refs[2 * count]
    qkv_ref, p_ref, o_ref, keep_ref, send_ref = refs[-5:]
    for i in range(count):
        rows = slice(256 * (first + i), 256 * (first + i + 1))
        x = rows_of(pieces[2 * i : 2 * i + 2], slice(0, 128))
        qkv_ref[rows, :] = dot(x, w_ref[:, :768], 1, 0, BF)
        for h in range(2):
            at = h * HEAD
            q = qkv_ref[rows, at : at + HEAD]
            k = qkv_ref[rows, 256 + at : 256 + at + HEAD]
            v = qkv_ref[rows, 512 + at : 512 + at + HEAD]
            s = dot(q, k, 1, 1) * SCALE
            e = jnp.exp(s - jnp.max(s, -1, keepdims=True))
            p = (e / jnp.sum(e, -1, keepdims=True)).astype(BF)
            p_ref[first + i, h] = p
            o_ref[rows, at : at + HEAD] = dot(p, v, 1, 0, BF)
        part = dot(o_ref[rows, :], w_ref[:, 768:1024], 1, 1, BF)
        keep_ref[i] = part[:128]
        send_ref[i] = part[128:]


def attend(first, count, pieces, weights, saved=(), order=()):
    return kernel(
        functools.partial(attend_body, first, count),
        (
            shape((1024, 768)),
            shape((4, 2, 256, 256)),
            shape((1024, 256)),
            shape((count, 128, 2048)),
            shape((count, 128, 2048)),
        ),
        (*pieces, weights, *saved),
        order,
        input_output_aliases={2 * count + 1 + n: n for n in range(3)} if saved else {},
        name="attend",
    )


def attend_back_body(i, ca, cb, qkv_ref, p_ref, w_ref, *refs):
    g_ref, all_ref, keep_ref, send_ref = refs[-4:]
    rows = slice(256 * i, 256 * (i + 1))
    c = rows_of((ca, cb))
    all_ref[rows, :] = c
    go = dot(c, w_ref[:, 768:1024], 1, 0, BF)
    for h in range(2):
        at = h * HEAD
        q = qkv_ref[rows, at : at + HEAD]
        k = qkv_ref[rows, 256 + at : 256 + at + HEAD]
        v = qkv_ref[rows, 512 + at : 512 + at + HEAD]
        low = p_ref[i, h]
        g = go[:, at : at + HEAD]
        g_ref[rows, 512 + at : 512 + at + HEAD] = dot(low, g, 0, 0, BF)
        gp = dot(g, v, 1, 1)
        p = low.astype(F32)
        gs = (p * (gp - jnp.sum(p * gp, -1, keepdims=True))).astype(BF)
        g_ref[rows, at : at + HEAD] = (dot(gs, k, 1, 0) * SCALE).astype(BF)
        g_ref[rows, 256 + at : 256 + at + HEAD] = (dot(gs, q, 0, 0) * SCALE).astype(BF)
    part = dot(g_ref[rows, :], w_ref[:, :768], 1, 1, BF)
    keep_ref[...] = part[:128]
    send_ref[...] = part[128:]


def attend_back(i, ca, cb, weights, qkv, p, saved, order=()):
    more = () if saved is None else saved
    return kernel(
        functools.partial(attend_back_body, i),
        (shape((1024, 768)), shape((1024, 2048)), shape((128, 2048)), shape((128, 2048))),
        (ca, cb, qkv, p, weights, *more),
        order,
        input_output_aliases={5: 0, 6: 1} if more else {},
        name="attend_back",
    )


def feed_body(i, xa, xb, ga, gb, w_ref, *refs):
    act_ref, g_ref, all_ref, keep_ref, send_ref = refs[-5:]
    rows = slice(256 * i, 256 * (i + 1))
    x = rows_of((xa, xb))
    all_ref[rows, :] = x
    final = rows_of((ga, gb), slice(128, 256))
    for at in range(0, 1024, 256):
        u = dot(x, w_ref[:, at : at + 256], 1, 0)
        ga_hidden = dot(final, w_ref[:, 1024 + at : 1280 + at], 1, 0)
        phi = 0.5 + 0.5 * lax.erf(u * 0.5**0.5)
        act_ref[rows, at : at + 256] = (u * phi).astype(BF)
        slope = phi + u * jnp.exp(-0.5 * u * u) * (0.5 / jnp.pi) ** 0.5
        g_ref[rows, at : at + 256] = (ga_hidden * slope).astype(BF)
    part = dot(g_ref[rows, :], w_ref[:, :1024], 1, 1, BF)
    keep_ref[...] = part[:128]
    send_ref[...] = part[128:]


def feed(i, xa, xb, ga, gb, weights, saved, order=()):
    more = () if saved is None else saved
    return kernel(
        functools.partial(feed_body, i),
        (
            shape((1024, 1024)),
            shape((1024, 1024)),
            shape((1024, 2048)),
            shape((128, 2048)),
            shape((128, 2048)),
        ),
        (xa, xb, ga, gb, weights, *more),
        order,
        input_output_aliases={5: 0, 6: 1, 7: 2} if more else {},
        name="feed",
    )


def feed_out_body(act_ref, down_ref, keep_ref, send_ref):
    part = dot(act_ref[...], down_ref[...], 1, 1, BF)
    for i in range(4):
        keep_ref[i] = part[256 * i : 256 * i + 128]
        send_ref[i] = part[256 * i + 128 : 256 * (i + 1)]


def feed_out(act, weights, order=()):
    out = pl.BlockSpec((4, 128, 256), lambda j: (0, 0, j))
    return kernel(
        feed_out_body,
        (far((4, 128, 2048)), far((4, 128, 2048))),
        (out_of(act), out_of(weights)),
        order,
        grid=(8,),
        in_specs=[
            pl.BlockSpec((1024, 1024), lambda j: (0, 0)),
            pl.BlockSpec((256, 1024), lambda j: (j, 1)),
        ],
        out_specs=(out, out),
        name="feed_out",
    )


def feed_grad_body(x, g, act, *refs):
    gm, out = refs[:8], refs[8]
    columns = pl.ds(pl.multiple_of(pl.program_id(0) * 256, 256), 256)
    out[:, :1024] = dot(x[:, columns], g[...], 0, 0, BF)
    out[:, 1024:] = dot(rows_of(gm), act[...], 0, 0, BF)


def feed_grad(x, g, act, pieces, order=()):
    return kernel(
        feed_grad_body,
        far((2048, 2048)),
        (x, g, act, *map(out_of, pieces)),
        order,
        grid=(8,),
        in_specs=[WHOLE] * 3 + [pl.BlockSpec((128, 256), lambda j: (1, j))] * 8,
        out_specs=pl.BlockSpec((256, 2048), lambda j: (j, 0)),
        name="feed_grad",
    )


def more_grad_body(g, c, o, cross, *refs):
    x, out = refs[:8], refs[8]
    start = pl.multiple_of(pl.program_id(0) * 256, 256)
    columns = pl.ds(start, 256)
    out[:, :768] = dot(rows_of(x), g[...], 0, 0, BF)
    out[:, 768:1024] = dot(c[:, columns], o[...], 0, 0, BF)
    out[:, 1024:] = cross[columns, :]


def more_grad(g, c, o, cross, pieces, order=()):
    return kernel(
        more_grad_body,
        far((2048, 1536)),
        (g, c, o, cross, *map(out_of, pieces)),
        order,
        grid=(8,),
        in_specs=[WHOLE] * 4 + [pl.BlockSpec((128, 256), lambda j: (0, j))] * 8,
        out_specs=pl.BlockSpec((256, 1536), lambda j: (j, 0)),
        name="more_grad",
    )


def fold_body(kv_ref, w_ref, kv_out, both_ref):
    kv = jnp.sum(kv_ref[...].astype(F32), 0).astype(BF)
    kv_out[...] = kv
    for n in range(4):
        at = n * HEAD
        part = dot(kv[:, at : at + HEAD], w_ref[:, at : at + HEAD], 1, 1, BF)
        for i in range(4):
            both_ref[i, n * CAP : (n + 1) * CAP, :] = part[i * CAP : (i + 1) * CAP]


def fold(kv, weights, order=()):
    outs = (shape((64, 512)), shape((4, 64, 2048)))
    return kernel(
        fold_body,
        outs,
        (kv, out_of(weights)),
        order,
        in_specs=[
            pl.BlockSpec((16, 64, 512), lambda j: (0, 0, 0)),
            pl.BlockSpec((2048, 512), lambda j: (0, 2)),
        ],
        out_specs=(
            pl.BlockSpec((64, 512), lambda j: (0, 0)),
            pl.BlockSpec((4, 64, 2048), lambda j: (0, 0, 0)),
        ),
        grid=(1,),
        name="fold",
    )


def unfold_body(b0, b1, b2, b3, kv_ref, w_ref, grad_ref, gkv_ref):
    for n in range(4):
        at = n * HEAD
        rows = rows_of((b0, b1, b2, b3), slice(n * CAP, (n + 1) * CAP))
        grad_ref[:, at : at + HEAD] = dot(rows, kv_ref[:, at : at + HEAD], 0, 0, BF)
        gkv_ref[:, at : at + HEAD] = dot(rows, w_ref[:, at : at + HEAD], 1, 0, BF)


def unfold(back, kv, weights, order=()):
    slot = pl.BlockSpec((64, 2048), lambda j: (0, 0))
    return kernel(
        unfold_body,
        (shape((2048, 512)), shape((64, 512))),
        (*back, kv, out_of(weights)),
        order,
        in_specs=[slot] * 4
        + [
            pl.BlockSpec((64, 512), lambda j: (0, 0)),
            pl.BlockSpec((2048, 512), lambda j: (0, 2)),
        ],
        out_specs=(
            pl.BlockSpec((2048, 512), lambda j: (0, 0)),
            pl.BlockSpec((64, 512), lambda j: (0, 0)),
        ),
        grid=(1,),
        name="unfold",
    )


def slots_of(refs, part):
    return jnp.concatenate([ref[i, part, :] for ref in refs for i in range(4)], 0)


def middle_body(length_ref, *refs):
    x, parts, slots = refs[0], refs[1:6], refs[6:8]
    n2_ref, i2_ref, p2_ref, x3_ref, n3_ref, i3_ref = refs[8:]
    x2 = x[...].astype(F32) + total_of(parts)
    normed, inverse = stats(x2)
    low = normed.astype(BF)
    n2_ref[...] = low
    i2_ref[...] = inverse
    m, n = slots_of(slots, slice(0, 32)), slots_of(slots, slice(32, 64))
    s = (dot(m, low, 1, 1) * SCALE).reshape(16, CAP, 128)
    live = lax.broadcasted_iota(jnp.int32, (1, CAP, 1), 1) < length_ref[0]
    s = jnp.where(live, s, -1e30)
    e = jnp.exp(s - jnp.max(s, 1, keepdims=True))
    p = (e / jnp.sum(e, 1, keepdims=True)).reshape(256, 128)
    p2_ref[...] = p
    x3 = x2 + dot(p.astype(BF), n, 0, 0)
    x3_ref[...] = x3
    normed, inverse = stats(x3)
    n3_ref[...] = normed.astype(BF)
    i3_ref[...] = inverse


def middle(length, x, parts, slots, order=()):
    column = shape((128, 1), F32)
    return kernel(
        middle_body,
        (
            shape((128, 2048)),
            column,
            shape((256, 128), F32),
            shape((128, 2048), F32),
            shape((128, 2048)),
            column,
        ),
        (length, x, *parts, *slots),
        order,
        vmem=16,
        in_specs=[SCALAR] + [WHOLE] * 8,
        name="middle",
    )


def middle_back_body(*refs):
    g3, parts, slots = refs[0], refs[1:6], refs[6:8]
    n2, i2, p2, n3, i3 = refs[8:13]
    g1_ref, low_ref, keep_ref, send_ref = refs[13:]
    g2 = g3[...].astype(F32) + norm_back(total_of(parts), n3[...].astype(F32), i3[...])
    c = g2.astype(BF)
    m, n = slots_of(slots, slice(0, 32)), slots_of(slots, slice(32, 64))
    p = p2[...].reshape(16, CAP, 128)
    gp = dot(n, c, 1, 1).reshape(16, CAP, 128)
    gs = (p * (gp - jnp.sum(p * gp, 1, keepdims=True))).reshape(256, 128) * SCALE
    gs = gs.astype(BF)
    g1 = g2 + norm_back(dot(gs, m, 0, 0), n2[...].astype(F32), i2[...])
    g1_ref[...] = g1
    low_ref[...] = g1.astype(BF)
    gm = dot(gs, n2[...], 1, 0, BF)
    gn = dot(p2[...].astype(BF), c, 1, 0, BF)
    for out, at in ((keep_ref, 0), (send_ref, 128)):
        for i in range(4):
            rows = slice(at + 32 * i, at + 32 * (i + 1))
            out[i, :32, :] = gm[rows]
            out[i, 32:, :] = gn[rows]


def middle_back(g3, parts, slots, n2, i2, p2, n3, i3, order=()):
    slot = shape((4, 64, 2048))
    outs = (shape((128, 2048), F32), shape((128, 2048)), slot, slot)
    args = (g3, *parts, *slots, n2, i2, p2, n3, i3)
    return kernel(middle_back_body, outs, args, order, vmem=16, name="middle_back")


def last_body(*refs):
    g1, parts, x, out = refs[0], refs[1:6], refs[6], refs[7]
    normed, inverse = stats(x[...].astype(F32))
    out[...] = g1[...] + norm_back(total_of(parts), normed, inverse)


def last(g1, parts, x, order=()):
    return kernel(last_body, shape((128, 2048), F32), (g1, *parts, x), order, name="last")


def mix_features(value):
    n = value.shape[0]
    return value.reshape(n, 2, 16, 64).transpose(0, 2, 1, 3).reshape(n, 2048)


def unmix_features(value):
    n = value.shape[0]
    return value.reshape(n, 16, 2, 64).transpose(0, 2, 1, 3).reshape(n, 2048)


def per_device(
    image_tokens,
    caption_embed,
    caption_lengths,
    output_grad,
    norm_self,
    norm_cross,
    norm_feed,
    self_query,
    self_key,
    self_value,
    self_output,
    cross_query,
    cross_key,
    cross_value,
    cross_output,
    up_weight,
    down_weight,
):
    xh = lax.axis_index("xh")
    xl = lax.axis_index("xl")
    core = lax.axis_index("c")
    place = [lax.axis_index("y"), lax.axis_index("z"), 2 * xh + xl, core]
    place = jnp.stack(place).astype(jnp.int32)
    gain_one = norm_self.astype(F32)[:, None]
    gain_two = norm_cross.astype(F32)[:, None]
    gain_three = norm_feed.astype(F32)[:, None]

    def gained(weight, gain):
        return (weight.astype(F32) * gain).astype(BF)

    def halves(weight):
        n = weight.shape[1] // 2
        first, second = weight[:, :n], weight[:, n:]
        return jnp.where(xh == 0, first, second), jnp.where(xh == 0, second, first)

    def in_order(mine, theirs):
        return jnp.where(xh == 0, mine, theirs), jnp.where(xh == 0, theirs, mine)

    def exchange(weights):
        pairs = [halves(w) for w in weights]
        mine = jnp.concatenate([p[0] for p in pairs], 1)
        return mine, swap(jnp.concatenate([p[1] for p in pairs], 1), "xh")

    def both_of(mine, theirs):
        return jnp.stack(in_order(mine, theirs), 0)

    def home(first, second):
        keep = jnp.where(xh == 0, first, second)
        theirs = swap(jnp.where(xh == 0, second, first).astype(BF), "xh")
        return keep, theirs.astype(F32)

    def join(keep, theirs):
        return jnp.concatenate(in_order(keep, theirs), 1)

    pair = both_of(*exchange(
        (
            gained(self_query, gain_one),
            gained(self_key, gain_one),
            gained(self_value, gain_one),
            self_output.T,
            gained(cross_query, gain_two),
            cross_output.T,
        )
    ))
    first = lax.all_gather(pair.reshape(128, 1536), PLANE, axis=0, tiled=True)
    mine_late, theirs_late = exchange(
        (
            gained(up_weight, gain_three),
            down_weight.T,
            cross_key[:64],
            cross_value[:64],
            cross_key[64:],
            cross_value[64:],
        )
    )
    resid = mix_features(image_tokens[0])
    normed_one, _ = stats(resid.astype(F32))
    grad_low = mix_features(output_grad[0])
    caption = after(caption_embed[0], pair)
    sibling = swap(caption, "c")
    caption = jnp.where(core == 0, jnp.stack([caption, sibling]), jnp.stack([sibling, caption]))
    caption = jnp.stack([caption, px(caption, 1), px(caption, -1), px(caption, 2)])
    caption = caption.reshape(64, 2, 16, 128).transpose(2, 0, 1, 3).reshape(16, 64, 256)
    tokens = after(jnp.concatenate([normed_one.astype(BF), grad_low], 0), caption)
    pieces = [tokens, px(tokens, 1), px(tokens, -1)]
    caption = lax.all_to_all(caption, PLANE, split_axis=0, concat_axis=0, tiled=True)
    caption = caption.reshape(1024, 256)
    across = far_of(pieces[1], pieces[2])
    pieces.append(jnp.concatenate(across, 0))
    tokens = [side for piece in pieces for side in (piece, swap(piece, "c"))]
    pair_kv = both_of(mine_late[:, 2048:], theirs_late[:, 2048:])
    pair_kv = jnp.stack([pair_kv[:, :, :512], pair_kv[:, :, 512:]], 1).reshape(256, 512)
    kv = dot(caption, pair_kv, 1, 0, BF)
    pair_late = both_of(mine_late[:, :2048], hold(theirs_late, [*across, kv])[:, :2048])
    feed_weight = pair_late.reshape(128, 2048)
    feed_weight = lax.all_gather(feed_weight, PLANE, axis=0, tiled=True)
    kv = lax.all_to_all(kv.reshape(16, 64, 512), PLANE, split_axis=0, concat_axis=0, tiled=True)
    qkv, p1, o1, keep, send = attend(0, 4, tokens, first)
    kv, both = fold(kv.reshape(16, 64, 512), first, [keep])
    kv_weight = lax.all_gather(after(pair_kv, kv), PLANE, axis=0, tiled=True)
    parts, _ = reduce_tokens(keep, swap(send, "c"))
    slots_come = [px(both[1], -1), px(both[2], 1), px(both[3], 2)]
    slots_come = [hold(slot, parts[2:]) for slot in slots_come]
    slots = jnp.stack([both[0], *slots_come], 0)
    slots = (slots, swap(slots, "c"))

    length = jnp.where(xl == 0, caption_lengths[0, 0], caption_lengths[0, 1])[None]
    n2, i2, p2, x3, n3, i3 = middle(length, resid, parts, slots, [feed_weight])

    theirs = swap(n3, "c")
    around = [px(n3, 1), px(n3, -1)]
    saved, keeps, others = None, [], []
    for i in range(4):
        if i == 0:
            mine = n3
        else:
            if i == 1:
                around = [hold(piece, keeps[:1]) for piece in around]
                across = far_of(*around)
            if i < 3:
                mine = around[i - 1]
            else:
                mine = jnp.concatenate([hold(piece, keeps[1:2]) for piece in across], 0)
            theirs = swap(mine, "c")
        *saved, keep, send = feed(
            i,
            mine,
            theirs,
            tokens[2 * i],
            tokens[2 * i + 1],
            feed_weight,
            saved and tuple(saved),
            others[:-1][-1:],
        )
        keeps.append(keep)
        others.append(swap(send, "c"))
    parts, low = reduce_tokens(keeps, others)
    act, grad, x3_all = saved
    total = feed_grad(x3_all, grad, act, tokens, low + [kv_weight])
    total = hold(total, parts[2:], True)
    g1, c1, keep_slots, send_slots = middle_back(
        grad_low, parts, slots, n2, i2, p2, n3, i3, [total]
    )
    total = lax.psum_scatter(total, PLANE, scatter_dimension=0, tiled=True)
    own, their_ff = home(total[:64], total[64:])
    own = own.astype(F32)
    up_out = join(own[:, :1024], their_ff[:, :1024])
    down_out = join(own[:, 1024:], their_ff[:, 1024:])

    theirs = swap(c1, "c")
    around = [px(c1, 1), px(c1, -1)]
    slot_back = keep_slots.astype(F32) + swap(send_slots, "c").astype(F32)
    back, keeps, others = None, [], []
    for i in range(4):
        if i == 0:
            mine = c1
        else:
            if i == 1:
                around = [hold(piece, keeps[:1]) for piece in around]
                across = far_of(*around)
                slot_back = after(slot_back.astype(BF), around[1])
                slot_back = [
                    slot_back[0],
                    px(slot_back[1], 1),
                    px(slot_back[2], -1),
                    px(slot_back[3], 2),
                ]
            if i < 3:
                mine = around[i - 1]
            else:
                mine = jnp.concatenate([hold(piece, keeps[1:2]) for piece in across], 0)
            theirs = swap(mine, "c")
        order = others[:-1][-1:] + (slot_back[1:] if i == 3 else [])
        *back, keep, send = attend_back(
            i, mine, theirs, first, qkv, p1, back and tuple(back), order
        )
        keeps.append(keep)
        others.append(swap(send, "c"))
    parts, low = reduce_tokens(keeps, others)
    cross_grad, grad_kv = unfold(slot_back, kv, first, keeps[-1:])
    more = more_grad(*back, o1, cross_grad, tokens, keeps[-1:])
    more = hold(more, [total, low[-1]], True)
    y_keep, y_send = feed_out(act, feed_weight, [more])
    rest = lax.psum_scatter(more, PLANE, scatter_dimension=0, tiled=True)
    y_parts, _ = reduce_tokens(y_keep, swap(y_send, "c"))
    block_out = x3
    for part in y_parts:
        block_out = block_out + part.astype(F32)
    grad_kv = after(grad_kv, more)
    kv_all = lax.all_to_all(
        jnp.broadcast_to(grad_kv[None], (16, 64, 512)),
        PLANE,
        split_axis=0,
        concat_axis=0,
        tiled=True,
    ).reshape(1024, 512)
    kv_grad = dot(caption, kv_all, 0, 0)
    ck_own, ck_their = home(kv_grad[:128], kv_grad[128:])
    ck_out = join(ck_own[:, :256], ck_their[:, :256])
    cv_out = join(ck_own[:, 256:], ck_their[:, 256:])
    cap_grad = dot(grad_kv, kv_weight, 1, 1, BF).reshape(4, 16, 4096)
    keep = jnp.where(core == 0, cap_grad[:, :8], cap_grad[:, 8:])
    send = jnp.where(core == 0, cap_grad[:, 8:], cap_grad[:, :8])
    send = swap(send, "c")
    low_cap = (keep.astype(F32) + send.astype(F32)).astype(BF)
    cap_out = low_cap[0].astype(F32)
    for image, step in ((1, -1), (2, 1), (3, 2)):
        cap_out = cap_out + px(low_cap[image], step).astype(F32)
    cap_out = cap_out.reshape(8, 16, 2, 128).transpose(0, 2, 1, 3).reshape(1, 8, 4096)
    rest = hold(rest, y_parts[2:], True)
    own, their = home(rest[:64], rest[64:])
    own = own.astype(F32)
    outs = [join(own[:, at : at + 256], their[:, at : at + 256]) for at in range(0, 1536, 256)]
    so_out, cq_out, co_out = outs[3:]

    image_grad = unmix_features(last(g1, parts, resid, [y_keep]))[None]

    first_gain = (
        jnp.sum(outs[0] * self_query.astype(F32), 1)
        + jnp.sum(outs[1] * self_key.astype(F32), 1)
        + jnp.sum(outs[2] * self_value.astype(F32), 1)
    )
    terms = jnp.stack(
        [
            first_gain,
            jnp.sum(cq_out * cross_query.astype(F32), 1),
            jnp.sum(up_out * up_weight.astype(F32), 1),
        ],
        0,
    )
    terms = terms + swap(terms, "xl")
    terms = terms + swap(terms, "c")

    return (
        unmix_features(block_out.astype(BF))[None],
        image_grad,
        cap_out,
        terms[0],
        terms[1],
        terms[2],
        outs[0] * gain_one,
        outs[1] * gain_one,
        outs[2] * gain_one,
        so_out.T,
        cq_out * gain_two,
        ck_out,
        cv_out,
        co_out.T,
        up_out * gain_three,
        down_out.T,
    )


def solution(mesh):
    names = ("xh", "y", "z", "xl", "c")
    fine = Mesh(mesh.devices.reshape(2, 4, 4, 2, 2), names)
    rows, text = ("xh", "y", "z"), ("xl", "c")
    tokens = P(rows, text, None)
    by_row = P(rows, text)
    by_text = P(text, rows)
    weights = (by_row, by_row, by_row, by_text, by_row, by_row, by_row, by_text, by_row, by_text)
    in_specs = (tokens, tokens, P(rows, None), tokens) + (P(rows),) * 3 + weights
    out_specs = (tokens,) * 3 + (P(rows),) * 3 + weights
    return jax.shard_map(
        per_device, mesh=fine, in_specs=in_specs, out_specs=out_specs, check_vma=False
    )
```

```python
import functools

import jax
import jax.numpy as jnp
from jax import lax
from jax.experimental import pallas as pl
from jax.experimental.pallas import tpu as pltpu
from jax.sharding import Mesh, PartitionSpec as P

HEAD = 128
CAP = 16
EPSILON = 1e-05
SCALE = HEAD ** (-0.5)
BF = jnp.bfloat16
F32 = jnp.float32
RING = ("xh", "xl")
PLANE = ("y", "z")
WHOLE = pl.BlockSpec(memory_space=pltpu.VMEM)
HBM = pl.BlockSpec(memory_space=pltpu.MemorySpace.HBM)
ANY = pl.BlockSpec(memory_space=pl.ANY)
SCALAR = pl.BlockSpec(memory_space=pltpu.SMEM)


def shape(dims, dtype=BF):
    return jax.ShapeDtypeStruct(dims, dtype)


def out_of(value):
    return pltpu.with_memory_space_constraint(value, pltpu.MemorySpace.HBM)


def far(dims, dtype=BF):
    return pltpu.MemorySpace.HBM(dims, dtype)


def kernel(body, outs, args, order=(), vmem=12, in_specs=None, out_specs=None, **more):
    order = [out_of(dep) if dep.size >= 2**20 else dep for dep in order]
    n, outer = len(order), body
    if in_specs is None:
        in_specs = [WHOLE] * len(args)
    if out_specs is None:
        out_specs = jax.tree.map(lambda _: WHOLE, outs)
    spec = more.pop("grid_spec", None)
    if n:
        m = len(args)

        def outer(*refs):
            body(*refs[:m], *refs[m + n :])

    specs = dict(in_specs=list(in_specs) + [HBM] * n, out_specs=out_specs)
    if spec is not None:
        scalars, grid, scratch = spec
        specs = dict(
            grid_spec=pltpu.PrefetchScalarGridSpec(
                num_scalar_prefetch=scalars, grid=grid, scratch_shapes=scratch, **specs
            )
        )
    return pl.pallas_call(
        outer,
        out_shape=outs,
        compiler_params=pltpu.CompilerParams(vmem_limit_bytes=vmem * 2**20),
        cost_estimate=pl.CostEstimate(flops=1000, bytes_accessed=1000, transcendentals=0),
        **specs,
        **more,
    )(*args, *order)


def hold_body(value, out):
    pass


def hold(value, order, away=False):
    return kernel(
        hold_body,
        far(value.shape, value.dtype) if away else shape(value.shape, value.dtype),
        (out_of(value) if away else value,),
        order,
        vmem=4,
        in_specs=[ANY],
        out_specs=ANY,
        input_output_aliases={0: 0},
        name="hold",
    )


def dot(a, b, ca, cb, out=F32):
    return lax.dot_general(a, b, (((ca,), (cb,)), ((), ())), preferred_element_type=F32).astype(out)


def px(value, step):
    return lax.ppermute(value, RING, [(i, (i + step) % 4) for i in range(4)])


def pp(value, axis, step):
    return lax.ppermute(value, axis, [(i, (i + step) % 4) for i in range(4)])


def swap(value, axis):
    return lax.ppermute(value, axis, [(0, 1), (1, 0)])


def after(value, dep):
    first = dep[(slice(0, 1),) * dep.ndim].reshape((1,) * value.ndim).astype(F32)
    return (value.astype(F32) + first * 0.0).astype(value.dtype)


def far_of(left, right):
    half = left.shape[0] // 2
    return [px(left[:half], 1), px(right[half:], -1)]


def pick(value, at):
    return lax.dynamic_index_in_dim(value, at & 3, 0, False, allow_negative_indices=False)


def reduce_tokens(keep, other):
    low = [(keep[i].astype(F32) + other[i].astype(F32)).astype(BF) for i in range(1, 4)]
    return [keep[0], other[0], px(low[0], -1), px(low[1], 1), px(low[2], 2)], low


def stats(resid):
    mean = jnp.mean(resid, -1, keepdims=True)
    centered = resid - mean
    inverse = lax.rsqrt(jnp.mean(centered * centered, -1, keepdims=True) + EPSILON)
    return centered * inverse, inverse


def norm_back(scaled, normed, inverse):
    return inverse * (
        scaled
        - jnp.mean(scaled, -1, keepdims=True)
        - normed * jnp.mean(scaled * normed, -1, keepdims=True)
    )


def total_of(refs):
    total = refs[0][...].astype(F32)
    for ref in refs[1:]:
        total = total + ref[...].astype(F32)
    return total


def rows_of(refs, part=slice(None)):
    return jnp.concatenate([ref[part, :] for ref in refs], 0)


def attend_body(first, count, *refs):
    pieces, w_ref = refs[: 2 * count], refs[2 * count]
    qkv_ref, p_ref, o_ref, keep_ref, send_ref = refs[-5:]
    for i in range(count):
        rows = slice(256 * (first + i), 256 * (first + i + 1))
        x = rows_of(pieces[2 * i : 2 * i + 2], slice(0, 128))
        qkv_ref[rows, :] = dot(x, w_ref[:, :768], 1, 0, BF)
        for h in range(2):
            at = h * HEAD
            q = qkv_ref[rows, at : at + HEAD]
            k = qkv_ref[rows, 256 + at : 256 + at + HEAD]
            v = qkv_ref[rows, 512 + at : 512 + at + HEAD]
            s = dot(q, k, 1, 1) * SCALE
            e = jnp.exp(s - jnp.max(s, -1, keepdims=True))
            p = (e / jnp.sum(e, -1, keepdims=True)).astype(BF)
            p_ref[first + i, h] = p
            o_ref[rows, at : at + HEAD] = dot(p, v, 1, 0, BF)
        part = dot(o_ref[rows, :], w_ref[:, 768:1024], 1, 1, BF)
        keep_ref[i] = part[:128]
        send_ref[i] = part[128:]


def attend(first, count, pieces, weights, saved=(), order=()):
    return kernel(
        functools.partial(attend_body, first, count),
        (
            shape((1024, 768)),
            shape((4, 2, 256, 256)),
            shape((1024, 256)),
            shape((count, 128, 2048)),
            shape((count, 128, 2048)),
        ),
        (*pieces, weights, *saved),
        order,
        input_output_aliases={2 * count + 1 + n: n for n in range(3)} if saved else {},
        name="attend",
    )


def attend_back_body(i, ca, cb, qkv_ref, p_ref, w_ref, *refs):
    g_ref, all_ref, keep_ref, send_ref = refs[-4:]
    rows = slice(256 * i, 256 * (i + 1))
    c = rows_of((ca, cb))
    all_ref[rows, :] = c
    go = dot(c, w_ref[:, 768:1024], 1, 0, BF)
    for h in range(2):
        at = h * HEAD
        q = qkv_ref[rows, at : at + HEAD]
        k = qkv_ref[rows, 256 + at : 256 + at + HEAD]
        v = qkv_ref[rows, 512 + at : 512 + at + HEAD]
        low = p_ref[i, h]
        g = go[:, at : at + HEAD]
        g_ref[rows, 512 + at : 512 + at + HEAD] = dot(low, g, 0, 0, BF)
        gp = dot(g, v, 1, 1)
        p = low.astype(F32)
        gs = (p * (gp - jnp.sum(p * gp, -1, keepdims=True))).astype(BF)
        g_ref[rows, at : at + HEAD] = (dot(gs, k, 1, 0) * SCALE).astype(BF)
        g_ref[rows, 256 + at : 256 + at + HEAD] = (dot(gs, q, 0, 0) * SCALE).astype(BF)
    part = dot(g_ref[rows, :], w_ref[:, :768], 1, 1, BF)
    keep_ref[...] = part[:128]
    send_ref[...] = part[128:]


def attend_back(i, ca, cb, weights, qkv, p, saved, order=()):
    more = () if saved is None else saved
    return kernel(
        functools.partial(attend_back_body, i),
        (shape((1024, 768)), shape((1024, 2048)), shape((128, 2048)), shape((128, 2048))),
        (ca, cb, qkv, p, weights, *more),
        order,
        input_output_aliases={5: 0, 6: 1} if more else {},
        name="attend_back",
    )


def feed_body(i, xa, xb, ga, gb, w_ref, *refs):
    act_ref, g_ref, all_ref, keep_ref, send_ref = refs[-5:]
    rows = slice(256 * i, 256 * (i + 1))
    x = rows_of((xa, xb))
    all_ref[...] = x
    final = rows_of((ga, gb), slice(128, 256))
    for at in range(0, 1024, 256):
        u = dot(x, w_ref[:, at : at + 256], 1, 0)
        ga_hidden = dot(final, w_ref[:, 1024 + at : 1280 + at], 1, 0)
        phi = 0.5 + 0.5 * lax.erf(u * 0.5**0.5)
        act_ref[rows, at : at + 256] = (u * phi).astype(BF)
        slope = phi + u * jnp.exp(-0.5 * u * u) * (0.5 / jnp.pi) ** 0.5
        g_ref[rows, at : at + 256] = (ga_hidden * slope).astype(BF)
    part = dot(g_ref[rows, :], w_ref[:, :1024], 1, 1, BF)
    keep_ref[...] = part[:128]
    send_ref[...] = part[128:]


def feed(i, xa, xb, ga, gb, weights, saved, order=()):
    more = () if saved is None else saved
    return kernel(
        functools.partial(feed_body, i),
        (
            shape((1024, 1024)),
            shape((1024, 1024)),
            far((1024, 2048)),
            shape((128, 2048)),
            shape((128, 2048)),
        ),
        (xa, xb, ga, gb, weights, *more[:2], *map(out_of, more[2:])),
        order,
        grid=(1,),
        in_specs=[WHOLE] * (5 + len(more[:2])) + [HBM] * len(more[2:]),
        out_specs=(
            WHOLE,
            WHOLE,
            pl.BlockSpec((256, 2048), lambda j: (i, 0)),
            WHOLE,
            WHOLE,
        ),
        input_output_aliases={5: 0, 6: 1, 7: 2} if more else {},
        name="feed",
    )


def feed_out_body(act_ref, down_ref, keep_ref, send_ref):
    part = dot(act_ref[...], down_ref[...], 1, 1, BF)
    for i in range(4):
        keep_ref[i] = part[256 * i : 256 * i + 128]
        send_ref[i] = part[256 * i + 128 : 256 * (i + 1)]


def feed_out(act, weights, order=()):
    out = pl.BlockSpec((4, 128, 256), lambda j: (0, 0, j))
    return kernel(
        feed_out_body,
        (far((4, 128, 2048)), far((4, 128, 2048))),
        (out_of(act), out_of(weights)),
        order,
        grid=(8,),
        in_specs=[
            pl.BlockSpec((1024, 1024), lambda j: (0, 0)),
            pl.BlockSpec((256, 1024), lambda j: (j, 1)),
        ],
        out_specs=(out, out),
        name="feed_out",
    )


def feed_grad_body(x, g, act, *refs):
    gm, out = refs[:8], refs[8]
    out[:, :1024] = dot(x[...], g[...], 0, 0, BF)
    out[:, 1024:] = dot(rows_of(gm), act[...], 0, 0, BF)


def feed_grad(x, g, act, pieces, order=()):
    return kernel(
        feed_grad_body,
        far((2048, 2048)),
        (out_of(x), g, act, *map(out_of, pieces)),
        order,
        grid=(8,),
        in_specs=[pl.BlockSpec((1024, 256), lambda j: (0, j)), WHOLE, WHOLE]
        + [pl.BlockSpec((128, 256), lambda j: (1, j))] * 8,
        out_specs=pl.BlockSpec((256, 2048), lambda j: (j, 0)),
        name="feed_grad",
    )


def more_grad_body(g, c, o, cross, *refs):
    x, out = refs[:8], refs[8]
    start = pl.multiple_of(pl.program_id(0) * 256, 256)
    columns = pl.ds(start, 256)
    out[:, :768] = dot(rows_of(x), g[...], 0, 0, BF)
    out[:, 768:1024] = dot(c[:, columns], o[...], 0, 0, BF)
    out[:, 1024:] = cross[columns, :]


def more_grad(g, c, o, cross, pieces, order=()):
    return kernel(
        more_grad_body,
        far((2048, 1536)),
        (g, c, o, cross, *map(out_of, pieces)),
        order,
        grid=(8,),
        in_specs=[WHOLE] * 4 + [pl.BlockSpec((128, 256), lambda j: (0, j))] * 8,
        out_specs=pl.BlockSpec((256, 1536), lambda j: (j, 0)),
        name="more_grad",
    )


def fold_body(kv_ref, w_ref, kv_out, both_ref):
    kv = jnp.sum(kv_ref[...].astype(F32), 0).astype(BF)
    kv_out[...] = kv
    for n in range(4):
        at = n * HEAD
        part = dot(kv[:, at : at + HEAD], w_ref[:, at : at + HEAD], 1, 1, BF)
        for i in range(4):
            both_ref[i, n * CAP : (n + 1) * CAP, :] = part[i * CAP : (i + 1) * CAP]


def fold(kv, weights, order=()):
    outs = (shape((64, 512)), shape((4, 64, 2048)))
    return kernel(
        fold_body,
        outs,
        (kv, out_of(weights)),
        order,
        in_specs=[
            pl.BlockSpec((16, 64, 512), lambda j: (0, 0, 0)),
            pl.BlockSpec((2048, 512), lambda j: (0, 2)),
        ],
        out_specs=(
            pl.BlockSpec((64, 512), lambda j: (0, 0)),
            pl.BlockSpec((4, 64, 2048), lambda j: (0, 0, 0)),
        ),
        grid=(1,),
        name="fold",
    )


def unfold_body(b0, b1, b2, b3, kv_ref, w_ref, grad_ref, gkv_ref):
    for n in range(4):
        at = n * HEAD
        rows = rows_of((b0, b1, b2, b3), slice(n * CAP, (n + 1) * CAP))
        grad_ref[:, at : at + HEAD] = dot(rows, kv_ref[:, at : at + HEAD], 0, 0, BF)
        gkv_ref[:, at : at + HEAD] = dot(rows, w_ref[:, at : at + HEAD], 1, 0, BF)


def unfold(back, kv, weights, order=()):
    slot = pl.BlockSpec((64, 2048), lambda j: (0, 0))
    return kernel(
        unfold_body,
        (shape((2048, 512)), shape((64, 512))),
        (*back, kv, out_of(weights)),
        order,
        in_specs=[slot] * 4
        + [
            pl.BlockSpec((64, 512), lambda j: (0, 0)),
            pl.BlockSpec((2048, 512), lambda j: (0, 2)),
        ],
        out_specs=(
            pl.BlockSpec((2048, 512), lambda j: (0, 0)),
            pl.BlockSpec((64, 512), lambda j: (0, 0)),
        ),
        grid=(1,),
        name="unfold",
    )


def slots_of(refs, part):
    return jnp.concatenate([ref[i, part, :] for ref in refs for i in range(4)], 0)


def middle_body(length_ref, *refs):
    x, parts, slots = refs[0], refs[1:6], refs[6:8]
    n2_ref, i2_ref, p2_ref, x3_ref, n3_ref, i3_ref = refs[8:]
    x2 = x[...].astype(F32) + total_of(parts)
    normed, inverse = stats(x2)
    low = normed.astype(BF)
    n2_ref[...] = low
    i2_ref[...] = inverse
    m, n = slots_of(slots, slice(0, 32)), slots_of(slots, slice(32, 64))
    s = (dot(m, low, 1, 1) * SCALE).reshape(16, CAP, 128)
    live = lax.broadcasted_iota(jnp.int32, (1, CAP, 1), 1) < length_ref[0]
    s = jnp.where(live, s, -1e30)
    e = jnp.exp(s - jnp.max(s, 1, keepdims=True))
    p = (e / jnp.sum(e, 1, keepdims=True)).reshape(256, 128)
    p2_ref[...] = p
    x3 = x2 + dot(p.astype(BF), n, 0, 0)
    x3_ref[...] = x3
    normed, inverse = stats(x3)
    n3_ref[...] = normed.astype(BF)
    i3_ref[...] = inverse


def middle(length, x, parts, slots, order=()):
    column = shape((128, 1), F32)
    return kernel(
        middle_body,
        (
            shape((128, 2048)),
            column,
            shape((256, 128), F32),
            shape((128, 2048), F32),
            shape((128, 2048)),
            column,
        ),
        (length, *map(out_of, (x, *parts, *slots))),
        order,
        vmem=24,
        grid=(1,),
        in_specs=[SCALAR]
        + [pl.BlockSpec((128, 2048), lambda j: (0, 0))] * 6
        + [pl.BlockSpec((4, 64, 2048), lambda j: (0, 0, 0))] * 2,
        name="middle",
    )


def middle_back_body(*refs):
    g3, parts, slots = refs[0], refs[1:6], refs[6:8]
    n2, i2, p2, n3, i3 = refs[8:13]
    g1_ref, low_ref, keep_ref, send_ref = refs[13:]
    g2 = g3[...].astype(F32) + norm_back(total_of(parts), n3[...].astype(F32), i3[...])
    c = g2.astype(BF)
    m, n = slots_of(slots, slice(0, 32)), slots_of(slots, slice(32, 64))
    p = p2[...].reshape(16, CAP, 128)
    gp = dot(n, c, 1, 1).reshape(16, CAP, 128)
    gs = (p * (gp - jnp.sum(p * gp, 1, keepdims=True))).reshape(256, 128) * SCALE
    gs = gs.astype(BF)
    g1 = g2 + norm_back(dot(gs, m, 0, 0), n2[...].astype(F32), i2[...])
    g1_ref[...] = g1
    low_ref[...] = g1.astype(BF)
    gm = dot(gs, n2[...], 1, 0, BF)
    gn = dot(p2[...].astype(BF), c, 1, 0, BF)
    for out, at in ((keep_ref, 0), (send_ref, 128)):
        for i in range(4):
            rows = slice(at + 32 * i, at + 32 * (i + 1))
            out[i, :32, :] = gm[rows]
            out[i, 32:, :] = gn[rows]


def middle_back(g3, parts, slots, n2, i2, p2, n3, i3, order=()):
    slot = shape((4, 64, 2048))
    outs = (shape((128, 2048), F32), shape((128, 2048)), slot, slot)
    args = (g3, *parts, *slots, n2, i2, p2, n3, i3)
    return kernel(middle_back_body, outs, args, order, vmem=16, name="middle_back")


def last_body(*refs):
    g1, parts, x, out = refs[0], refs[1:6], refs[6], refs[7]
    normed, inverse = stats(x[...].astype(F32))
    out[...] = g1[...] + norm_back(total_of(parts), normed, inverse)


def last(g1, parts, x, order=()):
    return kernel(last_body, shape((128, 2048), F32), (g1, *parts, x), order, name="last")


def mix_features(value):
    n = value.shape[0]
    return value.reshape(n, 2, 16, 64).transpose(0, 2, 1, 3).reshape(n, 2048)


def unmix_features(value):
    n = value.shape[0]
    return value.reshape(n, 16, 2, 64).transpose(0, 2, 1, 3).reshape(n, 2048)


def per_device(
    image_tokens,
    caption_embed,
    caption_lengths,
    output_grad,
    norm_self,
    norm_cross,
    norm_feed,
    self_query,
    self_key,
    self_value,
    self_output,
    cross_query,
    cross_key,
    cross_value,
    cross_output,
    up_weight,
    down_weight,
):
    xh = lax.axis_index("xh")
    xl = lax.axis_index("xl")
    core = lax.axis_index("c")
    place = [lax.axis_index("y"), lax.axis_index("z"), 2 * xh + xl, core]
    place = jnp.stack(place).astype(jnp.int32)
    gain_one = norm_self.astype(F32)[:, None]
    gain_two = norm_cross.astype(F32)[:, None]
    gain_three = norm_feed.astype(F32)[:, None]

    def gained(weight, gain):
        return (weight.astype(F32) * gain).astype(BF)

    def halves(weight):
        n = weight.shape[1] // 2
        first, second = weight[:, :n], weight[:, n:]
        return jnp.where(xh == 0, first, second), jnp.where(xh == 0, second, first)

    def in_order(mine, theirs):
        return jnp.where(xh == 0, mine, theirs), jnp.where(xh == 0, theirs, mine)

    def exchange(weights):
        pairs = [halves(w) for w in weights]
        mine = jnp.concatenate([p[0] for p in pairs], 1)
        return mine, swap(jnp.concatenate([p[1] for p in pairs], 1), "xh")

    def both_of(mine, theirs):
        return jnp.stack(in_order(mine, theirs), 0)

    def home(first, second):
        keep = jnp.where(xh == 0, first, second)
        theirs = swap(jnp.where(xh == 0, second, first).astype(BF), "xh")
        return keep, theirs.astype(F32)

    def join(keep, theirs):
        return jnp.concatenate(in_order(keep, theirs), 1)

    pair = both_of(*exchange(
        (
            gained(self_query, gain_one),
            gained(self_key, gain_one),
            gained(self_value, gain_one),
            self_output.T,
            gained(cross_query, gain_two),
            cross_output.T,
        )
    ))
    first = lax.all_gather(pair.reshape(128, 1536), PLANE, axis=0, tiled=True)
    mine_late, theirs_late = exchange(
        (
            gained(up_weight, gain_three),
            down_weight.T,
            cross_key[:64],
            cross_value[:64],
            cross_key[64:],
            cross_value[64:],
        )
    )
    resid = mix_features(image_tokens[0])
    normed_one, _ = stats(resid.astype(F32))
    grad_low = mix_features(output_grad[0])
    caption = after(caption_embed[0], pair)
    sibling = swap(caption, "c")
    caption = jnp.where(core == 0, jnp.stack([caption, sibling]), jnp.stack([sibling, caption]))
    caption = jnp.stack([caption, px(caption, 1), px(caption, -1), px(caption, 2)])
    caption = caption.reshape(64, 2, 16, 128).transpose(2, 0, 1, 3).reshape(16, 64, 256)
    tokens = after(jnp.concatenate([normed_one.astype(BF), grad_low], 0), caption)
    pieces = [tokens, px(tokens, 1), px(tokens, -1)]
    caption = lax.all_to_all(caption, PLANE, split_axis=0, concat_axis=0, tiled=True)
    caption = caption.reshape(1024, 256)
    across = far_of(pieces[1], pieces[2])
    pieces.append(jnp.concatenate(across, 0))
    tokens = [side for piece in pieces for side in (piece, swap(piece, "c"))]
    pair_kv = both_of(mine_late[:, 2048:], theirs_late[:, 2048:])
    pair_kv = jnp.stack([pair_kv[:, :, :512], pair_kv[:, :, 512:]], 1).reshape(256, 512)
    kv = dot(caption, pair_kv, 1, 0, BF)
    pair_late = both_of(mine_late[:, :2048], hold(theirs_late, [*across, kv])[:, :2048])
    feed_weight = pair_late.reshape(128, 2048)
    feed_weight = lax.all_gather(feed_weight, PLANE, axis=0, tiled=True)
    kv = lax.all_to_all(kv.reshape(16, 64, 512), PLANE, split_axis=0, concat_axis=0, tiled=True)
    qkv, p1, o1, keep, send = attend(0, 4, tokens, first)
    kv, both = fold(kv.reshape(16, 64, 512), first, [keep])
    kv_weight = lax.all_gather(after(pair_kv, kv), PLANE, axis=0, tiled=True)
    slots_come = [px(both[1], -1), px(both[2], 1), px(both[3], 2)]
    slots = jnp.stack([both[0], *slots_come], 0)
    slots = (slots, swap(slots, "c"))

    parts, _ = reduce_tokens(keep, swap(send, "c"))
    length = jnp.where(xl == 0, caption_lengths[0, 0], caption_lengths[0, 1])[None]
    n2, i2, p2, x3, n3, i3 = middle(length, resid, parts, slots, [feed_weight])

    theirs = swap(n3, "c")
    around = [px(n3, 1), px(n3, -1)]
    saved, keeps, others = None, [], []
    for i in range(4):
        if i == 0:
            mine = n3
        else:
            if i == 1:
                around = [hold(piece, keeps[:1]) for piece in around]
                across = far_of(*around)
            if i < 3:
                mine = around[i - 1]
            else:
                mine = jnp.concatenate([hold(piece, keeps[1:2]) for piece in across], 0)
            theirs = swap(mine, "c")
        *saved, keep, send = feed(
            i,
            mine,
            theirs,
            tokens[2 * i],
            tokens[2 * i + 1],
            feed_weight,
            saved and tuple(saved),
            others[:-1][-1:],
        )
        keeps.append(keep)
        others.append(swap(send, "c"))
    parts, low = reduce_tokens(keeps, others)
    act, grad, x3_all = saved
    total = feed_grad(x3_all, grad, act, tokens, low + [kv_weight])
    total = hold(total, parts[2:], True)
    g1, c1, keep_slots, send_slots = middle_back(
        grad_low, parts, slots, n2, i2, p2, n3, i3, [total]
    )
    total = lax.psum_scatter(total, PLANE, scatter_dimension=0, tiled=True)
    own, their_ff = home(total[:64], total[64:])
    own = own.astype(F32)
    up_out = join(own[:, :1024], their_ff[:, :1024])
    down_out = join(own[:, 1024:], their_ff[:, 1024:])

    theirs = swap(c1, "c")
    around = [px(c1, 1), px(c1, -1)]
    slot_back = keep_slots.astype(F32) + swap(send_slots, "c").astype(F32)
    back, keeps, others = None, [], []
    for i in range(4):
        if i == 0:
            mine = c1
        else:
            if i == 1:
                around = [hold(piece, keeps[:1]) for piece in around]
                across = far_of(*around)
                slot_back = after(slot_back.astype(BF), around[1])
                slot_back = [
                    slot_back[0],
                    px(slot_back[1], 1),
                    px(slot_back[2], -1),
                    px(slot_back[3], 2),
                ]
            if i < 3:
                mine = around[i - 1]
            else:
                mine = jnp.concatenate([hold(piece, keeps[1:2]) for piece in across], 0)
            theirs = swap(mine, "c")
        order = others[:-1][-1:] + (slot_back[1:] if i == 3 else [])
        *back, keep, send = attend_back(
            i, mine, theirs, first, qkv, p1, back and tuple(back), order
        )
        keeps.append(keep)
        others.append(swap(send, "c"))
    parts, low = reduce_tokens(keeps, others)
    cross_grad, grad_kv = unfold(slot_back, kv, first, keeps[-1:])
    more = more_grad(*back, o1, cross_grad, tokens, keeps[-1:])
    more = hold(more, [total, low[-1]], True)
    y_keep, y_send = feed_out(act, feed_weight, [more])
    rest = lax.psum_scatter(more, PLANE, scatter_dimension=0, tiled=True)
    y_parts, _ = reduce_tokens(y_keep, swap(y_send, "c"))
    block_out = x3
    for part in y_parts:
        block_out = block_out + part.astype(F32)
    grad_kv = after(grad_kv, more)
    kv_all = lax.all_to_all(
        jnp.broadcast_to(grad_kv[None], (16, 64, 512)),
        PLANE,
        split_axis=0,
        concat_axis=0,
        tiled=True,
    ).reshape(1024, 512)
    kv_grad = dot(caption, kv_all, 0, 0)
    ck_own, ck_their = home(kv_grad[:128], kv_grad[128:])
    ck_out = join(ck_own[:, :256], ck_their[:, :256])
    cv_out = join(ck_own[:, 256:], ck_their[:, 256:])
    cap_grad = dot(grad_kv, kv_weight, 1, 1, BF).reshape(4, 16, 4096)
    keep = jnp.where(core == 0, cap_grad[:, :8], cap_grad[:, 8:])
    send = jnp.where(core == 0, cap_grad[:, 8:], cap_grad[:, :8])
    send = swap(send, "c")
    low_cap = (keep.astype(F32) + send.astype(F32)).astype(BF)
    cap_out = low_cap[0].astype(F32)
    for image, step in ((1, -1), (2, 1), (3, 2)):
        cap_out = cap_out + px(low_cap[image], step).astype(F32)
    cap_out = cap_out.reshape(8, 16, 2, 128).transpose(0, 2, 1, 3).reshape(1, 8, 4096)
    rest = hold(rest, y_parts[2:], True)
    own, their = home(rest[:64], rest[64:])
    own = own.astype(F32)
    outs = [join(own[:, at : at + 256], their[:, at : at + 256]) for at in range(0, 1536, 256)]
    so_out, cq_out, co_out = outs[3:]

    image_grad = unmix_features(last(g1, parts, resid, [y_keep]))[None]

    first_gain = (
        jnp.sum(outs[0] * self_query.astype(F32), 1)
        + jnp.sum(outs[1] * self_key.astype(F32), 1)
        + jnp.sum(outs[2] * self_value.astype(F32), 1)
    )
    terms = jnp.stack(
        [
            first_gain,
            jnp.sum(cq_out * cross_query.astype(F32), 1),
            jnp.sum(up_out * up_weight.astype(F32), 1),
        ],
        0,
    )
    terms = terms + swap(terms, "xl")
    terms = terms + swap(terms, "c")

    return (
        unmix_features(block_out.astype(BF))[None],
        image_grad,
        cap_out,
        terms[0],
        terms[1],
        terms[2],
        outs[0] * gain_one,
        outs[1] * gain_one,
        outs[2] * gain_one,
        so_out.T,
        cq_out * gain_two,
        ck_out,
        cv_out,
        co_out.T,
        up_out * gain_three,
        down_out.T,
    )


def solution(mesh):
    names = ("xh", "y", "z", "xl", "c")
    fine = Mesh(mesh.devices.reshape(2, 4, 4, 2, 2), names)
    rows, text = ("xh", "y", "z"), ("xl", "c")
    tokens = P(rows, text, None)
    by_row = P(rows, text)
    by_text = P(text, rows)
    weights = (by_row, by_row, by_row, by_text, by_row, by_row, by_row, by_text, by_row, by_text)
    in_specs = (tokens, tokens, P(rows, None), tokens) + (P(rows),) * 3 + weights
    out_specs = (tokens,) * 3 + (P(rows),) * 3 + weights
    return jax.shard_map(
        per_device, mesh=fine, in_specs=in_specs, out_specs=out_specs, check_vma=False
    )
```
